32 devices in a mesh: blk: 8 (over z, x), batch: 4 (over y, core).
Axes of the slice: x: 2, y: 2, z: 4, core: 2. Of those that a mesh axis runs over, the one named last changes fastest.
Arguments:
- inputs: float32 [64, 128, 4096], P('batch', None, 'blk'), may hold values from -6 to 6
- weight_in: float32 [512, 128], replicated, may hold values from -0.5 to 0.5
- bias_in: float32 [512], replicated, may hold values from -3 to 3
- slope_in: float32 [512], replicated, may hold values from 0.05 to 0.6
- gain_in: float32 [512], replicated, may hold values from 0.25 to 1.75
- shift_in: float32 [512], replicated, may hold values from -3 to 3
- depthwise_weight: float32 [512, 3], replicated, may hold values from -3.5 to 3.5
- depthwise_bias: float32 [512], replicated, may hold values from -3 to 3
- slope_mid: float32 [512], replicated, may hold values from 0.05 to 0.6
- gain_mid: float32 [512], replicated, may hold values from 0.25 to 1.75
- shift_mid: float32 [512], replicated, may hold values from -3 to 3
- weight_res: float32 [128, 512], replicated, may hold values from -0.25 to 0.25
- bias_res: float32 [128], replicated, may hold values from -3 to 3
- weight_skip: float32 [128, 512], replicated, may hold values from -0.25 to 0.25
- bias_skip: float32 [128], replicated, may hold values from -3 to 3
- lengths: int32 [64], P('batch'), may hold values from 2049 to 4096, as said below
- cot_res: float32 [64, 128, 4096], P('batch', None, 'blk'), may hold values from -6 to 6
- cot_skip: float32 [64, 128, 4096], P('batch', None, 'blk'), may hold values from -6 to 6
Outputs:
- residual_out: float32 [64, 128, 4096], P('batch', None, 'blk')
- skip_out: float32 [64, 128, 4096], P('batch', None, 'blk')
- grad_inputs: float32 [64, 128, 4096], P('batch', None, 'blk')
- grad_weight_in: float32 [512, 128], replicated
- grad_bias_in: float32 [512], replicated
- grad_slope_in: float32 [512], replicated
- grad_gain_in: float32 [512], replicated
- grad_shift_in: float32 [512], replicated
- grad_weight_depth: float32 [512, 3], replicated
- grad_bias_depth: float32 [512], replicated
- grad_slope_mid: float32 [512], replicated
- grad_gain_mid: float32 [512], replicated
- grad_shift_mid: float32 [512], replicated
- grad_weight_res: float32 [128, 512], replicated
- grad_bias_res: float32 [128], replicated
- grad_weight_skip: float32 [128, 512], replicated
- grad_bias_skip: float32 [128], replicated
The draws below stay inside these ranges and needn't reach their ends.
Inputs may be any that keep to these rules, and one draw needn't show every extreme that they name: `lengths`: in each aligned group of 16 consecutive items one item, which one drawn from the seed, has 4096 valid frames.
All inputs are finite; a program needn't handle non-finite values.
Results may differ from the reference program's by a relative error of at most 0.0003.
Values sent between devices are 32-bit elements; how exact they have to be, the bound alone decides.
No kernel may reach another device: no remote copies, remote signals or barrier semaphores. Data moves between devices by JAX's collectives and lax.ppermute only.
A program may use at most 256 MiB of HBM per device.

```python
import jax
import jax.numpy as jnp
from jax import lax

NCH = 512
BCH = 128
DILATION_STEP = 8
ITEMS_DEV = 16
LENGTH = 4096
ITEMS = 64


def draw_lengths(key, part):
    key = jax.random.fold_in(key, 11)
    first, second = jax.random.split(key)
    base = jax.random.randint(first, (ITEMS,), LENGTH // 2 + 1, LENGTH + 1)
    pick = jax.random.randint(second, (ITEMS // ITEMS_DEV,), 0, ITEMS_DEV)
    index = jnp.arange(ITEMS)
    full = index % ITEMS_DEV == jnp.repeat(pick, ITEMS_DEV)
    return jnp.where(full, LENGTH, base).astype(jnp.int32)


def steps_of(own_key, shape, cuts, smallest, top_value):
    level, own = 1.0, jax.random.fold_in(own_key, 6)
    for dim, blocks in cuts:
        heights = jnp.exp(jax.random.uniform(jax.random.fold_in(own, dim), (blocks,), jnp.float32, smallest / len(cuts), top_value / len(cuts)))
        level = level * jnp.repeat(heights, shape[dim] // blocks).reshape([-1 if axis == dim else 1 for axis in range(len(shape))])
    return level


def gaussian(own_key, dims, spread, most, cuts=(), kind=jnp.bfloat16):
    array = spread * jax.random.normal(own_key, dims, jnp.float32)
    if cuts:
        array = array * steps_of(own_key, dims, cuts, -0.22, 0.18)
    return jnp.clip(array, -most, most).astype(kind)


def setup_inputs(seed: int = 0) -> dict:
    key_list = jax.random.split(jax.random.key(seed), 19)
    return {
        "inputs": gaussian(key_list[0], (ITEMS, BCH, LENGTH), 1.0, 6.0, ((0, 4), (2, 8)), jnp.float32),
        "weight_in": gaussian(key_list[1], (NCH, BCH), BCH ** -0.5, 0.5, (), jnp.float32),
        "bias_in": gaussian(key_list[2], (NCH,), 0.5, 3.0, (), jnp.float32),
        "slope_in": jnp.clip(jax.random.uniform(key_list[3], (NCH,), jnp.float32, 0.05, 0.6), 0.05, 0.6),
        "gain_in": jnp.clip(1.0 + 0.15 * jax.random.normal(key_list[4], (NCH,), jnp.float32), 0.25, 1.75),
        "shift_in": gaussian(key_list[5], (NCH,), 0.5, 3.0, (), jnp.float32),
        "depthwise_weight": gaussian(key_list[6], (NCH, 3), 3 ** -0.5, 3.5, (), jnp.float32),
        "depthwise_bias": gaussian(key_list[7], (NCH,), 0.5, 3.0, (), jnp.float32),
        "slope_mid": jnp.clip(jax.random.uniform(key_list[8], (NCH,), jnp.float32, 0.05, 0.6), 0.05, 0.6),
        "gain_mid": jnp.clip(1.0 + 0.15 * jax.random.normal(key_list[9], (NCH,), jnp.float32), 0.25, 1.75),
        "shift_mid": gaussian(key_list[10], (NCH,), 0.5, 3.0, (), jnp.float32),
        "weight_res": gaussian(key_list[11], (BCH, NCH), NCH ** -0.5, 0.25, (), jnp.float32),
        "bias_res": gaussian(key_list[12], (BCH,), 0.5, 3.0, (), jnp.float32),
        "weight_skip": gaussian(key_list[13], (BCH, NCH), NCH ** -0.5, 0.25, (), jnp.float32),
        "bias_skip": gaussian(key_list[14], (BCH,), 0.5, 3.0, (), jnp.float32),
        "lengths": draw_lengths(jax.random.fold_in(key_list[18], 71), 0),
        "cot_res": gaussian(key_list[16], (ITEMS, BCH, LENGTH), 1.0, 6.0, ((0, 4), (2, 8)), jnp.float32),
        "cot_skip": gaussian(key_list[17], (ITEMS, BCH, LENGTH), 1.0, 6.0, ((0, 4), (2, 8)), jnp.float32),
    }


@jax.custom_vjp
def low(v):
    return lax.optimization_barrier(v.astype(jnp.bfloat16)).astype(jnp.float32)

@jax.custom_vjp
def low_back(v):
    return v

def low_keep(v):
    return (low(v), None)

def low_pass(kept, grad):
    return (grad,)

def back_keep(v):
    return (v, None)

def back_low(kept, grad):
    return (low(grad),)
low.defvjp(low_keep, low_pass)
low_back.defvjp(back_keep, back_low)
EPS = 1e-05

def smooth_act(value, slope):
    soft = jax.nn.silu(value)
    return soft + slope * (value - soft)

def global_norm(value, gain, shift, valid, count):
    masked = value * valid
    mean = jnp.sum(masked) / count
    var = jnp.sum(masked * value) / count - mean * mean
    normal = (value - mean) * lax.rsqrt(var + EPS)
    return valid * (gain[:, None] * normal + shift[:, None])

def item_forward(item, params, valid, count):
    weight_in, bias_in, slope_in, gain_in, shift_in, depthwise_weight, depthwise_bias, slope_mid, gain_mid, shift_mid, weight_res, bias_res, weight_skip, bias_skip = params
    hp = lax.Precision.HIGHEST
    upper = jnp.dot(weight_in, item, precision=hp) + bias_in[:, None]
    act_one = smooth_act(upper, slope_in[:, None])
    normalized_input = global_norm(act_one, gain_in, shift_in, valid, count)
    padded_input = jnp.pad(normalized_input, ((0, 0), (DILATION_STEP, DILATION_STEP)))
    depthwise_output = depthwise_weight[:, 0:1] * padded_input[:, :-2 * DILATION_STEP] + depthwise_weight[:, 1:2] * normalized_input + depthwise_weight[:, 2:3] * padded_input[:, 2 * DILATION_STEP:] + depthwise_bias[:, None]
    act_two = smooth_act(depthwise_output, slope_mid[:, None])
    hidden = global_norm(act_two, gain_mid, shift_mid, valid, count)
    res = item + jnp.dot(weight_res, hidden, precision=hp) + bias_res[:, None]
    skip = jnp.dot(weight_skip, hidden, precision=hp) + bias_skip[:, None]
    return (res, skip)

def reference(inputs, weight_in, bias_in, slope_in, gain_in, shift_in, depthwise_weight, depthwise_bias, slope_mid, gain_mid, shift_mid, weight_res, bias_res, weight_skip, bias_skip, lengths, cot_res, cot_skip):
    params = (weight_in, bias_in, slope_in, gain_in, shift_in, depthwise_weight, depthwise_bias, slope_mid, gain_mid, shift_mid, weight_res, bias_res, weight_skip, bias_skip)
    frames = lax.iota(jnp.int32, LENGTH)

    def one_item(carry, pieces):
        item, length, cres, cskip = pieces
        valid = (frames < length).astype(jnp.float32)[None, :]
        count = length.astype(jnp.float32) * NCH

        def forward(xval, *ps):
            return item_forward(xval, ps, valid, count)
        outs, pull = jax.vjp(forward, item, *params)
        grads = pull((valid * cres, valid * cskip))
        carry = tuple((c + g for c, g in zip(carry, grads[1:])))
        return (carry, (outs[0], outs[1], grads[0]))
    start = tuple((jnp.zeros_like(p) for p in params))
    totals, stacked = lax.scan(one_item, start, (inputs, lengths, cot_res, cot_skip))
    return (stacked[0], stacked[1], stacked[2]) + tuple(totals)
```

```python
import functools

import jax
import jax.numpy as jnp
from jax import lax
from jax.experimental import pallas as pl
from jax.experimental.pallas import tpu as pltpu
from jax.sharding import PartitionSpec as P

STEP = 8
HALO = 2 * STEP
EPS = 1e-05
LANE = 128
ROWS = 64
SECOND_ROWS = 128
THIRD_ROWS = 64
PIECE = 256
F32 = jnp.float32
BF16 = jnp.bfloat16
VMEM_LIMIT = 60 * 1024 * 1024


def split(value):
    high = value.astype(BF16)
    low = (value - high.astype(F32)).astype(BF16)
    return high, low


def product(left, right):
    return jnp.dot(left, right, preferred_element_type=F32)


def product_nt(left, right):
    return lax.dot_general(left, right, (((1,), (1,)), ((), ())), preferred_element_type=F32)


def tile(row):
    return jnp.broadcast_to(row, (8, LANE))


def load(ref, base, rows, lanes):
    return ref[pl.ds(base, rows), lanes].reshape(rows // 8, 8, LANE)


def frame_of(base, rows):
    shape = (rows // 8, 8, LANE)
    return lax.broadcasted_iota(jnp.int32, shape, 0) * 8 + lax.broadcasted_iota(jnp.int32, shape, 1) + base


def half_slopes(row):
    return tile(0.5 - 0.5 * row), tile(0.5 + 0.5 * row)


def act_half(half, c0, c1):
    return half * (c1 + c0 * jnp.tanh(half))


def act_parts(half, c0, c1):
    th = jnp.tanh(half)
    rest = half - half * th
    cut = c0 * rest
    return half - cut, (c1 + cut) + (c0 + cut) * th, rest


def total(value):
    return jnp.sum(jnp.sum(value, axis=0, keepdims=True), axis=1, keepdims=True)


def place(values):
    lane = lax.broadcasted_iota(jnp.int32, (1, LANE), 1)
    row = jnp.zeros((1, LANE), F32)
    for position, value in enumerate(values):
        row = jnp.where(lane == position, value, row)
    return row


def lane_tiles(width):
    return [slice(start, start + LANE) for start in range(0, width, LANE)]


def first_kernel(
    ends_ref, x_ref, w_in_ref, bias_ref, slope_ref, w_res_ref, w_skip_ref, gain_ref,
    half_ref, sums_ref, left_ref, right_ref, w_cat_ref, w_out_ref,
):
    group, cin, frames = x_ref.shape
    width = w_in_ref.shape[0]

    @pl.when(pl.program_id(0) == 0)
    def _():
        high, low = split(0.5 * w_in_ref[...].T)
        w_cat_ref[0:cin] = high
        w_cat_ref[cin : 2 * cin] = high
        w_cat_ref[2 * cin : 3 * cin] = low
        for number, ref in enumerate((w_res_ref, w_skip_ref)):
            high, low = split(ref[...] * gain_ref[...])
            start = number * cin
            w_out_ref[start : start + cin] = high
            w_out_ref[2 * cin + start : 3 * cin + start] = high
            w_out_ref[4 * cin + start : 5 * cin + start] = low

    step = min(PIECE, frames)
    for number in range(group):
        item = pl.program_id(0) * group + number
        end = ends_ref[item]
        first = second = jnp.zeros((8, LANE), F32)
        for start in range(0, frames, step):
            xt = x_ref[number, :, start : start + step].T
            if start == 0:
                left_ref[number] = xt[0:HALO]
            if start + step == frames:
                right_ref[number] = xt[step - HALO : step]
            high, low = split(xt)
            half = product(jnp.concatenate([high, low, high], axis=1), w_cat_ref[...]) + 0.5 * bias_ref[...]
            half_ref[number, start : start + step] = half
            valid = frame_of(start, step) < end
            for lanes in lane_tiles(width):
                c0, c1 = half_slopes(slope_ref[0:1, lanes])
                value = act_half(half[:, lanes].reshape(step // 8, 8, LANE), c0, c1)
                value = jnp.where(valid, value, 0.0)
                first = first + jnp.sum(value, axis=0)
                second = second + jnp.sum(value * value, axis=0)
        row = place((total(first), total(second)))
        for block in range(sums_ref.shape[0]):
            sums_ref[block, pl.ds(item, 1), :] = row


def at(base):
    return base if isinstance(base, int) else pl.multiple_of(base, 8)


def sweep(frames, rows, end, body, init, rest=None):
    if end is None:
        carry = init
        for base in range(0, frames, rows):
            carry = body(base, False, carry)
        return carry
    live = jnp.clip(end, 0, frames)
    full, some = lax.div(live, rows), lax.div(live + (rows - 1), rows)
    carry = lax.fori_loop(0, full, lambda n, c: body(pl.multiple_of(n * rows, rows), False, c), init)
    carry = lax.fori_loop(full, some, lambda n, c: body(pl.multiple_of(n * rows, rows), True, c), carry)
    if rest is not None:

        def clear(n, c):
            rest(pl.multiple_of(n * rows, rows))
            return c

        lax.fori_loop(some, frames // rows, clear, 0)
    return carry


def both_ways(full, run):
    pl.when(full)(lambda: run(True))
    pl.when(jnp.logical_not(full))(lambda: run(False))


def where_valid(valid, value):
    return value if valid is None else jnp.where(valid, value, 0.0)


def counts(ends_ref, origin_ref, items, width):
    row = lax.broadcasted_iota(jnp.int32, (items, 1), 0)
    lengths = jnp.zeros((items, 1), jnp.int32)
    for item in range(items):
        lengths = jnp.where(row == item, ends_ref[item] + origin_ref[0], lengths)
    return lengths.astype(F32) * float(width)


def first_norm(sums_ref, count):
    sums = jnp.sum(sums_ref[...], axis=0)
    mean = 2.0 * sums[:, 0:1] / count
    var = 4.0 * sums[:, 1:2] / count - mean * mean
    return mean, lax.rsqrt(var + EPS)


def second_kernel(
    ends_ref, origin_ref, sums_ref, from_left_ref, from_right_ref, half_ref, res_ref, skip_ref,
    w_cat_ref, w_out_ref, bias_ref, slope_ref, gain_ref, shift_ref, taps_ref, tap_bias_ref, slope_mid_ref,
    mid_ref, back_ref, left_ref, right_ref, out_ref,
    halo_ref, normal_ref, coef_ref,
):
    item = pl.program_id(0)
    items = out_ref.shape[1]
    cin, frames = res_ref.shape[1:]
    width = w_cat_ref.shape[1]
    end, origin = ends_ref[item], origin_ref[0]

    @pl.when(item == 0)
    def _():
        mean, scale = first_norm(sums_ref, counts(ends_ref, origin_ref, items, width))
        coef_ref[0] = jnp.broadcast_to(scale, (items, LANE))
        coef_ref[1] = jnp.broadcast_to(scale * mean, (items, LANE))
        for side, ref in enumerate((from_left_ref, from_right_ref)):
            high, low = split(ref[...].reshape(items * HALO, cin))
            value = product(jnp.concatenate([high, low, high], axis=1), w_cat_ref[...]) + 0.5 * bias_ref[...]
            halo_ref[side] = value.reshape(items, HALO, width)

    def run(full):
        rows = SECOND_ROWS if full and frames % SECOND_ROWS == 0 else ROWS
        d_high, d_low = split(jnp.concatenate([res_ref[0], skip_ref[0]], axis=0))
        high, low = d_high.T, d_low.T
        back_ref[0] = product(jnp.concatenate([high, low, high], axis=1), w_out_ref[...])
        left_ref[0] = back_ref[0, 0:STEP]
        right_ref[0] = back_ref[0, frames - STEP : frames]

        scale, scale_mean = coef_ref[0, pl.ds(item, 1), :], coef_ref[1, pl.ds(item, 1), :]
        window = jnp.clip(end - STEP, 0, frames - HALO)
        window = pl.multiple_of(lax.div(window, 8) * 8, 8)
        tots = [jnp.zeros((8, LANE), F32)] * 10
        for lanes in lane_tiles(width):
            c0, c1 = half_slopes(slope_ref[0:1, lanes])
            gain, shift = gain_ref[0:1, lanes], shift_ref[0:1, lanes]
            factor, offset = tile(2.0 * gain * scale), tile(shift - gain * scale_mean)

            def normed(half, valid):
                return where_valid(valid, factor * act_half(half, c0, c1) + offset)

            def store(base, count, value):
                normal_ref[pl.ds(base, count), lanes] = value.reshape(count, LANE)

            frame = frame_of(-HALO, HALO)
            store(0, HALO, normed(halo_ref[0, item, :, lanes].reshape(2, 8, LANE), (frame < end) & (frame >= -origin)))
            frame = frame_of(frames, HALO)
            store(HALO + frames, HALO, normed(halo_ref[1, item, :, lanes].reshape(2, 8, LANE), frame < end))

            def fill(base, masked, carry):
                valid = frame_of(base, rows) < end if masked else None
                store(at(base + HALO), rows, normed(load(half_ref.at[0], base, rows, lanes), valid))
                return carry

            def clear(base):
                normal_ref[pl.ds(at(base + HALO), rows), lanes] = jnp.zeros((rows, LANE), F32)

            sweep(frames, rows, None if full else end, fill, 0, clear)

            taps = [tile(0.5 * taps_ref[tap : tap + 1, lanes]) for tap in range(3)]
            tap_bias = tile(0.5 * tap_bias_ref[0:1, lanes])
            m0, m1 = half_slopes(slope_mid_ref[0:1, lanes])

            def conv(base, count):
                value = taps[0] * load(normal_ref, base, count, lanes)
                value = value + taps[1] * load(normal_ref, at(base + STEP), count, lanes)
                value = value + taps[2] * load(normal_ref, at(base + HALO), count, lanes) + tap_bias
                mid_ref[0, pl.ds(base, count), lanes] = value.reshape(count, LANE)
                return value

            conv(0, STEP)
            conv(frames + STEP, STEP)

            def gather(base, masked, carry):
                valid = frame_of(base, rows) < end if masked else None
                mid = conv(at(base + STEP), rows)
                act, grad, _ = act_parts(mid, m0, m1)
                back = where_valid(valid, load(back_ref.at[0], base, rows, lanes))
                act, grad = where_valid(valid, act), where_valid(valid, grad)
                ex, ez = grad * back, grad * act
                terms = (act, act * act, back, back * act, ex, grad, ez, ex * mid, grad * mid, ez * mid)
                return tuple(old + jnp.sum(new, axis=0) for old, new in zip(carry, terms))

            sums = sweep(frames, rows, None if full else end, gather, (jnp.zeros((8, LANE), F32),) * 10)

            def edge_sums(base, mask):
                mid = load(mid_ref.at[0], at(base + STEP), HALO, lanes)
                act, grad, _ = act_parts(mid, m0, m1)
                back = load(back_ref.at[0], base, HALO, lanes)
                return [jnp.sum(jnp.where(mask, term, 0.0), axis=0) for term in (grad * back, grad, grad * act)]

            frame = frame_of(0, HALO)
            low_sums = edge_sums(0, (frame < end) & (frame + origin < STEP))
            frame = frame_of(window, HALO)
            high_sums = edge_sums(window, (frame < end) & (frame >= end - STEP))
            w0, w1, w2 = (tile(taps_ref[tap : tap + 1, lanes]) for tap in range(3))
            for term in range(4):
                tots[term] = tots[term] + sums[term]
            for term in range(3):
                plain = sums[4 + term]
                edged = (w0 + w1 + w2) * plain - w0 * low_sums[term] - w2 * high_sums[term]
                tots[4 + term] = tots[4 + term] + gain * edged
                tots[7 + term] = (
                    tots[7 + term] + 2.0 * sums[7 + term] - tap_bias_ref[0:1, lanes] * plain - shift * edged
                )
        row = place([total(value) for value in tots])
        for block in range(out_ref.shape[0]):
            out_ref[block, pl.ds(item, 1), :] = row

    both_ways(end >= frames, run)


GRAD_ROWS = 16


def second_norm(mids_ref, count):
    mids = jnp.sum(mids_ref[...], axis=0)
    m = [mids[:, term : term + 1] for term in range(10)]
    mean = 2.0 * m[0] / count
    return m, mean, lax.rsqrt(4.0 * m[1] / count - mean * mean + EPS)


def flatten(flat_ref, grads_ref, half):
    height, width = grads_ref.shape
    tiles = lane_tiles(width)
    count = len(tiles) // 2
    for number, lanes in enumerate(tiles[half * count : (half + 1) * count]):
        flat_ref[number * height : (number + 1) * height] = grads_ref[:, lanes]
    used = height * count
    if used < flat_ref.shape[0]:
        flat_ref[used:] = jnp.zeros((flat_ref.shape[0] - used, LANE), F32)


def third_kernel(
    ends_ref, origin_ref, core_ref, sums_ref, mids_ref, x_ref, res_ref, skip_ref, half_ref, mid_ref, back_ref,
    from_left_ref, from_right_ref,
    slope_ref, gain_ref, shift_ref, taps_ref, slope_mid_ref,
    u_high_ref, u_low_ref, keep_ref, send_ref,
    grad_ref, coef_ref, vector_ref, grads_ref, z_high_ref, z_low_ref, cot_ref,
):
    item = pl.program_id(0)
    items = coef_ref.shape[1]
    cin, frames = x_ref.shape[1:]
    width = half_ref.shape[2]
    end, origin = ends_ref[item], origin_ref[0]

    @pl.when(item == 0)
    def _():
        count = counts(ends_ref, origin_ref, items, width)
        mean1, scale1 = first_norm(sums_ref, count)
        m, mean2, scale2 = second_norm(mids_ref, count)
        beta = scale2 * scale2 * (2.0 * m[3] - mean2 * m[2]) / count
        alpha = m[2] / count - mean2 * beta
        mean_a = scale2 * (m[4] - alpha * m[5] - 2.0 * beta * m[6]) / count
        mean_b = scale2 * (m[7] - alpha * m[8] - 2.0 * beta * m[9]) / count
        values = (
            scale1, scale1 * mean1, scale1 * (mean_a - mean1 * scale1 * mean_b), 2.0 * scale1 * scale1 * mean_b,
            scale2, scale2 * alpha, 2.0 * scale2 * beta, 2.0 * scale2, scale2 * mean2,
        )
        for number, value in enumerate(values):
            coef_ref[number] = jnp.broadcast_to(value, (items, LANE))
        vector_ref[...] = jnp.zeros(vector_ref.shape, F32)
        grads_ref[...] = jnp.zeros(grads_ref.shape, F32)
        cot_ref[...] = jnp.zeros(cot_ref.shape, F32)

    def run(full):
        rows = THIRD_ROWS if full else ROWS
        coefs = [tile(coef_ref[number, pl.ds(item, 1), :]) for number in range(9)]
        scale1, scale_mean1, dp_a, dp_b, dr_0, dr_a, dr_b, z_0, z_a = coefs
        both = jnp.concatenate([res_ref[0], skip_ref[0]], axis=0)
        d_high, d_low = split(both)
        lane = lax.broadcasted_iota(jnp.int32, (1, LANE), 1)
        cots = cot_ref[...]
        for lanes in lane_tiles(frames):
            piece = both[:, lanes]
            cots = cots + (piece if full else jnp.where(lane + lanes.start < end, piece, 0.0))
        cot_ref[...] = cots

        for lanes in lane_tiles(width):
            m0, m1 = half_slopes(slope_mid_ref[0:1, lanes])

            def middle(base, count, valid, back):
                act, slope, rest = act_parts(load(mid_ref.at[0], base, count, lanes), m0, m1)
                grad = (dr_0 * back - dr_a) - dr_b * act
                grad = where_valid(valid, grad)
                grad_ref[pl.ds(base, count), lanes] = (grad * slope).reshape(count, LANE)
                return act, grad * rest

            frame = frame_of(-STEP, STEP)
            middle(0, STEP, (frame < end) & (frame >= -origin), from_left_ref[0:1, :, lanes])
            middle(frames + STEP, STEP, frame_of(frames, STEP) < end, from_right_ref[0:1, :, lanes])

            def inner(base, masked, carry):
                valid = frame_of(base, rows) < end if masked else None
                act, term = middle(at(base + STEP), rows, valid, load(back_ref.at[0], base, rows, lanes))
                high, low = split(where_valid(valid, z_0 * act - z_a).reshape(rows, LANE))
                z_high_ref[pl.ds(base, rows), lanes] = high
                z_low_ref[pl.ds(base, rows), lanes] = low
                return carry + jnp.sum(term, axis=0)

            def inner_clear(base):
                grad_ref[pl.ds(at(base + STEP), rows), lanes] = jnp.zeros((rows, LANE), F32)
                z_high_ref[pl.ds(base, rows), lanes] = jnp.zeros((rows, LANE), BF16)
                z_low_ref[pl.ds(base, rows), lanes] = jnp.zeros((rows, LANE), BF16)

            vector_ref[8, :, lanes] += sweep(
                frames, rows, None if full else end, inner, jnp.zeros((8, LANE), F32), inner_clear
            )

            c0, c1 = half_slopes(slope_ref[0:1, lanes])
            gain, shift = gain_ref[0:1, lanes], shift_ref[0:1, lanes]
            taps = [tile(taps_ref[tap : tap + 1, lanes]) for tap in range(3)]
            outer = gain * scale1

            def body(base, masked, carry):
                valid = frame_of(base, rows) < end if masked else None
                ahead = load(grad_ref, at(base + HALO), rows, lanes)
                here = load(grad_ref, at(base + STEP), rows, lanes)
                behind = where_valid(valid, load(grad_ref, base, rows, lanes))
                act, slope, rest = act_parts(load(half_ref.at[0], base, rows, lanes), c0, c1)
                dn = taps[0] * ahead + taps[1] * here + taps[2] * behind
                dp = where_valid(valid, (outer * dn - dp_a) - dp_b * act)
                du = dp * slope
                high, low = split(du.reshape(rows, LANE))
                u_high_ref[0, pl.ds(base, rows), lanes] = high
                u_low_ref[0, pl.ds(base, rows), lanes] = low
                terms = (du, dp * rest, here, ahead * act, here * act, behind * act)
                return tuple(old + jnp.sum(new, axis=0) for old, new in zip(carry, terms))

            def clear(base):
                u_high_ref[0, pl.ds(base, rows), lanes] = jnp.zeros((rows, LANE), BF16)
                u_low_ref[0, pl.ds(base, rows), lanes] = jnp.zeros((rows, LANE), BF16)

            sums = sweep(frames, rows, None if full else end, body, (jnp.zeros((8, LANE), F32),) * 6, clear)
            window = pl.multiple_of(lax.div(jnp.clip(end, 0, frames - HALO), 8) * 8, 8)
            row = frame_of(window, HALO)
            inside = jnp.where((row >= end) & (row < end + STEP), load(grad_ref, window, HALO, lanes), 0.0)
            plains = (
                sums[2] - grad_ref[STEP:HALO, lanes] + grad_ref[frames + STEP : frames + HALO, lanes],
                sums[2],
                sums[2] - grad_ref[frames : frames + STEP, lanes] + grad_ref[0:STEP, lanes] - jnp.sum(inside, axis=0),
            )
            factor, offset = 2.0 * outer, shift - gain * scale_mean1
            vector_ref[0, :, lanes] += sums[0]
            vector_ref[1, :, lanes] += sums[1]
            gain_sum = shift_sum = jnp.zeros((8, LANE), F32)
            for tap in range(3):
                plain, times = plains[tap], sums[3 + tap]
                vector_ref[4 + tap, :, lanes] += factor * times + offset * plain
                gain_sum = gain_sum + taps[tap] * (2.0 * scale1 * times - scale_mean1 * plain)
                shift_sum = shift_sum + taps[tap] * plain
            vector_ref[2, :, lanes] += gain_sum
            vector_ref[3, :, lanes] += shift_sum
            vector_ref[7, :, lanes] += sums[2]

        z_high, z_low = z_high_ref[...], z_low_ref[...]
        grads_ref[0 : 2 * cin] += product(
            jnp.concatenate([d_high, d_low, d_high], axis=1), jnp.concatenate([z_high, z_high, z_low], axis=0)
        )
        u_high, u_low = u_high_ref[0], u_low_ref[0]
        x_high, x_low = split(x_ref[0])
        grads_ref[2 * cin : 3 * cin] += product(
            jnp.concatenate([x_high, x_low, x_high], axis=1), jnp.concatenate([u_high, u_high, u_low], axis=0)
        )

    both_ways(end >= frames, run)

    @pl.when(item == items - 1)
    def _():
        base = 3 * cin
        for row in range(9):
            grads_ref[base + row : base + row + 1] = jnp.sum(vector_ref[row], axis=0, keepdims=True)
        column = jnp.broadcast_to(jnp.sum(cot_ref[...], axis=1, keepdims=True), cot_ref.shape).T[0:1]
        grads_ref[base + 9 : base + 10] = jnp.zeros((1, width), F32)
        for number in range(2 * cin // LANE):
            grads_ref[base + 9 + number : base + 10 + number, 0:LANE] = column[:, number * LANE : (number + 1) * LANE]
            grads_ref[base + 9 + number : base + 10 + number, width // 2 : width // 2 + LANE] = column[
                :, number * LANE : (number + 1) * LANE
            ]
        for core in range(2):

            @pl.when(core_ref[0] == core)
            def _():
                flatten(keep_ref, grads_ref, core)
                flatten(send_ref, grads_ref, 1 - core)


def outer_kernel(
    ends_ref, origin_ref, mids_ref, x_ref, mid_ref, w_out_ref, w_res_ref, w_skip_ref, gain_ref, shift_ref, slope_ref,
    bias_res_ref, bias_skip_ref, res_out_ref, skip_out_ref, coef_ref, column_ref, wide_ref, turned_ref,
):
    items = coef_ref.shape[1]
    group, cin, frames = x_ref.shape
    width = w_out_ref.shape[1]

    @pl.when(pl.program_id(0) == 0)
    def _():
        _, mean, scale = second_norm(mids_ref, counts(ends_ref, origin_ref, items, width))
        high, low = w_out_ref[0 : 2 * cin].T, w_out_ref[4 * cin : 6 * cin].T
        turned_ref[0:width] = high
        turned_ref[width : 2 * width] = high
        turned_ref[2 * width : 3 * width] = low
        coef_ref[0] = jnp.broadcast_to(2.0 * scale, (items, LANE))
        coef_ref[1] = jnp.broadcast_to(scale * mean, (items, LANE))
        for number, (w_ref, b_ref) in enumerate(((w_res_ref, bias_res_ref), (w_skip_ref, bias_skip_ref))):
            rows = slice(number * cin, (number + 1) * cin)
            column_ref[0, rows] = jnp.broadcast_to(b_ref[...], (LANE, cin)).T
            for place_of, vector_of in ((1, shift_ref), (2, gain_ref)):
                value = jnp.sum(w_ref[...] * vector_of[...], axis=1, keepdims=True)
                column_ref[place_of, rows] = jnp.broadcast_to(value, (cin, LANE))

    lane = lax.broadcasted_iota(jnp.int32, (1, LANE), 1)
    for number in range(group):
        item = pl.program_id(0) * group + number
        end = ends_ref[item]
        z_0, z_a = coef_ref[0, pl.ds(item, 1), :], coef_ref[1, pl.ds(item, 1), :]
        for lanes in lane_tiles(width):
            m0, m1 = half_slopes(slope_ref[0:1, lanes])
            for base in range(0, frames, ROWS):
                act = act_half(load(mid_ref.at[number], base + STEP, ROWS, lanes), m0, m1)
                act = jnp.where(frame_of(base, ROWS) < end, act, 0.0)
                high, low = split(act.reshape(ROWS, LANE))
                spot = number % 2
                wide_ref[spot, base : base + ROWS, lanes] = high
                wide_ref[spot, base : base + ROWS, width + lanes.start : width + lanes.stop] = low
        r_high, r_low = wide_ref[spot, :, 0:width], wide_ref[spot, :, width:]
        out = product(jnp.concatenate([r_high, r_low, r_high], axis=1), turned_ref[...]).T
        inside = column_ref[1] - z_a * column_ref[2]
        for lanes in lane_tiles(frames):
            wide = column_ref[0] + jnp.where(lane + lanes.start < end, inside, 0.0) + z_0 * out[:, lanes]
            res_out_ref[number, :, lanes] = wide[0:cin] + x_ref[number, :, lanes]
            skip_out_ref[number, :, lanes] = wide[cin : 2 * cin]


def inner_kernel(ends_ref, res_ref, u_high_ref, u_low_ref, w_cat_ref, x_grad_ref, turned_ref):
    group, cin, frames = res_ref.shape

    @pl.when(pl.program_id(0) == 0)
    def _():
        turned_ref[:, 0:cin] = w_cat_ref[0:cin].T
        turned_ref[:, cin : 2 * cin] = w_cat_ref[2 * cin : 3 * cin].T

    lane = lax.broadcasted_iota(jnp.int32, (1, LANE), 1)
    for number in range(group):
        end = ends_ref[pl.program_id(0) * group + number]
        pair = product(u_high_ref[number], turned_ref[...])
        x_grad = (pair[:, 0:cin] + pair[:, cin : 2 * cin] + product(u_low_ref[number], turned_ref[:, 0:cin])).T
        for lanes in lane_tiles(frames):
            valid = lane + lanes.start < end
            x_grad_ref[number, :, lanes] = jnp.where(valid, res_ref[number, :, lanes], 0.0) + 2.0 * x_grad[:, lanes]


def last_kernel(
    core_ref, mine_ref, theirs_ref, w_res_ref, w_skip_ref, gain_ref, shift_ref,
    w_in_out, bias_in_out, slope_in_out, gain_in_out, shift_in_out, taps_out, tap_bias_out, slope_mid_out,
    gain_mid_out, shift_mid_out, w_res_out, bias_res_out, w_skip_out, bias_skip_out,
):
    cin, width = w_res_ref.shape
    height = 3 * cin + GRAD_ROWS
    base = 3 * cin
    vectors = ((0, bias_in_out), (1, slope_in_out), (2, gain_in_out), (3, shift_in_out), (7, tap_bias_out), (8, slope_mid_out))
    groups = ((w_res_ref, w_res_out), (w_skip_ref, w_skip_out))
    columns = []
    for number, bias_out in enumerate((bias_res_out, bias_skip_out)):
        row = mine_ref[base + 9 + number : base + 10 + number]
        bias_out[...] = row
        columns.append(jnp.broadcast_to(row, (cin, cin)).T[:, 0:1])
    tiles = lane_tiles(width)
    count = len(tiles) // 2

    def place_half(ref, half):
        for number, lanes in enumerate(tiles[half * count : (half + 1) * count]):
            grads = ref.at[number * height : (number + 1) * height]
            w_in_out[lanes] = grads[2 * cin : 3 * cin].T
            for row, out in vectors:
                out[:, lanes] = grads[base + row : base + row + 1]
            taps_out[:, lanes] = grads[base + 4 : base + 7]
            gain_sum = shift_sum = jnp.zeros((1, LANE), F32)
            for group, (w_ref, w_out) in enumerate(groups):
                products = grads[group * cin : (group + 1) * cin]
                column = columns[group]
                w_out[:, lanes] = gain_ref[:, lanes] * products + shift_ref[:, lanes] * column
                gain_sum = gain_sum + jnp.sum(w_ref[:, lanes] * products, axis=0, keepdims=True)
                shift_sum = shift_sum + jnp.sum(w_ref[:, lanes] * column, axis=0, keepdims=True)
            gain_mid_out[:, lanes] = gain_sum
            shift_mid_out[:, lanes] = shift_sum

    for core in range(2):

        @pl.when(core_ref[0] == core)
        def _():
            place_half(mine_ref, core)
            place_half(theirs_ref, 1 - core)


def whole(array, space=pltpu.VMEM):
    if space is pltpu.SMEM:
        return pl.BlockSpec(memory_space=pltpu.SMEM)
    return pl.BlockSpec(array.shape, lambda item: (0,) * len(array.shape))


def per_item(array, group=1, offset=0):
    return pl.BlockSpec((group,) + array.shape[1:], lambda item: (item + offset, 0, 0))


def sds(*shape, dtype=F32):
    return jax.ShapeDtypeStruct(shape, dtype)


def cost(flops, size):
    return pl.CostEstimate(flops=flops, bytes_accessed=size, transcendentals=0)


def params():
    return pltpu.CompilerParams(dimension_semantics=("arbitrary",), vmem_limit_bytes=VMEM_LIMIT)


def exchange(pieces, axes):
    return lax.all_to_all(pieces, axes, 0, 0)


def local(
    inputs, weight_in, bias_in, slope_in, gain_in, shift_in, depthwise_weight, depthwise_bias, slope_mid, gain_mid,
    shift_mid, weight_res, bias_res, weight_skip, bias_skip, lengths, cot_res, cot_skip,
):
    items, cin, frames = inputs.shape
    width = weight_in.shape[0]
    blocks = lax.axis_size("blk")
    origin = (lax.axis_index("blk") * frames).astype(jnp.int32).reshape(1)
    core = lax.axis_index("core").astype(jnp.int32).reshape(1)
    ends = lengths - origin[0]
    bias_in, slope_in, gain_in, shift_in, tap_bias, slope_mid, gain_mid, shift_mid, bias_res, bias_skip = (
        vector.reshape(1, -1)
        for vector in (
            bias_in, slope_in, gain_in, shift_in, depthwise_bias, slope_mid, gain_mid, shift_mid, bias_res, bias_skip
        )
    )
    taps = depthwise_weight.T
    ends_spec = whole(ends, pltpu.SMEM)

    half = sds(items, frames, width)
    halo = sds(items, HALO, cin)
    sums = sds(blocks, items, LANE)
    w_cat, w_out = sds(3 * cin, width, dtype=BF16), sds(6 * cin, width, dtype=BF16)
    weights = (weight_in, bias_in, slope_in, weight_res, weight_skip, gain_mid)
    pair = 2 if items % 2 == 0 else 1
    quad = 4 if items % 4 == 0 else 1
    half, first_sums, to_left, to_right, w_cat, w_out = pl.pallas_call(
        first_kernel,
        grid=(items // pair,),
        in_specs=[ends_spec, per_item(inputs, pair)] + [whole(array) for array in weights],
        out_specs=[per_item(half, pair), whole(sums), per_item(halo, pair), per_item(halo, pair), whole(w_cat), whole(w_out)],
        out_shape=[half, sums, halo, halo, w_cat, w_out],
        compiler_params=params(),
    )(ends, inputs, *weights)

    forward = [(block, block + 1) for block in range(blocks - 1)]
    backward = [(target, source) for source, target in forward]
    first_sums = exchange(first_sums, "blk")
    from_left = lax.ppermute(to_right, "blk", forward)
    from_right = lax.ppermute(to_left, "blk", backward)

    mid, edge = sds(items, frames + HALO, width), sds(items, STEP, width)
    small = (first_sums, from_left, from_right)
    weights = (w_cat, w_out, bias_in, slope_in, gain_in, shift_in, taps, tap_bias, slope_mid)
    rounded = sds(items, frames, width, dtype=BF16)
    mid, back, to_left, to_right, mid_sums = pl.pallas_call(
        second_kernel,
        grid=(items,),
        in_specs=[ends_spec, ends_spec]
        + [whole(array) for array in small]
        + [per_item(half), per_item(cot_res), per_item(cot_skip)]
        + [whole(array) for array in weights],
        out_specs=[per_item(mid), per_item(half), per_item(edge), per_item(edge), whole(sums)],
        out_shape=[mid, sds(*half.shape), edge, edge, sums],
        scratch_shapes=[
            pltpu.VMEM((2, items, HALO, width), F32),
            pltpu.VMEM((frames + 2 * HALO, width), F32),
            pltpu.VMEM((2, items, LANE), F32),
        ],
        compiler_params=params(),
    )(ends, origin, *small, half, cot_res, cot_skip, *weights)
    from_left = lax.ppermute(to_right, "blk", forward)
    from_right = lax.ppermute(to_left, "blk", backward)
    mid_sums = exchange(mid_sums, "blk")

    small = (first_sums, mid_sums)
    large = (inputs, cot_res, cot_skip, half, mid, back, from_left, from_right)
    weights = (slope_in, gain_in, shift_in, taps, slope_mid)
    height = 3 * cin + GRAD_ROWS
    chips = blocks * lax.axis_size("side")
    piece = -(-height * (width // LANE) // (2 * chips * 8)) * 8
    flat = sds(chips * piece, LANE)
    u_high, u_low, keep, send = pl.pallas_call(
        third_kernel,
        grid=(items,),
        in_specs=[ends_spec] * 3
        + [whole(array) for array in small]
        + [per_item(array) for array in large]
        + [whole(array) for array in weights],
        out_specs=[per_item(rounded)] * 2 + [whole(flat)] * 2,
        out_shape=[rounded] * 2 + [flat] * 2,
        scratch_shapes=[
            pltpu.VMEM((frames + HALO, width), F32),
            pltpu.VMEM((9, items, LANE), F32),
            pltpu.VMEM((9, 8, width), F32),
            pltpu.VMEM((height, width), F32),
            pltpu.VMEM((frames, width), BF16),
            pltpu.VMEM((frames, width), BF16),
            pltpu.VMEM((2 * cin, LANE), F32),
        ],
        compiler_params=params(),
        cost_estimate=cost(18 * items * frames * cin * width, items * frames * width * 20),
    )(ends, origin, core, *small, *large, *weights)

    swap = [(0, 1), (1, 0)]
    keep = keep + lax.ppermute(send, "core", swap)
    keep, mid = lax.optimization_barrier((keep, mid))
    pieces = exchange(keep.reshape(chips, piece, LANE), ("blk", "side"))

    wide = sds(*inputs.shape)
    large = (inputs, mid)
    weights = (w_out, weight_res, weight_skip, gain_mid, shift_mid, slope_mid, bias_res, bias_skip)
    residual_out, skip_out = pl.pallas_call(
        outer_kernel,
        grid=(items // quad,),
        in_specs=[ends_spec] * 2
        + [whole(mid_sums)]
        + [per_item(array, quad) for array in large]
        + [whole(array) for array in weights],
        out_specs=[per_item(wide, quad)] * 2,
        out_shape=[wide] * 2,
        scratch_shapes=[pltpu.VMEM((2, items, LANE), F32), pltpu.VMEM((3, 2 * cin, LANE), F32)]
        + [pltpu.VMEM((2, frames, 2 * width), BF16), pltpu.VMEM((3 * width, 2 * cin), BF16)],
        compiler_params=params(),
        cost_estimate=cost(12 * items * frames * cin * width, items * frames * width * 8),
    )(ends, origin, mid_sums, *large, *weights)
    pieces, residual_out, u_high = lax.optimization_barrier((pieces, residual_out, u_high))
    mine = exchange(jnp.broadcast_to(jnp.sum(pieces, axis=0), pieces.shape), ("blk", "side")).reshape(-1, LANE)
    large = (cot_res, u_high, u_low)
    grad_inputs = pl.pallas_call(
        inner_kernel,
        grid=(items // quad,),
        in_specs=[ends_spec] + [per_item(array, quad) for array in large] + [whole(w_cat)],
        out_specs=per_item(wide, quad),
        out_shape=wide,
        scratch_shapes=[pltpu.VMEM((width, 2 * cin), BF16)],
        compiler_params=params(),
        cost_estimate=cost(6 * items * frames * cin * width, items * frames * width * 6),
    )(ends, *large, w_cat)
    mine, grad_inputs = lax.optimization_barrier((mine, grad_inputs))
    theirs = lax.ppermute(mine, "core", swap)
    vector, short = sds(1, width), sds(1, cin)
    ends_of = (
        sds(width, cin), vector, vector, vector, vector, sds(3, width), vector, vector, vector, vector,
        sds(cin, width), short, sds(cin, width), short,
    )
    tail = pl.pallas_call(
        last_kernel,
        in_specs=[pl.BlockSpec(memory_space=pltpu.SMEM)] + [pl.BlockSpec(memory_space=pltpu.VMEM)] * 6,
        out_shape=ends_of,
    )(core, mine, theirs, weight_res, weight_skip, gain_mid, shift_mid)
    tail = [
        value if number in (0, 10, 12) else value.T if number == 5 else value.reshape(-1)
        for number, value in enumerate(tail)
    ]
    return (residual_out, skip_out, grad_inputs) + tuple(tail)


def solution(mesh):
    devices = mesh.devices
    split_mesh = jax.sharding.Mesh(devices.reshape(devices.shape[0], -1, 2), ("blk", "side", "core"))
    batch = ("side", "core")
    items = P(batch, None, "blk")
    return jax.shard_map(
        local,
        mesh=split_mesh,
        in_specs=(items,) + (P(),) * 14 + (P(batch), items, items),
        out_specs=(items,) * 3 + (P(),) * 14,
        check_vma=False,
    )
```

```python
import functools

import jax
import jax.numpy as jnp
from jax import lax
from jax.experimental import pallas as pl
from jax.experimental.pallas import tpu as pltpu
from jax.sharding import PartitionSpec as P

STEP = 8
HALO = 2 * STEP
EPS = 1e-05
LANE = 128
ROWS = 64
SECOND_ROWS = 128
PIECE = 256
THIRD_ROWS = 128
F32 = jnp.float32
BF16 = jnp.bfloat16
VMEM_LIMIT = 60 * 1024 * 1024


def split(value):
    high = value.astype(BF16)
    low = (value - high.astype(F32)).astype(BF16)
    return high, low


def product(left, right):
    return jnp.dot(left, right, preferred_element_type=F32)


def product_nt(left, right):
    return lax.dot_general(left, right, (((1,), (1,)), ((), ())), preferred_element_type=F32)


def tile(row):
    return jnp.broadcast_to(row, (8, LANE))


def load(ref, base, rows, lanes):
    return ref[pl.ds(base, rows), lanes].reshape(rows // 8, 8, LANE)


def frame_of(base, rows):
    shape = (rows // 8, 8, LANE)
    return lax.broadcasted_iota(jnp.int32, shape, 0) * 8 + lax.broadcasted_iota(jnp.int32, shape, 1) + base


def half_slopes(row):
    return tile(0.5 - 0.5 * row), tile(0.5 + 0.5 * row)


def act_half(half, c0, c1):
    return half * (c1 + c0 * jnp.tanh(half))


def act_parts(half, c0, c1):
    th = jnp.tanh(half)
    ratio = c1 + c0 * th
    act = half * ratio
    cut = half - act
    return act, ratio + cut * (1.0 + th), cut


def total(value):
    return jnp.sum(jnp.sum(value, axis=0, keepdims=True), axis=1, keepdims=True)


def place(values):
    lane = lax.broadcasted_iota(jnp.int32, (1, LANE), 1)
    row = jnp.zeros((1, LANE), F32)
    for position, value in enumerate(values):
        row = jnp.where(lane == position, value, row)
    return row


def lane_tiles(width):
    return [slice(start, start + LANE) for start in range(0, width, LANE)]


def first_kernel(
    ends_ref, x_ref, res_l_ref, res_r_ref, skip_l_ref, skip_r_ref, w_in_ref, bias_ref, slope_ref,
    w_res_ref, w_skip_ref, gain_ref,
    sums_ref, left_ref, right_ref, w_cat_ref, w_out_ref,
):
    group, cin, frames = x_ref.shape
    width = w_in_ref.shape[0]

    @pl.when(pl.program_id(0) == 0)
    def _():
        high, low = split(0.5 * w_in_ref[...].T)
        w_cat_ref[0:cin] = high
        w_cat_ref[cin : 2 * cin] = high
        w_cat_ref[2 * cin : 3 * cin] = low
        row = lax.broadcasted_iota(jnp.int32, (LANE, width), 0)
        bias = jnp.broadcast_to(0.5 * bias_ref[...], (LANE, width))
        near = bias.astype(BF16).astype(F32)
        w_cat_ref[3 * cin :] = jnp.where(row == 0, near, jnp.where(row == 1, bias - near, 0.0)).astype(BF16)
        for number, ref in enumerate((w_res_ref, w_skip_ref)):
            high, low = split(ref[...] * gain_ref[...])
            start = number * cin
            w_out_ref[start : start + cin] = high
            w_out_ref[2 * cin + start : 3 * cin + start] = high
            w_out_ref[4 * cin + start : 5 * cin + start] = low

    step = min(PIECE, frames)
    for number in range(group):
        item = pl.program_id(0) * group + number
        end = ends_ref[item]
        first = second = jnp.zeros((8, LANE), F32)
        for start in range(0, frames, step):
            xt = x_ref[number, :, start : start + step].astype(BF16).T
            ones = jnp.ones((step, LANE), BF16)
            weights = jnp.concatenate([w_cat_ref[0:cin], w_cat_ref[3 * cin :]], axis=0)
            half = product(jnp.concatenate([xt, ones], axis=1), weights)
            valid = frame_of(start, step) < end
            for lanes in lane_tiles(width):
                c0, c1 = half_slopes(slope_ref[0:1, lanes])
                value = act_half(half[:, lanes].reshape(step // 8, 8, LANE), c0, c1)
                value = jnp.where(valid, value, 0.0)
                first = first + jnp.sum(value, axis=0)
                second = second + jnp.sum(value * value, axis=0)
        row = place((total(first), total(second)))
        for block in range(sums_ref.shape[0]):
            sums_ref[block, pl.ds(item, 1), :] = row
        left_ref[number, :, 0:cin] = x_ref[number, :, 0:LANE].T[0:HALO]
        right_ref[number, :, 0:cin] = x_ref[number, :, frames - LANE : frames].T[LANE - HALO : LANE]
        left_ref[number, 0:STEP, cin : 2 * cin] = res_l_ref[number].T[0:STEP]
        left_ref[number, STEP:HALO, cin : 2 * cin] = skip_l_ref[number].T[0:STEP]
        right_ref[number, 0:STEP, cin : 2 * cin] = res_r_ref[number].T[LANE - STEP : LANE]
        right_ref[number, STEP:HALO, cin : 2 * cin] = skip_r_ref[number].T[LANE - STEP : LANE]


def at(base):
    return base if isinstance(base, int) else pl.multiple_of(base, 8)


def sweep(frames, rows, end, body, init, rest=None):
    if end is None:
        carry = init
        for base in range(0, frames, rows):
            carry = body(base, False, carry)
        return carry
    live = jnp.clip(end, 0, frames)
    full, some = lax.div(live, rows), lax.div(live + (rows - 1), rows)
    carry = lax.fori_loop(0, full, lambda n, c: body(pl.multiple_of(n * rows, rows), False, c), init)
    carry = lax.fori_loop(full, some, lambda n, c: body(pl.multiple_of(n * rows, rows), True, c), carry)
    if rest is not None:

        def clear(n, c):
            rest(pl.multiple_of(n * rows, rows))
            return c

        lax.fori_loop(some, frames // rows, clear, 0)
    return carry


def both_ways(full, run):
    pl.when(full)(lambda: run(True))
    pl.when(jnp.logical_not(full))(lambda: run(False))


def where_valid(valid, value):
    return value if valid is None else jnp.where(valid, value, 0.0)


def counts(ends_ref, origin_ref, items, width):
    row = lax.broadcasted_iota(jnp.int32, (items, 1), 0)
    lengths = jnp.zeros((items, 1), jnp.int32)
    for item in range(items):
        lengths = jnp.where(row == item, ends_ref[item] + origin_ref[0], lengths)
    return lengths.astype(F32) * float(width)


def first_norm(sums_ref, count):
    sums = jnp.sum(sums_ref[...], axis=0)
    mean = 2.0 * sums[:, 0:1] / count
    var = 4.0 * sums[:, 1:2] / count - mean * mean
    return mean, lax.rsqrt(var + EPS)


def second_kernel(
    ends_ref, origin_ref, sums_ref, from_left_ref, from_right_ref, x_all, res_all, skip_all,
    w_cat_ref, w_out_ref, slope_ref, gain_ref, shift_ref, taps_ref, tap_bias_ref, slope_mid_ref,
    half_all, mid_all, back_all, edge_ref, out_ref,
    halo_ref, normal_ref, coef_ref,
):
    items = out_ref.shape[1]
    group, frames, width = half_all.shape
    cin = x_all.shape[1]
    origin = origin_ref[0]

    @pl.when(pl.program_id(0) == 0)
    def _():
        mean, scale = first_norm(sums_ref, counts(ends_ref, origin_ref, items, width))
        coef_ref[0] = jnp.broadcast_to(scale, (items, LANE))
        coef_ref[1] = jnp.broadcast_to(scale * mean, (items, LANE))
        for side, ref in enumerate((from_left_ref, from_right_ref)):
            high, low = split(ref[:, :, 0:cin].reshape(items * HALO, cin))
            ones = jnp.ones((items * HALO, LANE), BF16)
            value = product(jnp.concatenate([high, low, high, ones], axis=1), w_cat_ref[...])
            halo_ref[side] = value.reshape(items, HALO, width)
            cots = jnp.concatenate([ref[:, 0:STEP, cin : 2 * cin], ref[:, STEP:HALO, cin : 2 * cin]], axis=2)
            high, low = split(cots.reshape(items * STEP, 2 * cin))
            value = product(jnp.concatenate([high, low, high], axis=1), w_out_ref[...])
            edge_ref[:, side * STEP : (side + 1) * STEP, :] = value.reshape(items, STEP, width)

    def run(number, item, end, full):
        half_ref, res_ref, skip_ref, mid_ref, back_ref = (
            ref.at[number : number + 1] for ref in (half_all, res_all, skip_all, mid_all, back_all)
        )
        high, low = split(x_all[number].T)
        ones = jnp.ones((frames, LANE), BF16)
        half_ref[0] = product(jnp.concatenate([high, low, high, ones], axis=1), w_cat_ref[...])
        rows = SECOND_ROWS if full and frames % SECOND_ROWS == 0 else ROWS
        d_high, d_low = split(jnp.concatenate([res_ref[0], skip_ref[0]], axis=0))
        high, low = d_high.T, d_low.T
        back_ref[0] = product(jnp.concatenate([high, low, high], axis=1), w_out_ref[...])

        scale, scale_mean = coef_ref[0, pl.ds(item, 1), :], coef_ref[1, pl.ds(item, 1), :]
        window = jnp.clip(end - STEP, 0, frames - HALO)
        window = pl.multiple_of(lax.div(window, 8) * 8, 8)
        tots = [jnp.zeros((8, LANE), F32)] * 10
        for lanes in lane_tiles(width):
            c0, c1 = half_slopes(slope_ref[0:1, lanes])
            gain, shift = gain_ref[0:1, lanes], shift_ref[0:1, lanes]
            factor, offset = 2.0 * gain * scale, shift - gain * scale_mean
            hole = tile(-offset / factor)

            def normed(half, valid):
                value = act_half(half, c0, c1)
                return value if valid is None else jnp.where(valid, value, hole)

            def store(base, count, value):
                normal_ref[pl.ds(base, count), lanes] = value.reshape(count, LANE)

            frame = frame_of(-HALO, HALO)
            store(0, HALO, normed(halo_ref[0, item, :, lanes].reshape(2, 8, LANE), (frame < end) & (frame >= -origin)))
            frame = frame_of(frames, HALO)
            store(HALO + frames, HALO, normed(halo_ref[1, item, :, lanes].reshape(2, 8, LANE), frame < end))

            def fill(base, masked, carry):
                valid = frame_of(base, rows) < end if masked else None
                store(at(base + HALO), rows, normed(load(half_ref.at[0], base, rows, lanes), valid))
                return carry

            def clear(base):
                normal_ref[pl.ds(at(base + HALO), rows), lanes] = jnp.broadcast_to(-offset / factor, (rows, LANE))

            sweep(frames, rows, None if full else end, fill, 0, clear)

            rows_of = [0.5 * taps_ref[tap : tap + 1, lanes] for tap in range(3)]
            taps = [tile(factor * row) for row in rows_of]
            tap_bias = tile(0.5 * tap_bias_ref[0:1, lanes] + offset * (rows_of[0] + rows_of[1] + rows_of[2]))
            m0, m1 = half_slopes(slope_mid_ref[0:1, lanes])

            def conv(base, count):
                value = taps[0] * load(normal_ref, base, count, lanes)
                value = value + taps[1] * load(normal_ref, at(base + STEP), count, lanes)
                value = value + taps[2] * load(normal_ref, at(base + HALO), count, lanes) + tap_bias
                mid_ref[0, pl.ds(base, count), lanes] = value.reshape(count, LANE)
                return value

            conv(0, STEP)
            conv(frames + STEP, STEP)

            def gather(base, masked, carry):
                valid = frame_of(base, rows) < end if masked else None
                mid = conv(at(base + STEP), rows)
                act, grad, _ = act_parts(mid, m0, m1)
                back = load(back_ref.at[0], base, rows, lanes)
                act, grad, back = where_valid(valid, act), where_valid(valid, grad), where_valid(valid, back)
                ex, ez = grad * back, grad * act
                terms = (act, act * act, back, back * act, ex, grad, ez, ex * mid, grad * mid, ez * mid)
                return tuple(old + jnp.sum(new, axis=0) for old, new in zip(carry, terms))

            sums = sweep(frames, rows, None if full else end, gather, (jnp.zeros((8, LANE), F32),) * 10)

            def edge_sums(base, mask):
                mid = load(mid_ref.at[0], at(base + STEP), HALO, lanes)
                act, grad, _ = act_parts(mid, m0, m1)
                back = load(back_ref.at[0], base, HALO, lanes)
                return [jnp.sum(jnp.where(mask, term, 0.0), axis=0) for term in (grad * back, grad, grad * act)]

            frame = frame_of(0, HALO)
            low_sums = edge_sums(0, (frame < end) & (frame + origin < STEP))
            frame = frame_of(window, HALO)
            high_sums = edge_sums(window, (frame < end) & (frame >= end - STEP))
            w0, w1, w2 = (tile(taps_ref[tap : tap + 1, lanes]) for tap in range(3))
            for term in range(4):
                tots[term] = tots[term] + sums[term]
            for term in range(3):
                plain = sums[4 + term]
                edged = (w0 + w1 + w2) * plain - w0 * low_sums[term] - w2 * high_sums[term]
                tots[4 + term] = tots[4 + term] + gain * edged
                tots[7 + term] = (
                    tots[7 + term] + 2.0 * sums[7 + term] - tap_bias_ref[0:1, lanes] * plain - shift * edged
                )

        row = place([total(value) for value in tots])
        for block in range(out_ref.shape[0]):
            out_ref[block, pl.ds(item, 1), :] = row

    for number in range(group):
        item = pl.program_id(0) * group + number
        end = ends_ref[item]
        both_ways(end >= frames, functools.partial(run, number, item, end))


GRAD_ROWS = 16


def second_norm(mids_ref, count):
    mids = jnp.sum(mids_ref[...], axis=0)
    m = [mids[:, term : term + 1] for term in range(10)]
    mean = 2.0 * m[0] / count
    return m, mean, lax.rsqrt(4.0 * m[1] / count - mean * mean + EPS)


def flatten(flat_ref, grads_ref, half):
    height, width = grads_ref.shape
    tiles = lane_tiles(width)
    count = len(tiles) // 2
    for number, lanes in enumerate(tiles[half * count : (half + 1) * count]):
        flat_ref[number * height : (number + 1) * height] = grads_ref[:, lanes]
    used = height * count
    if used < flat_ref.shape[0]:
        flat_ref[used:] = jnp.zeros((flat_ref.shape[0] - used, LANE), F32)


def third_kernel(
    ends_ref, origin_ref, core_ref, sums_ref, mids_ref, x_all, res_all, skip_all, half_all, mid_all, back_all, edge_all,
    slope_ref, gain_ref, shift_ref, taps_ref, slope_mid_ref,
    r_high_all, r_low_all, u_high_all, u_low_all, keep_ref, send_ref,
    grad_ref, coef_ref, vector_ref, grads_ref, cot_ref,
):
    items = coef_ref.shape[1]
    group, cin, frames = x_all.shape
    width = half_all.shape[2]
    origin = origin_ref[0]

    @pl.when(pl.program_id(0) == 0)
    def _():
        count = counts(ends_ref, origin_ref, items, width)
        mean1, scale1 = first_norm(sums_ref, count)
        m, mean2, scale2 = second_norm(mids_ref, count)
        beta = scale2 * scale2 * (2.0 * m[3] - mean2 * m[2]) / count
        alpha = m[2] / count - mean2 * beta
        mean_a = scale2 * (m[4] - alpha * m[5] - 2.0 * beta * m[6]) / count
        mean_b = scale2 * (m[7] - alpha * m[8] - 2.0 * beta * m[9]) / count
        values = (
            scale1, scale1 * mean1, scale1 * (mean_a - mean1 * scale1 * mean_b), 2.0 * scale1 * scale1 * mean_b,
            scale2, alpha, 2.0 * beta, scale2 * mean2,
        )
        for number, value in enumerate(values):
            coef_ref[number] = jnp.broadcast_to(value, (items, LANE))
        vector_ref[...] = jnp.zeros(vector_ref.shape, F32)
        grads_ref[...] = jnp.zeros(grads_ref.shape, F32)
        cot_ref[...] = jnp.zeros(cot_ref.shape, F32)

    def run(number, item, end, full):
        x_ref, res_ref, skip_ref, half_ref, mid_ref, back_ref, edge_ref = (
            ref.at[number : number + 1] for ref in (x_all, res_all, skip_all, half_all, mid_all, back_all, edge_all)
        )
        r_high_ref, r_low_ref, u_high_ref, u_low_ref = (
            ref.at[number : number + 1] for ref in (r_high_all, r_low_all, u_high_all, u_low_all)
        )
        rows = THIRD_ROWS if full else ROWS
        coefs = [tile(coef_ref[number, pl.ds(item, 1), :]) for number in range(8)]
        scale1, scale_mean1, dp_a, dp_b, scale2, dr_a, dr_b, z_a = coefs
        both = jnp.concatenate([res_ref[0], skip_ref[0]], axis=0)
        d_high, d_low = split(both)
        lane = lax.broadcasted_iota(jnp.int32, (1, LANE), 1)
        cots = jnp.zeros((2 * cin, LANE), F32)
        for lanes in lane_tiles(frames):
            piece = both[:, lanes]
            cots = cots + (piece if full else jnp.where(lane + lanes.start < end, piece, 0.0))
        cot_ref[0] += cots
        cot_ref[1] += z_a[0:1] * cots

        for lanes in lane_tiles(width):
            m0, m1 = half_slopes(slope_mid_ref[0:1, lanes])

            def middle(base, count, valid, back):
                act, slope, cut = act_parts(load(mid_ref.at[0], base, count, lanes), m0, m1)
                grad = (back - dr_a) - dr_b * act
                grad = where_valid(valid, grad)
                grad_ref[pl.ds(base, count), lanes] = (grad * slope).reshape(count, LANE)
                return act, grad * cut

            frame = frame_of(-STEP, STEP)
            middle(0, STEP, (frame < end) & (frame >= -origin), edge_ref[0:1, 0:STEP, lanes])
            middle(frames + STEP, STEP, frame_of(frames, STEP) < end, edge_ref[0:1, STEP:HALO, lanes])

            def inner(base, masked, carry):
                valid = frame_of(base, rows) < end if masked else None
                act, term = middle(at(base + STEP), rows, valid, load(back_ref.at[0], base, rows, lanes))
                high, low = split(where_valid(valid, act).reshape(rows, LANE))
                r_high_ref[0, pl.ds(base, rows), lanes] = high
                r_low_ref[0, pl.ds(base, rows), lanes] = low
                return carry + jnp.sum(term, axis=0)

            def inner_clear(base):
                grad_ref[pl.ds(at(base + STEP), rows), lanes] = jnp.zeros((rows, LANE), F32)
                r_high_ref[0, pl.ds(base, rows), lanes] = jnp.zeros((rows, LANE), BF16)
                r_low_ref[0, pl.ds(base, rows), lanes] = jnp.zeros((rows, LANE), BF16)

            vector_ref[8, :, lanes] += scale2 / m0 * sweep(
                frames, rows, None if full else end, inner, jnp.zeros((8, LANE), F32), inner_clear
            )

            c0, c1 = half_slopes(slope_ref[0:1, lanes])
            gain, shift = gain_ref[0:1, lanes], shift_ref[0:1, lanes]
            taps = [tile(taps_ref[tap : tap + 1, lanes]) for tap in range(3)]
            outer = gain * scale1
            scaled = [tap * (outer * scale2) for tap in taps]

            def body(base, masked, carry):
                valid = frame_of(base, rows) < end if masked else None
                ahead = load(grad_ref, at(base + HALO), rows, lanes)
                here = load(grad_ref, at(base + STEP), rows, lanes)
                behind = where_valid(valid, load(grad_ref, base, rows, lanes))
                act, slope, cut = act_parts(load(half_ref.at[0], base, rows, lanes), c0, c1)
                dp = scaled[0] * ahead + scaled[1] * here + scaled[2] * behind
                dp = where_valid(valid, (dp - dp_a) - dp_b * act)
                du = dp * slope
                high, low = split(du.reshape(rows, LANE))
                u_high_ref[0, pl.ds(base, rows), lanes] = high
                u_low_ref[0, pl.ds(base, rows), lanes] = low
                terms = (dp * cut, here, ahead * act, here * act, behind * act)
                return tuple(old + jnp.sum(new, axis=0) for old, new in zip(carry, terms))

            def clear(base):
                u_high_ref[0, pl.ds(base, rows), lanes] = jnp.zeros((rows, LANE), BF16)
                u_low_ref[0, pl.ds(base, rows), lanes] = jnp.zeros((rows, LANE), BF16)

            sums = sweep(frames, rows, None if full else end, body, (jnp.zeros((8, LANE), F32),) * 5, clear)
            window = pl.multiple_of(lax.div(jnp.clip(end, 0, frames - HALO), 8) * 8, 8)
            row = frame_of(window, HALO)
            inside = jnp.where((row >= end) & (row < end + STEP), load(grad_ref, window, HALO, lanes), 0.0)
            plains = (
                sums[1] - grad_ref[STEP:HALO, lanes] + grad_ref[frames + STEP : frames + HALO, lanes],
                sums[1],
                sums[1] - grad_ref[frames : frames + STEP, lanes] + grad_ref[0:STEP, lanes] - jnp.sum(inside, axis=0),
            )
            factor, offset = 2.0 * outer, shift - gain * scale_mean1
            vector_ref[1, :, lanes] += sums[0] / c0
            gain_sum = shift_sum = jnp.zeros((8, LANE), F32)
            for tap in range(3):
                plain, times = scale2 * plains[tap], scale2 * sums[2 + tap]
                vector_ref[4 + tap, :, lanes] += factor * times + offset * plain
                gain_sum = gain_sum + taps[tap] * (2.0 * scale1 * times - scale_mean1 * plain)
                shift_sum = shift_sum + taps[tap] * plain
            vector_ref[2, :, lanes] += gain_sum
            vector_ref[3, :, lanes] += shift_sum
            vector_ref[7, :, lanes] += scale2 * sums[1]

        r_high, r_low = r_high_ref[0], r_low_ref[0]
        mixed = product(
            jnp.concatenate([d_high, d_low, d_high], axis=1), jnp.concatenate([r_high, r_high, r_low], axis=0)
        )
        z_0 = 2.0 * scale2[0:1]
        for lanes in lane_tiles(width):
            grads_ref[0 : 2 * cin, lanes] += z_0 * mixed[:, lanes]
        u_high, u_low = u_high_ref[0], u_low_ref[0]
        x_high, x_low = split(x_ref[0])
        rows_of = jnp.concatenate([x_high, x_low, x_high], axis=1)
        ones = jnp.ones((GRAD_ROWS, frames), BF16)
        ones = jnp.concatenate([ones, jnp.zeros((GRAD_ROWS, frames), BF16), ones], axis=1)
        grads_ref[2 * cin : 3 * cin + GRAD_ROWS] += product(
            jnp.concatenate([rows_of, ones], axis=0), jnp.concatenate([u_high, u_high, u_low], axis=0)
        )

    for number in range(group):
        item = pl.program_id(0) * group + number
        end = ends_ref[item]
        both_ways(end >= frames, functools.partial(run, number, item, end))

    @pl.when(pl.program_id(0) == items // group - 1)
    def _():
        base = 3 * cin
        grads_ref[0 : 2 * cin] = grads_ref[0 : 2 * cin] - jnp.sum(cot_ref[1], axis=1, keepdims=True)
        for row in range(1, 9):
            grads_ref[base + row : base + row + 1] = jnp.sum(vector_ref[row], axis=0, keepdims=True)
        column = jnp.broadcast_to(jnp.sum(cot_ref[0], axis=1, keepdims=True), (2 * cin, LANE)).T[0:1]
        grads_ref[base + 9 : base + 10] = jnp.zeros((1, width), F32)
        for number in range(2 * cin // LANE):
            grads_ref[base + 9 + number : base + 10 + number, 0:LANE] = column[:, number * LANE : (number + 1) * LANE]
            grads_ref[base + 9 + number : base + 10 + number, width // 2 : width // 2 + LANE] = column[
                :, number * LANE : (number + 1) * LANE
            ]
        for core in range(2):

            @pl.when(core_ref[0] == core)
            def _():
                flatten(keep_ref, grads_ref, core)
                flatten(send_ref, grads_ref, 1 - core)


def outer_kernel(
    ends_ref, origin_ref, mids_ref, x_ref, res_ref, r_high_ref, r_low_ref, u_high_ref, u_low_ref,
    w_cat_ref, w_out_ref, w_res_ref, w_skip_ref, gain_ref, shift_ref, bias_res_ref, bias_skip_ref, *rest_refs, offset,
):
    res_out_ref, skip_out_ref, x_grad_ref, coef_ref, column_ref, out_turned_ref, in_turned_ref = rest_refs[-7:]
    items = coef_ref.shape[1]
    group, cin, frames = x_ref.shape
    width = w_cat_ref.shape[1]

    @pl.when(pl.program_id(0) == 0)
    def _():
        _, mean, scale = second_norm(mids_ref, counts(ends_ref, origin_ref, items, width))
        coef_ref[0] = jnp.broadcast_to(2.0 * scale, (items, LANE))
        coef_ref[1] = jnp.broadcast_to(scale * mean, (items, LANE))
        high, low = w_out_ref[0 : 2 * cin].T, w_out_ref[4 * cin : 6 * cin].T
        out_turned_ref[0:width] = high
        out_turned_ref[width : 2 * width] = high
        out_turned_ref[2 * width : 3 * width] = low
        in_turned_ref[:, 0:cin] = w_cat_ref[0:cin].T
        in_turned_ref[:, cin : 2 * cin] = w_cat_ref[2 * cin : 3 * cin].T
        for number, (w_ref, b_ref) in enumerate(((w_res_ref, bias_res_ref), (w_skip_ref, bias_skip_ref))):
            rows = slice(number * cin, (number + 1) * cin)
            column_ref[0, rows] = jnp.broadcast_to(b_ref[...], (LANE, cin)).T
            for spot, vector_of in ((1, shift_ref), (2, gain_ref)):
                value = jnp.sum(w_ref[...] * vector_of[...], axis=1, keepdims=True)
                column_ref[spot, rows] = jnp.broadcast_to(value, (cin, LANE))

    lane = lax.broadcasted_iota(jnp.int32, (1, LANE), 1)
    for number in range(group):
        item = offset + pl.program_id(0) * group + number
        end = ends_ref[item]
        z_0, z_a = coef_ref[0, pl.ds(item, 1), :], coef_ref[1, pl.ds(item, 1), :]
        r_high, r_low = r_high_ref[number], r_low_ref[number]
        out = product(jnp.concatenate([r_high, r_low, r_high], axis=1), out_turned_ref[...]).T
        pair = product(u_high_ref[number], in_turned_ref[...])
        x_grad = (pair[:, 0:cin] + pair[:, cin : 2 * cin] + product(u_low_ref[number], in_turned_ref[:, 0:cin])).T
        inside = column_ref[1] - z_a * column_ref[2]
        for lanes in lane_tiles(frames):
            valid = lane + lanes.start < end
            wide = column_ref[0] + jnp.where(valid, inside, 0.0) + z_0 * out[:, lanes]
            res_out_ref[number, :, lanes] = wide[0:cin] + x_ref[number, :, lanes]
            skip_out_ref[number, :, lanes] = wide[cin : 2 * cin]
            x_grad_ref[number, :, lanes] = jnp.where(valid, res_ref[number, :, lanes], 0.0) + 2.0 * x_grad[:, lanes]


def last_kernel(
    core_ref, mine_ref, theirs_ref, w_res_ref, w_skip_ref, gain_ref, shift_ref,
    w_in_out, bias_in_out, slope_in_out, gain_in_out, shift_in_out, taps_out, tap_bias_out, slope_mid_out,
    gain_mid_out, shift_mid_out, w_res_out, bias_res_out, w_skip_out, bias_skip_out,
):
    cin, width = w_res_ref.shape
    height = 3 * cin + GRAD_ROWS
    base = 3 * cin
    vectors = ((0, bias_in_out), (1, slope_in_out), (2, gain_in_out), (3, shift_in_out), (7, tap_bias_out), (8, slope_mid_out))
    groups = ((w_res_ref, w_res_out), (w_skip_ref, w_skip_out))
    columns = []
    for number, bias_out in enumerate((bias_res_out, bias_skip_out)):
        row = mine_ref[base + 9 + number : base + 10 + number]
        bias_out[...] = row
        columns.append(jnp.broadcast_to(row, (cin, cin)).T[:, 0:1])
    tiles = lane_tiles(width)
    count = len(tiles) // 2

    def place_half(ref, half):
        for number, lanes in enumerate(tiles[half * count : (half + 1) * count]):
            grads = ref.at[number * height : (number + 1) * height]
            w_in_out[lanes] = grads[2 * cin : 3 * cin].T
            for row, out in vectors:
                out[:, lanes] = grads[base + row : base + row + 1]
            taps_out[:, lanes] = grads[base + 4 : base + 7]
            gain_sum = shift_sum = jnp.zeros((1, LANE), F32)
            for group, (w_ref, w_out) in enumerate(groups):
                products = grads[group * cin : (group + 1) * cin]
                column = columns[group]
                w_out[:, lanes] = gain_ref[:, lanes] * products + shift_ref[:, lanes] * column
                gain_sum = gain_sum + jnp.sum(w_ref[:, lanes] * products, axis=0, keepdims=True)
                shift_sum = shift_sum + jnp.sum(w_ref[:, lanes] * column, axis=0, keepdims=True)
            gain_mid_out[:, lanes] = gain_sum
            shift_mid_out[:, lanes] = shift_sum

    for core in range(2):

        @pl.when(core_ref[0] == core)
        def _():
            place_half(mine_ref, core)
            place_half(theirs_ref, 1 - core)


def whole(array, space=pltpu.VMEM):
    if space is pltpu.SMEM:
        return pl.BlockSpec(memory_space=pltpu.SMEM)
    return pl.BlockSpec(array.shape, lambda item: (0,) * len(array.shape))


def per_item(array, group=1, offset=0):
    return pl.BlockSpec((group,) + array.shape[1:], lambda item: (item + offset, 0, 0))


def edge_block(array, group, position):
    return pl.BlockSpec((group, array.shape[1], LANE), lambda item: (item, 0, position))


def sds(*shape, dtype=F32):
    return jax.ShapeDtypeStruct(shape, dtype)


def cost(flops, size):
    return pl.CostEstimate(flops=flops, bytes_accessed=size, transcendentals=0)


def params():
    return pltpu.CompilerParams(dimension_semantics=("arbitrary",), vmem_limit_bytes=VMEM_LIMIT)


def exchange(pieces, axes):
    return lax.all_to_all(pieces, axes, 0, 0)


def local(
    inputs, weight_in, bias_in, slope_in, gain_in, shift_in, depthwise_weight, depthwise_bias, slope_mid, gain_mid,
    shift_mid, weight_res, bias_res, weight_skip, bias_skip, lengths, cot_res, cot_skip,
):
    items, cin, frames = inputs.shape
    width = weight_in.shape[0]
    blocks = lax.axis_size("blk")
    origin = (lax.axis_index("blk") * frames).astype(jnp.int32).reshape(1)
    core = lax.axis_index("core").astype(jnp.int32).reshape(1)
    ends = lengths - origin[0]
    bias_in, slope_in, gain_in, shift_in, tap_bias, slope_mid, gain_mid, shift_mid, bias_res, bias_skip = (
        vector.reshape(1, -1)
        for vector in (
            bias_in, slope_in, gain_in, shift_in, depthwise_bias, slope_mid, gain_mid, shift_mid, bias_res, bias_skip
        )
    )
    taps = depthwise_weight.T
    ends_spec = whole(ends, pltpu.SMEM)

    half = sds(items, frames, width)
    halo = sds(items, HALO, 2 * cin)
    last = frames // LANE - 1
    sums = sds(blocks, items, LANE)
    w_cat, w_out = sds(3 * cin + LANE, width, dtype=BF16), sds(6 * cin, width, dtype=BF16)
    weights = (weight_in, bias_in, slope_in, weight_res, weight_skip, gain_mid)
    pair = 2 if items % 2 == 0 else 1
    quad = 4 if items % 4 == 0 else 1
    first_sums, to_left, to_right, w_cat, w_out = pl.pallas_call(
        first_kernel,
        grid=(items // quad,),
        in_specs=[ends_spec, per_item(inputs, quad)]
        + [edge_block(array, quad, spot) for array in (cot_res, cot_skip) for spot in (0, last)]
        + [whole(array) for array in weights],
        out_specs=[whole(sums), per_item(halo, quad), per_item(halo, quad), whole(w_cat), whole(w_out)],
        out_shape=[sums, halo, halo, w_cat, w_out],
        compiler_params=params(),
    )(ends, inputs, cot_res, cot_res, cot_skip, cot_skip, *weights)

    forward = [(block, block + 1) for block in range(blocks - 1)]
    backward = [(target, source) for source, target in forward]
    first_sums = exchange(first_sums, "blk")
    from_left = lax.ppermute(to_right, "blk", forward)
    from_right = lax.ppermute(to_left, "blk", backward)

    mid, edge = sds(items, frames + HALO, width), sds(items, HALO, width)
    small = (first_sums, from_left, from_right)
    weights = (w_cat, w_out, slope_in, gain_in, shift_in, taps, tap_bias, slope_mid)
    rounded = sds(items, frames, width, dtype=BF16)
    half, mid, back, edge, mid_sums = pl.pallas_call(
        second_kernel,
        grid=(items // pair,),
        in_specs=[ends_spec, ends_spec]
        + [whole(array) for array in small]
        + [per_item(array, pair) for array in (inputs, cot_res, cot_skip)]
        + [whole(array) for array in weights],
        out_specs=[per_item(half, pair), per_item(mid, pair), per_item(half, pair), whole(edge), whole(sums)],
        out_shape=[half, mid, half, edge, sums],
        scratch_shapes=[
            pltpu.VMEM((2, items, HALO, width), F32),
            pltpu.VMEM((frames + 2 * HALO, width), F32),
            pltpu.VMEM((2, items, LANE), F32),
        ],
        compiler_params=params(),
        cost_estimate=cost(20 * items * frames * cin * width, items * frames * width * 14),
    )(ends, origin, *small, inputs, cot_res, cot_skip, *weights)
    mid_sums = exchange(mid_sums, "blk")

    small = (first_sums, mid_sums)
    large = (inputs, cot_res, cot_skip, half, mid, back, edge)
    weights = (slope_in, gain_in, shift_in, taps, slope_mid)
    wide = sds(*inputs.shape)
    height = 3 * cin + GRAD_ROWS
    chips = blocks * lax.axis_size("side")
    piece = -(-height * (width // LANE) // (2 * chips * 8)) * 8
    flat = sds(chips * piece, LANE)
    r_high, r_low, u_high, u_low, keep, send = pl.pallas_call(
        third_kernel,
        grid=(items // pair,),
        in_specs=[ends_spec] * 3
        + [whole(array) for array in small]
        + [per_item(array, pair) for array in large]
        + [whole(array) for array in weights],
        out_specs=[per_item(rounded, pair)] * 4 + [whole(flat)] * 2,
        out_shape=[rounded] * 4 + [flat] * 2,
        scratch_shapes=[
            pltpu.VMEM((frames + HALO, width), F32),
            pltpu.VMEM((8, items, LANE), F32),
            pltpu.VMEM((9, 8, width), F32),
            pltpu.VMEM((height, width), F32),
            pltpu.VMEM((2, 2 * cin, LANE), F32),
        ],
        compiler_params=params(),
        cost_estimate=cost(18 * items * frames * cin * width, items * frames * width * 20),
    )(ends, origin, core, *small, *large, *weights)

    swap = [(0, 1), (1, 0)]
    keep = keep + lax.ppermute(send, "core", swap)
    keep, r_high = lax.optimization_barrier((keep, r_high))
    pieces = exchange(keep.reshape(chips, piece, LANE), ("blk", "side"))

    weights = (w_cat, w_out, weight_res, weight_skip, gain_mid, shift_mid, bias_res, bias_skip)
    count = items // 2

    def outer(offset, size, earlier):
        pair = 2 if size % 2 == 0 and offset % 2 == 0 else 1
        large = (inputs, cot_res, r_high, r_low, u_high, u_low)
        return pl.pallas_call(
            functools.partial(outer_kernel, offset=offset),
            grid=(size // pair,),
            in_specs=[ends_spec, ends_spec, whole(mid_sums)]
            + [per_item(array, pair, offset // pair) for array in large]
            + [whole(array) for array in weights]
            + [pl.BlockSpec(memory_space=pl.ANY)] * len(earlier),
            out_specs=[per_item(wide, pair, offset // pair)] * 3,
            out_shape=[wide] * 3,
            scratch_shapes=[
                pltpu.VMEM((2, items, LANE), F32),
                pltpu.VMEM((3, 2 * cin, LANE), F32),
                pltpu.VMEM((3 * width, 2 * cin), BF16),
                pltpu.VMEM((width, 2 * cin), BF16),
            ],
            input_output_aliases={17: 0, 18: 1, 19: 2} if earlier else {},
            compiler_params=params(),
            cost_estimate=cost(12 * size * frames * cin * width, size * frames * width * 8),
        )(ends, origin, mid_sums, *large, *weights, *earlier)

    residual_out, skip_out, grad_inputs = outer(0, count, ())
    pieces, residual_out = lax.optimization_barrier((pieces, residual_out))
    mine = exchange(jnp.broadcast_to(jnp.sum(pieces, axis=0), pieces.shape), ("blk", "side")).reshape(-1, LANE)
    residual_out, skip_out, grad_inputs = outer(count, items - count, (residual_out, skip_out, grad_inputs))
    mine, residual_out = lax.optimization_barrier((mine, residual_out))
    theirs = lax.ppermute(mine, "core", swap)
    vector, short = sds(1, width), sds(1, cin)
    ends_of = (
        sds(width, cin), vector, vector, vector, vector, sds(3, width), vector, vector, vector, vector,
        sds(cin, width), short, sds(cin, width), short,
    )
    tail = pl.pallas_call(
        last_kernel,
        in_specs=[pl.BlockSpec(memory_space=pltpu.SMEM)] + [pl.BlockSpec(memory_space=pltpu.VMEM)] * 6,
        out_shape=ends_of,
    )(core, mine, theirs, weight_res, weight_skip, gain_mid, shift_mid)
    tail = [
        value if number in (0, 10, 12) else value.T if number == 5 else value.reshape(-1)
        for number, value in enumerate(tail)
    ]
    return (residual_out, skip_out, grad_inputs) + tuple(tail)


def solution(mesh):
    devices = mesh.devices
    split_mesh = jax.sharding.Mesh(devices.reshape(devices.shape[0], -1, 2), ("blk", "side", "core"))
    batch = ("side", "core")
    items = P(batch, None, "blk")
    return jax.shard_map(
        local,
        mesh=split_mesh,
        in_specs=(items,) + (P(),) * 14 + (P(batch), items, items),
        out_specs=(items,) * 3 + (P(),) * 14,
        check_vma=False,
    )
```

```python
import functools

import jax
import jax.numpy as jnp
from jax import lax
from jax.experimental import pallas as pl
from jax.experimental.pallas import tpu as pltpu
from jax.sharding import PartitionSpec as P

STEP = 8
HALO = 2 * STEP
EPS = 1e-05
LANE = 128
ROWS = 64
SECOND_ROWS = 32
PIECE = 256
THIRD_ROWS = 32
F32 = jnp.float32
BF16 = jnp.bfloat16
VMEM_LIMIT = 60 * 1024 * 1024


def split(value):
    high = value.astype(BF16)
    low = (value - high.astype(F32)).astype(BF16)
    return high, low


def product(left, right):
    return jnp.dot(left, right, preferred_element_type=F32)


def product_nt(left, right):
    return lax.dot_general(left, right, (((1,), (1,)), ((), ())), preferred_element_type=F32)


def tile(row):
    return jnp.broadcast_to(row, (8, LANE))


def load(ref, base, rows, lanes):
    return ref[pl.ds(base, rows), lanes].reshape(rows // 8, 8, LANE)


def frame_of(base, rows):
    shape = (rows // 8, 8, LANE)
    return lax.broadcasted_iota(jnp.int32, shape, 0) * 8 + lax.broadcasted_iota(jnp.int32, shape, 1) + base


def half_slopes(row):
    return tile(0.5 - 0.5 * row), tile(0.5 + 0.5 * row)


def act_half(half, c0, c1):
    return half * (c1 + c0 * jnp.tanh(half))


def act_parts(half, c0, c1):
    th = jnp.tanh(half)
    ratio = c1 + c0 * th
    act = half * ratio
    cut = half - act
    return act, ratio + cut * (1.0 + th), cut


def total(value):
    return jnp.sum(jnp.sum(value, axis=0, keepdims=True), axis=1, keepdims=True)


def place(values):
    lane = lax.broadcasted_iota(jnp.int32, (1, LANE), 1)
    row = jnp.zeros((1, LANE), F32)
    for position, value in enumerate(values):
        row = jnp.where(lane == position, value, row)
    return row


def lane_tiles(width):
    return [slice(start, start + LANE) for start in range(0, width, LANE)]


def first_kernel(
    ends_ref, x_ref, res_l_ref, res_r_ref, skip_l_ref, skip_r_ref, w_in_ref, bias_ref, slope_ref,
    w_res_ref, w_skip_ref, gain_ref,
    sums_ref, left_ref, right_ref, w_cat_ref, w_out_ref,
):
    group, cin, frames = x_ref.shape
    width = w_in_ref.shape[0]

    @pl.when(pl.program_id(0) == 0)
    def _():
        high, low = split(0.5 * w_in_ref[...].T)
        w_cat_ref[0:cin] = high
        w_cat_ref[cin : 2 * cin] = high
        w_cat_ref[2 * cin : 3 * cin] = low
        row = lax.broadcasted_iota(jnp.int32, (LANE, width), 0)
        bias = jnp.broadcast_to(0.5 * bias_ref[...], (LANE, width))
        near = bias.astype(BF16).astype(F32)
        w_cat_ref[3 * cin :] = jnp.where(row == 0, near, jnp.where(row == 1, bias - near, 0.0)).astype(BF16)
        for number, ref in enumerate((w_res_ref, w_skip_ref)):
            high, low = split(ref[...] * gain_ref[...])
            start = number * cin
            w_out_ref[start : start + cin] = high
            w_out_ref[2 * cin + start : 3 * cin + start] = high
            w_out_ref[4 * cin + start : 5 * cin + start] = low

    step = min(PIECE, frames)
    for number in range(group):
        item = pl.program_id(0) * group + number
        end = ends_ref[item]
        first = second = jnp.zeros((8, LANE), F32)
        for start in range(0, frames, step):
            xt = x_ref[number, :, start : start + step].astype(BF16).T
            ones = jnp.ones((step, LANE), BF16)
            weights = jnp.concatenate([w_cat_ref[0:cin], w_cat_ref[3 * cin :]], axis=0)
            half = product(jnp.concatenate([xt, ones], axis=1), weights)
            valid = frame_of(start, step) < end
            for lanes in lane_tiles(width):
                c0, c1 = half_slopes(slope_ref[0:1, lanes])
                value = act_half(half[:, lanes].reshape(step // 8, 8, LANE), c0, c1)
                value = jnp.where(valid, value, 0.0)
                first = first + jnp.sum(value, axis=0)
                second = second + jnp.sum(value * value, axis=0)
        row = place((total(first), total(second)))
        for block in range(sums_ref.shape[0]):
            sums_ref[block, pl.ds(item, 1), :] = row
        left_ref[number, :, 0:cin] = x_ref[number, :, 0:LANE].T[0:HALO]
        right_ref[number, :, 0:cin] = x_ref[number, :, frames - LANE : frames].T[LANE - HALO : LANE]
        left_ref[number, 0:STEP, cin : 2 * cin] = res_l_ref[number].T[0:STEP]
        left_ref[number, STEP:HALO, cin : 2 * cin] = skip_l_ref[number].T[0:STEP]
        right_ref[number, 0:STEP, cin : 2 * cin] = res_r_ref[number].T[LANE - STEP : LANE]
        right_ref[number, STEP:HALO, cin : 2 * cin] = skip_r_ref[number].T[LANE - STEP : LANE]


def at(base):
    return base if isinstance(base, int) else pl.multiple_of(base, 8)


def sweep(frames, rows, end, body, init, rest=None):
    if end is None:
        carry = init
        for base in range(0, frames, rows):
            carry = body(base, False, carry)
        return carry
    live = jnp.clip(end, 0, frames)
    full, some = lax.div(live, rows), lax.div(live + (rows - 1), rows)
    carry = lax.fori_loop(0, full, lambda n, c: body(pl.multiple_of(n * rows, rows), False, c), init)
    carry = lax.fori_loop(full, some, lambda n, c: body(pl.multiple_of(n * rows, rows), True, c), carry)
    if rest is not None:

        def clear(n, c):
            rest(pl.multiple_of(n * rows, rows))
            return c

        lax.fori_loop(some, frames // rows, clear, 0)
    return carry


def both_ways(full, run):
    pl.when(full)(lambda: run(True))
    pl.when(jnp.logical_not(full))(lambda: run(False))


def where_valid(valid, value):
    return value if valid is None else jnp.where(valid, value, 0.0)


def counts(ends_ref, origin_ref, items, width):
    row = lax.broadcasted_iota(jnp.int32, (items, 1), 0)
    lengths = jnp.zeros((items, 1), jnp.int32)
    for item in range(items):
        lengths = jnp.where(row == item, ends_ref[item] + origin_ref[0], lengths)
    return lengths.astype(F32) * float(width)


def first_norm(sums_ref, count):
    sums = jnp.sum(sums_ref[...], axis=0)
    mean = 2.0 * sums[:, 0:1] / count
    var = 4.0 * sums[:, 1:2] / count - mean * mean
    return mean, lax.rsqrt(var + EPS)


def second_kernel(
    ends_ref, origin_ref, sums_ref, from_left_ref, from_right_ref, x_all, res_all, skip_all,
    w_cat_ref, w_out_ref, slope_ref, gain_ref, shift_ref, taps_ref, tap_bias_ref, slope_mid_ref,
    half_all, mid_all, back_all, edge_ref, out_ref,
    halo_ref, normal_ref, coef_ref,
):
    items = out_ref.shape[1]
    group, frames, width = half_all.shape
    cin = x_all.shape[1]
    origin = origin_ref[0]

    @pl.when(pl.program_id(0) == 0)
    def _():
        mean, scale = first_norm(sums_ref, counts(ends_ref, origin_ref, items, width))
        coef_ref[0] = jnp.broadcast_to(scale, (items, LANE))
        coef_ref[1] = jnp.broadcast_to(scale * mean, (items, LANE))
        for side, ref in enumerate((from_left_ref, from_right_ref)):
            high, low = split(ref[:, :, 0:cin].reshape(items * HALO, cin))
            ones = jnp.ones((items * HALO, LANE), BF16)
            value = product(jnp.concatenate([high, low, high, ones], axis=1), w_cat_ref[...])
            halo_ref[side] = value.reshape(items, HALO, width)
            cots = jnp.concatenate([ref[:, 0:STEP, cin : 2 * cin], ref[:, STEP:HALO, cin : 2 * cin]], axis=2)
            high, low = split(cots.reshape(items * STEP, 2 * cin))
            value = product(jnp.concatenate([high, low, high], axis=1), w_out_ref[...])
            edge_ref[:, side * STEP : (side + 1) * STEP, :] = value.reshape(items, STEP, width)

    def run(number, item, end, full):
        half_ref, res_ref, skip_ref, mid_ref, back_ref = (
            ref.at[number : number + 1] for ref in (half_all, res_all, skip_all, mid_all, back_all)
        )
        high, low = split(x_all[number].T)
        ones = jnp.ones((frames, LANE), BF16)
        half_ref[0] = product(jnp.concatenate([high, low, high, ones], axis=1), w_cat_ref[...])
        rows = SECOND_ROWS if full and frames % SECOND_ROWS == 0 else ROWS
        d_high, d_low = split(jnp.concatenate([res_ref[0], skip_ref[0]], axis=0))
        high, low = d_high.T, d_low.T
        back_ref[0] = product(jnp.concatenate([high, low, high], axis=1), w_out_ref[...])

        scale, scale_mean = coef_ref[0, pl.ds(item, 1), :], coef_ref[1, pl.ds(item, 1), :]
        window = jnp.clip(end - STEP, 0, frames - HALO)
        window = pl.multiple_of(lax.div(window, 8) * 8, 8)
        tots = [jnp.zeros((8, LANE), F32)] * 10
        for lanes in lane_tiles(width):
            c0, c1 = half_slopes(slope_ref[0:1, lanes])
            gain, shift = gain_ref[0:1, lanes], shift_ref[0:1, lanes]
            factor, offset = 2.0 * gain * scale, shift - gain * scale_mean
            hole = tile(-offset / factor)

            def normed(half, valid):
                value = act_half(half, c0, c1)
                return value if valid is None else jnp.where(valid, value, hole)

            def store(base, count, value):
                normal_ref[pl.ds(base, count), lanes] = value.reshape(count, LANE)

            frame = frame_of(-HALO, HALO)
            store(0, HALO, normed(halo_ref[0, item, :, lanes].reshape(2, 8, LANE), (frame < end) & (frame >= -origin)))
            frame = frame_of(frames, HALO)
            store(HALO + frames, HALO, normed(halo_ref[1, item, :, lanes].reshape(2, 8, LANE), frame < end))

            def fill(base, masked, carry):
                valid = frame_of(base, rows) < end if masked else None
                store(at(base + HALO), rows, normed(load(half_ref.at[0], base, rows, lanes), valid))
                return carry

            def clear(base):
                normal_ref[pl.ds(at(base + HALO), rows), lanes] = jnp.broadcast_to(-offset / factor, (rows, LANE))

            sweep(frames, rows, None if full else end, fill, 0, clear)

            rows_of = [0.5 * taps_ref[tap : tap + 1, lanes] for tap in range(3)]
            taps = [tile(factor * row) for row in rows_of]
            tap_bias = tile(0.5 * tap_bias_ref[0:1, lanes] + offset * (rows_of[0] + rows_of[1] + rows_of[2]))
            m0, m1 = half_slopes(slope_mid_ref[0:1, lanes])

            def conv(base, count):
                value = taps[0] * load(normal_ref, base, count, lanes)
                value = value + taps[1] * load(normal_ref, at(base + STEP), count, lanes)
                value = value + taps[2] * load(normal_ref, at(base + HALO), count, lanes) + tap_bias
                mid_ref[0, pl.ds(base, count), lanes] = value.reshape(count, LANE)
                return value

            conv(0, STEP)
            conv(frames + STEP, STEP)

            def gather(base, masked, carry):
                valid = frame_of(base, rows) < end if masked else None
                mid = conv(at(base + STEP), rows)
                act, grad, _ = act_parts(mid, m0, m1)
                back = load(back_ref.at[0], base, rows, lanes)
                act, grad, back = where_valid(valid, act), where_valid(valid, grad), where_valid(valid, back)
                ex, ez = grad * back, grad * act
                terms = (act, act * act, back, back * act, ex, grad, ez, ex * mid, grad * mid, ez * mid)
                return tuple(old + jnp.sum(new, axis=0) for old, new in zip(carry, terms))

            sums = sweep(frames, rows, None if full else end, gather, (jnp.zeros((8, LANE), F32),) * 10)

            def edge_sums(base, mask):
                mid = load(mid_ref.at[0], at(base + STEP), HALO, lanes)
                act, grad, _ = act_parts(mid, m0, m1)
                back = load(back_ref.at[0], base, HALO, lanes)
                return [jnp.sum(jnp.where(mask, term, 0.0), axis=0) for term in (grad * back, grad, grad * act)]

            frame = frame_of(0, HALO)
            low_sums = edge_sums(0, (frame < end) & (frame + origin < STEP))
            frame = frame_of(window, HALO)
            high_sums = edge_sums(window, (frame < end) & (frame >= end - STEP))
            w0, w1, w2 = (tile(taps_ref[tap : tap + 1, lanes]) for tap in range(3))
            for term in range(4):
                tots[term] = tots[term] + sums[term]
            for term in range(3):
                plain = sums[4 + term]
                edged = (w0 + w1 + w2) * plain - w0 * low_sums[term] - w2 * high_sums[term]
                tots[4 + term] = tots[4 + term] + gain * edged
                tots[7 + term] = (
                    tots[7 + term] + 2.0 * sums[7 + term] - tap_bias_ref[0:1, lanes] * plain - shift * edged
                )

        row = place([total(value) for value in tots])
        for block in range(out_ref.shape[0]):
            out_ref[block, pl.ds(item, 1), :] = row

    for number in range(group):
        item = pl.program_id(0) * group + number
        end = ends_ref[item]
        both_ways(end >= frames, functools.partial(run, number, item, end))


GRAD_ROWS = 16


def second_norm(mids_ref, count):
    mids = jnp.sum(mids_ref[...], axis=0)
    m = [mids[:, term : term + 1] for term in range(10)]
    mean = 2.0 * m[0] / count
    return m, mean, lax.rsqrt(4.0 * m[1] / count - mean * mean + EPS)


def flatten(flat_ref, grads_ref, half):
    height, width = grads_ref.shape
    tiles = lane_tiles(width)
    count = len(tiles) // 2
    for number, lanes in enumerate(tiles[half * count : (half + 1) * count]):
        flat_ref[number * height : (number + 1) * height] = grads_ref[:, lanes]
    used = height * count
    if used < flat_ref.shape[0]:
        flat_ref[used:] = jnp.zeros((flat_ref.shape[0] - used, LANE), F32)


def third_kernel(
    ends_ref, origin_ref, core_ref, sums_ref, mids_ref, x_all, res_all, skip_all, half_all, mid_all, back_all, edge_all,
    slope_ref, gain_ref, shift_ref, taps_ref, slope_mid_ref,
    r_high_all, r_low_all, u_high_all, u_low_all, keep_ref, send_ref,
    grad_ref, coef_ref, vector_ref, grads_ref, cot_ref,
):
    items = coef_ref.shape[1]
    group, cin, frames = x_all.shape
    width = half_all.shape[2]
    origin = origin_ref[0]

    @pl.when(pl.program_id(0) == 0)
    def _():
        count = counts(ends_ref, origin_ref, items, width)
        mean1, scale1 = first_norm(sums_ref, count)
        m, mean2, scale2 = second_norm(mids_ref, count)
        beta = scale2 * scale2 * (2.0 * m[3] - mean2 * m[2]) / count
        alpha = m[2] / count - mean2 * beta
        mean_a = scale2 * (m[4] - alpha * m[5] - 2.0 * beta * m[6]) / count
        mean_b = scale2 * (m[7] - alpha * m[8] - 2.0 * beta * m[9]) / count
        values = (
            scale1, scale1 * mean1, scale1 * (mean_a - mean1 * scale1 * mean_b), 2.0 * scale1 * scale1 * mean_b,
            scale2, alpha, 2.0 * beta, scale2 * mean2,
        )
        for number, value in enumerate(values):
            coef_ref[number] = jnp.broadcast_to(value, (items, LANE))
        vector_ref[...] = jnp.zeros(vector_ref.shape, F32)
        grads_ref[...] = jnp.zeros(grads_ref.shape, F32)
        cot_ref[...] = jnp.zeros(cot_ref.shape, F32)

    def run(number, item, end, full):
        x_ref, res_ref, skip_ref, half_ref, mid_ref, back_ref, edge_ref = (
            ref.at[number : number + 1] for ref in (x_all, res_all, skip_all, half_all, mid_all, back_all, edge_all)
        )
        r_high_ref, r_low_ref, u_high_ref, u_low_ref = (
            ref.at[number : number + 1] for ref in (r_high_all, r_low_all, u_high_all, u_low_all)
        )
        rows = THIRD_ROWS if full else ROWS
        coefs = [tile(coef_ref[number, pl.ds(item, 1), :]) for number in range(8)]
        scale1, scale_mean1, dp_a, dp_b, scale2, dr_a, dr_b, z_a = coefs
        both = jnp.concatenate([res_ref[0], skip_ref[0]], axis=0)
        d_high, d_low = split(both)
        lane = lax.broadcasted_iota(jnp.int32, (1, LANE), 1)
        cots = jnp.zeros((2 * cin, LANE), F32)
        for lanes in lane_tiles(frames):
            piece = both[:, lanes]
            cots = cots + (piece if full else jnp.where(lane + lanes.start < end, piece, 0.0))
        cot_ref[0] += cots
        cot_ref[1] += z_a[0:1] * cots

        for lanes in lane_tiles(width):
            m0, m1 = half_slopes(slope_mid_ref[0:1, lanes])

            def middle(base, count, valid, back):
                act, slope, cut = act_parts(load(mid_ref.at[0], base, count, lanes), m0, m1)
                grad = (back - dr_a) - dr_b * act
                grad = where_valid(valid, grad)
                grad_ref[pl.ds(base, count), lanes] = (grad * slope).reshape(count, LANE)
                return act, grad * cut

            frame = frame_of(-STEP, STEP)
            middle(0, STEP, (frame < end) & (frame >= -origin), edge_ref[0:1, 0:STEP, lanes])
            middle(frames + STEP, STEP, frame_of(frames, STEP) < end, edge_ref[0:1, STEP:HALO, lanes])

            def inner(base, masked, carry):
                valid = frame_of(base, rows) < end if masked else None
                act, term = middle(at(base + STEP), rows, valid, load(back_ref.at[0], base, rows, lanes))
                high, low = split(where_valid(valid, act).reshape(rows, LANE))
                r_high_ref[0, pl.ds(base, rows), lanes] = high
                r_low_ref[0, pl.ds(base, rows), lanes] = low
                return carry + jnp.sum(term, axis=0)

            def inner_clear(base):
                grad_ref[pl.ds(at(base + STEP), rows), lanes] = jnp.zeros((rows, LANE), F32)
                r_high_ref[0, pl.ds(base, rows), lanes] = jnp.zeros((rows, LANE), BF16)
                r_low_ref[0, pl.ds(base, rows), lanes] = jnp.zeros((rows, LANE), BF16)

            vector_ref[8, :, lanes] += scale2 / m0 * sweep(
                frames, rows, None if full else end, inner, jnp.zeros((8, LANE), F32), inner_clear
            )

            c0, c1 = half_slopes(slope_ref[0:1, lanes])
            gain, shift = gain_ref[0:1, lanes], shift_ref[0:1, lanes]
            taps = [tile(taps_ref[tap : tap + 1, lanes]) for tap in range(3)]
            outer = gain * scale1
            scaled = [tap * (outer * scale2) for tap in taps]

            def body(base, masked, carry):
                valid = frame_of(base, rows) < end if masked else None
                ahead = load(grad_ref, at(base + HALO), rows, lanes)
                here = load(grad_ref, at(base + STEP), rows, lanes)
                behind = where_valid(valid, load(grad_ref, base, rows, lanes))
                act, slope, cut = act_parts(load(half_ref.at[0], base, rows, lanes), c0, c1)
                dp = scaled[0] * ahead + scaled[1] * here + scaled[2] * behind
                dp = where_valid(valid, (dp - dp_a) - dp_b * act)
                du = dp * slope
                high, low = split(du.reshape(rows, LANE))
                u_high_ref[0, pl.ds(base, rows), lanes] = high
                u_low_ref[0, pl.ds(base, rows), lanes] = low
                terms = (dp * cut, here, ahead * act, here * act, behind * act)
                return tuple(old + jnp.sum(new, axis=0) for old, new in zip(carry, terms))

            def clear(base):
                u_high_ref[0, pl.ds(base, rows), lanes] = jnp.zeros((rows, LANE), BF16)
                u_low_ref[0, pl.ds(base, rows), lanes] = jnp.zeros((rows, LANE), BF16)

            sums = sweep(frames, rows, None if full else end, body, (jnp.zeros((8, LANE), F32),) * 5, clear)
            window = pl.multiple_of(lax.div(jnp.clip(end, 0, frames - HALO), 8) * 8, 8)
            row = frame_of(window, HALO)
            inside = jnp.where((row >= end) & (row < end + STEP), load(grad_ref, window, HALO, lanes), 0.0)
            plains = (
                sums[1] - grad_ref[STEP:HALO, lanes] + grad_ref[frames + STEP : frames + HALO, lanes],
                sums[1],
                sums[1] - grad_ref[frames : frames + STEP, lanes] + grad_ref[0:STEP, lanes] - jnp.sum(inside, axis=0),
            )
            factor, offset = 2.0 * outer, shift - gain * scale_mean1
            vector_ref[1, :, lanes] += sums[0] / c0
            gain_sum = shift_sum = jnp.zeros((8, LANE), F32)
            for tap in range(3):
                plain, times = scale2 * plains[tap], scale2 * sums[2 + tap]
                vector_ref[4 + tap, :, lanes] += factor * times + offset * plain
                gain_sum = gain_sum + taps[tap] * (2.0 * scale1 * times - scale_mean1 * plain)
                shift_sum = shift_sum + taps[tap] * plain
            vector_ref[2, :, lanes] += gain_sum
            vector_ref[3, :, lanes] += shift_sum
            vector_ref[7, :, lanes] += scale2 * sums[1]

        r_high, r_low = r_high_ref[0], r_low_ref[0]
        mixed = product(
            jnp.concatenate([d_high, d_low, d_high], axis=1), jnp.concatenate([r_high, r_high, r_low], axis=0)
        )
        z_0 = 2.0 * scale2[0:1]
        for lanes in lane_tiles(width):
            grads_ref[0 : 2 * cin, lanes] += z_0 * mixed[:, lanes]
        u_high, u_low = u_high_ref[0], u_low_ref[0]
        x_high, x_low = split(x_ref[0])
        rows_of = jnp.concatenate([x_high, x_low, x_high], axis=1)
        ones = jnp.ones((GRAD_ROWS, frames), BF16)
        ones = jnp.concatenate([ones, jnp.zeros((GRAD_ROWS, frames), BF16), ones], axis=1)
        grads_ref[2 * cin : 3 * cin + GRAD_ROWS] += product(
            jnp.concatenate([rows_of, ones], axis=0), jnp.concatenate([u_high, u_high, u_low], axis=0)
        )

    for number in range(group):
        item = pl.program_id(0) * group + number
        end = ends_ref[item]
        both_ways(end >= frames, functools.partial(run, number, item, end))

    @pl.when(pl.program_id(0) == items // group - 1)
    def _():
        base = 3 * cin
        grads_ref[0 : 2 * cin] = grads_ref[0 : 2 * cin] - jnp.sum(cot_ref[1], axis=1, keepdims=True)
        for row in range(1, 9):
            grads_ref[base + row : base + row + 1] = jnp.sum(vector_ref[row], axis=0, keepdims=True)
        column = jnp.broadcast_to(jnp.sum(cot_ref[0], axis=1, keepdims=True), (2 * cin, LANE)).T[0:1]
        grads_ref[base + 9 : base + 10] = jnp.zeros((1, width), F32)
        for number in range(2 * cin // LANE):
            grads_ref[base + 9 + number : base + 10 + number, 0:LANE] = column[:, number * LANE : (number + 1) * LANE]
            grads_ref[base + 9 + number : base + 10 + number, width // 2 : width // 2 + LANE] = column[
                :, number * LANE : (number + 1) * LANE
            ]
        for core in range(2):

            @pl.when(core_ref[0] == core)
            def _():
                flatten(keep_ref, grads_ref, core)
                flatten(send_ref, grads_ref, 1 - core)


def outer_kernel(
    ends_ref, origin_ref, mids_ref, x_ref, res_ref, r_high_ref, r_low_ref, u_high_ref, u_low_ref,
    w_cat_ref, w_out_ref, w_res_ref, w_skip_ref, gain_ref, shift_ref, bias_res_ref, bias_skip_ref, *rest_refs, offset,
):
    res_out_ref, skip_out_ref, x_grad_ref, coef_ref, column_ref, out_turned_ref, in_turned_ref = rest_refs[-7:]
    items = coef_ref.shape[1]
    group, cin, frames = x_ref.shape
    width = w_cat_ref.shape[1]

    @pl.when(pl.program_id(0) == 0)
    def _():
        _, mean, scale = second_norm(mids_ref, counts(ends_ref, origin_ref, items, width))
        coef_ref[0] = jnp.broadcast_to(2.0 * scale, (items, LANE))
        coef_ref[1] = jnp.broadcast_to(scale * mean, (items, LANE))
        high, low = w_out_ref[0 : 2 * cin].T, w_out_ref[4 * cin : 6 * cin].T
        out_turned_ref[0:width] = high
        out_turned_ref[width : 2 * width] = high
        out_turned_ref[2 * width : 3 * width] = low
        in_turned_ref[:, 0:cin] = w_cat_ref[0:cin].T
        in_turned_ref[:, cin : 2 * cin] = w_cat_ref[2 * cin : 3 * cin].T
        for number, (w_ref, b_ref) in enumerate(((w_res_ref, bias_res_ref), (w_skip_ref, bias_skip_ref))):
            rows = slice(number * cin, (number + 1) * cin)
            column_ref[0, rows] = jnp.broadcast_to(b_ref[...], (LANE, cin)).T
            for spot, vector_of in ((1, shift_ref), (2, gain_ref)):
                value = jnp.sum(w_ref[...] * vector_of[...], axis=1, keepdims=True)
                column_ref[spot, rows] = jnp.broadcast_to(value, (cin, LANE))

    lane = lax.broadcasted_iota(jnp.int32, (1, LANE), 1)
    for number in range(group):
        item = offset + pl.program_id(0) * group + number
        end = ends_ref[item]
        z_0, z_a = coef_ref[0, pl.ds(item, 1), :], coef_ref[1, pl.ds(item, 1), :]
        r_high, r_low = r_high_ref[number], r_low_ref[number]
        out = product(jnp.concatenate([r_high, r_low, r_high], axis=1), out_turned_ref[...]).T
        pair = product(u_high_ref[number], in_turned_ref[...])
        x_grad = (pair[:, 0:cin] + pair[:, cin : 2 * cin] + product(u_low_ref[number], in_turned_ref[:, 0:cin])).T
        inside = column_ref[1] - z_a * column_ref[2]
        for lanes in lane_tiles(frames):
            valid = lane + lanes.start < end
            wide = column_ref[0] + jnp.where(valid, inside, 0.0) + z_0 * out[:, lanes]
            res_out_ref[number, :, lanes] = wide[0:cin] + x_ref[number, :, lanes]
            skip_out_ref[number, :, lanes] = wide[cin : 2 * cin]
            x_grad_ref[number, :, lanes] = jnp.where(valid, res_ref[number, :, lanes], 0.0) + 2.0 * x_grad[:, lanes]


def last_kernel(
    core_ref, mine_ref, theirs_ref, w_res_ref, w_skip_ref, gain_ref, shift_ref,
    w_in_out, bias_in_out, slope_in_out, gain_in_out, shift_in_out, taps_out, tap_bias_out, slope_mid_out,
    gain_mid_out, shift_mid_out, w_res_out, bias_res_out, w_skip_out, bias_skip_out,
):
    cin, width = w_res_ref.shape
    height = 3 * cin + GRAD_ROWS
    base = 3 * cin
    vectors = ((0, bias_in_out), (1, slope_in_out), (2, gain_in_out), (3, shift_in_out), (7, tap_bias_out), (8, slope_mid_out))
    groups = ((w_res_ref, w_res_out), (w_skip_ref, w_skip_out))
    columns = []
    for number, bias_out in enumerate((bias_res_out, bias_skip_out)):
        row = mine_ref[base + 9 + number : base + 10 + number]
        bias_out[...] = row
        columns.append(jnp.broadcast_to(row, (cin, cin)).T[:, 0:1])
    tiles = lane_tiles(width)
    count = len(tiles) // 2

    def place_half(ref, half):
        for number, lanes in enumerate(tiles[half * count : (half + 1) * count]):
            grads = ref.at[number * height : (number + 1) * height]
            w_in_out[lanes] = grads[2 * cin : 3 * cin].T
            for row, out in vectors:
                out[:, lanes] = grads[base + row : base + row + 1]
            taps_out[:, lanes] = grads[base + 4 : base + 7]
            gain_sum = shift_sum = jnp.zeros((1, LANE), F32)
            for group, (w_ref, w_out) in enumerate(groups):
                products = grads[group * cin : (group + 1) * cin]
                column = columns[group]
                w_out[:, lanes] = gain_ref[:, lanes] * products + shift_ref[:, lanes] * column
                gain_sum = gain_sum + jnp.sum(w_ref[:, lanes] * products, axis=0, keepdims=True)
                shift_sum = shift_sum + jnp.sum(w_ref[:, lanes] * column, axis=0, keepdims=True)
            gain_mid_out[:, lanes] = gain_sum
            shift_mid_out[:, lanes] = shift_sum

    for core in range(2):

        @pl.when(core_ref[0] == core)
        def _():
            place_half(mine_ref, core)
            place_half(theirs_ref, 1 - core)


def whole(array, space=pltpu.VMEM):
    if space is pltpu.SMEM:
        return pl.BlockSpec(memory_space=pltpu.SMEM)
    return pl.BlockSpec(array.shape, lambda item: (0,) * len(array.shape))


def per_item(array, group=1, offset=0):
    return pl.BlockSpec((group,) + array.shape[1:], lambda item: (item + offset, 0, 0))


def edge_block(array, group, position):
    return pl.BlockSpec((group, array.shape[1], LANE), lambda item: (item, 0, position))


def sds(*shape, dtype=F32):
    return jax.ShapeDtypeStruct(shape, dtype)


def cost(flops, size):
    return pl.CostEstimate(flops=flops, bytes_accessed=size, transcendentals=0)


def params():
    return pltpu.CompilerParams(dimension_semantics=("arbitrary",), vmem_limit_bytes=VMEM_LIMIT)


def exchange(pieces, axes):
    return lax.all_to_all(pieces, axes, 0, 0)


def local(
    inputs, weight_in, bias_in, slope_in, gain_in, shift_in, depthwise_weight, depthwise_bias, slope_mid, gain_mid,
    shift_mid, weight_res, bias_res, weight_skip, bias_skip, lengths, cot_res, cot_skip,
):
    items, cin, frames = inputs.shape
    width = weight_in.shape[0]
    blocks = lax.axis_size("blk")
    origin = (lax.axis_index("blk") * frames).astype(jnp.int32).reshape(1)
    core = lax.axis_index("core").astype(jnp.int32).reshape(1)
    ends = lengths - origin[0]
    bias_in, slope_in, gain_in, shift_in, tap_bias, slope_mid, gain_mid, shift_mid, bias_res, bias_skip = (
        vector.reshape(1, -1)
        for vector in (
            bias_in, slope_in, gain_in, shift_in, depthwise_bias, slope_mid, gain_mid, shift_mid, bias_res, bias_skip
        )
    )
    taps = depthwise_weight.T
    ends_spec = whole(ends, pltpu.SMEM)

    half = sds(items, frames, width)
    halo = sds(items, HALO, 2 * cin)
    last = frames // LANE - 1
    sums = sds(blocks, items, LANE)
    w_cat, w_out = sds(3 * cin + LANE, width, dtype=BF16), sds(6 * cin, width, dtype=BF16)
    weights = (weight_in, bias_in, slope_in, weight_res, weight_skip, gain_mid)
    pair = 2 if items % 2 == 0 else 1
    quad = 4 if items % 4 == 0 else 1
    first_sums, to_left, to_right, w_cat, w_out = pl.pallas_call(
        first_kernel,
        grid=(items // quad,),
        in_specs=[ends_spec, per_item(inputs, quad)]
        + [edge_block(array, quad, spot) for array in (cot_res, cot_skip) for spot in (0, last)]
        + [whole(array) for array in weights],
        out_specs=[whole(sums), per_item(halo, quad), per_item(halo, quad), whole(w_cat), whole(w_out)],
        out_shape=[sums, halo, halo, w_cat, w_out],
        compiler_params=params(),
    )(ends, inputs, cot_res, cot_res, cot_skip, cot_skip, *weights)

    forward = [(block, block + 1) for block in range(blocks - 1)]
    backward = [(target, source) for source, target in forward]
    first_sums = exchange(first_sums, "blk")
    from_left = lax.ppermute(to_right, "blk", forward)
    from_right = lax.ppermute(to_left, "blk", backward)

    mid, edge = sds(items, frames + HALO, width), sds(items, HALO, width)
    small = (first_sums, from_left, from_right)
    weights = (w_cat, w_out, slope_in, gain_in, shift_in, taps, tap_bias, slope_mid)
    rounded = sds(items, frames, width, dtype=BF16)
    half, mid, back, edge, mid_sums = pl.pallas_call(
        second_kernel,
        grid=(items // pair,),
        in_specs=[ends_spec, ends_spec]
        + [whole(array) for array in small]
        + [per_item(array, pair) for array in (inputs, cot_res, cot_skip)]
        + [whole(array) for array in weights],
        out_specs=[per_item(half, pair), per_item(mid, pair), per_item(half, pair), whole(edge), whole(sums)],
        out_shape=[half, mid, half, edge, sums],
        scratch_shapes=[
            pltpu.VMEM((2, items, HALO, width), F32),
            pltpu.VMEM((frames + 2 * HALO, width), F32),
            pltpu.VMEM((2, items, LANE), F32),
        ],
        compiler_params=params(),
        cost_estimate=cost(20 * items * frames * cin * width, items * frames * width * 14),
    )(ends, origin, *small, inputs, cot_res, cot_skip, *weights)
    mid_sums = exchange(mid_sums, "blk")

    small = (first_sums, mid_sums)
    large = (inputs, cot_res, cot_skip, half, mid, back, edge)
    weights = (slope_in, gain_in, shift_in, taps, slope_mid)
    wide = sds(*inputs.shape)
    height = 3 * cin + GRAD_ROWS
    chips = blocks * lax.axis_size("side")
    piece = -(-height * (width // LANE) // (2 * chips * 8)) * 8
    flat = sds(chips * piece, LANE)
    r_high, r_low, u_high, u_low, keep, send = pl.pallas_call(
        third_kernel,
        grid=(items // pair,),
        in_specs=[ends_spec] * 3
        + [whole(array) for array in small]
        + [per_item(array, pair) for array in large]
        + [whole(array) for array in weights],
        out_specs=[per_item(rounded, pair)] * 4 + [whole(flat)] * 2,
        out_shape=[rounded] * 4 + [flat] * 2,
        scratch_shapes=[
            pltpu.VMEM((frames + HALO, width), F32),
            pltpu.VMEM((8, items, LANE), F32),
            pltpu.VMEM((9, 8, width), F32),
            pltpu.VMEM((height, width), F32),
            pltpu.VMEM((2, 2 * cin, LANE), F32),
        ],
        compiler_params=params(),
        cost_estimate=cost(18 * items * frames * cin * width, items * frames * width * 20),
    )(ends, origin, core, *small, *large, *weights)

    swap = [(0, 1), (1, 0)]
    keep = keep + lax.ppermute(send, "core", swap)
    keep, r_high = lax.optimization_barrier((keep, r_high))
    pieces = exchange(keep.reshape(chips, piece, LANE), ("blk", "side"))

    weights = (w_cat, w_out, weight_res, weight_skip, gain_mid, shift_mid, bias_res, bias_skip)
    count = items // 2

    def outer(offset, size, earlier):
        pair = 2 if size % 2 == 0 and offset % 2 == 0 else 1
        large = (inputs, cot_res, r_high, r_low, u_high, u_low)
        return pl.pallas_call(
            functools.partial(outer_kernel, offset=offset),
            grid=(size // pair,),
            in_specs=[ends_spec, ends_spec, whole(mid_sums)]
            + [per_item(array, pair, offset // pair) for array in large]
            + [whole(array) for array in weights]
            + [pl.BlockSpec(memory_space=pl.ANY)] * len(earlier),
            out_specs=[per_item(wide, pair, offset // pair)] * 3,
            out_shape=[wide] * 3,
            scratch_shapes=[
                pltpu.VMEM((2, items, LANE), F32),
                pltpu.VMEM((3, 2 * cin, LANE), F32),
                pltpu.VMEM((3 * width, 2 * cin), BF16),
                pltpu.VMEM((width, 2 * cin), BF16),
            ],
            input_output_aliases={17: 0, 18: 1, 19: 2} if earlier else {},
            compiler_params=params(),
            cost_estimate=cost(12 * size * frames * cin * width, size * frames * width * 8),
        )(ends, origin, mid_sums, *large, *weights, *earlier)

    residual_out, skip_out, grad_inputs = outer(0, count, ())
    pieces, residual_out = lax.optimization_barrier((pieces, residual_out))
    mine = exchange(jnp.broadcast_to(jnp.sum(pieces, axis=0), pieces.shape), ("blk", "side")).reshape(-1, LANE)
    residual_out, skip_out, grad_inputs = outer(count, items - count, (residual_out, skip_out, grad_inputs))
    mine, residual_out = lax.optimization_barrier((mine, residual_out))
    theirs = lax.ppermute(mine, "core", swap)
    vector, short = sds(1, width), sds(1, cin)
    ends_of = (
        sds(width, cin), vector, vector, vector, vector, sds(3, width), vector, vector, vector, vector,
        sds(cin, width), short, sds(cin, width), short,
    )
    tail = pl.pallas_call(
        last_kernel,
        in_specs=[pl.BlockSpec(memory_space=pltpu.SMEM)] + [pl.BlockSpec(memory_space=pltpu.VMEM)] * 6,
        out_shape=ends_of,
    )(core, mine, theirs, weight_res, weight_skip, gain_mid, shift_mid)
    tail = [
        value if number in (0, 10, 12) else value.T if number == 5 else value.reshape(-1)
        for number, value in enumerate(tail)
    ]
    return (residual_out, skip_out, grad_inputs) + tuple(tail)


def solution(mesh):
    devices = mesh.devices
    split_mesh = jax.sharding.Mesh(devices.reshape(devices.shape[0], -1, 2), ("blk", "side", "core"))
    batch = ("side", "core")
    items = P(batch, None, "blk")
    return jax.shard_map(
        local,
        mesh=split_mesh,
        in_specs=(items,) + (P(),) * 14 + (P(batch), items, items),
        out_specs=(items,) * 3 + (P(),) * 14,
        check_vma=False,
    )
```

```python
import functools

import jax
import jax.numpy as jnp
from jax import lax
from jax.experimental import pallas as pl
from jax.experimental.pallas import tpu as pltpu
from jax.sharding import PartitionSpec as P

STEP = 8
HALO = 2 * STEP
EPS = 1e-05
LANE = 128
ROWS = 64
SECOND_ROWS = 128
PIECE = 256
THIRD_ROWS = 32
F32 = jnp.float32
BF16 = jnp.bfloat16
VMEM_LIMIT = 60 * 1024 * 1024


def split(value):
    high = value.astype(BF16)
    low = (value - high.astype(F32)).astype(BF16)
    return high, low


def product(left, right):
    return jnp.dot(left, right, preferred_element_type=F32)


def product_nt(left, right):
    return lax.dot_general(left, right, (((1,), (1,)), ((), ())), preferred_element_type=F32)


def tile(row):
    return jnp.broadcast_to(row, (8, LANE))


def load(ref, base, rows, lanes):
    return ref[pl.ds(base, rows), lanes].reshape(rows // 8, 8, LANE)


def frame_of(base, rows):
    shape = (rows // 8, 8, LANE)
    return lax.broadcasted_iota(jnp.int32, shape, 0) * 8 + lax.broadcasted_iota(jnp.int32, shape, 1) + base


def half_slopes(row):
    return tile(0.5 - 0.5 * row), tile(0.5 + 0.5 * row)


def act_half(half, c0, c1):
    return half * (c1 + c0 * jnp.tanh(half))


def act_parts(half, c0, c1):
    th = jnp.tanh(half)
    ratio = c1 + c0 * th
    act = half * ratio
    cut = half - act
    return act, ratio + cut * (1.0 + th), cut


def total(value):
    return jnp.sum(jnp.sum(value, axis=0, keepdims=True), axis=1, keepdims=True)


def place(values):
    lane = lax.broadcasted_iota(jnp.int32, (1, LANE), 1)
    row = jnp.zeros((1, LANE), F32)
    for position, value in enumerate(values):
        row = jnp.where(lane == position, value, row)
    return row


def lane_tiles(width):
    return [slice(start, start + LANE) for start in range(0, width, LANE)]


def first_kernel(
    lengths_ref, origin_ref, x_ref, res_l_ref, res_r_ref, skip_l_ref, skip_r_ref, w_in_ref, bias_ref, slope_ref,
    w_res_ref, w_skip_ref, gain_ref,
    sums_ref, left_ref, right_ref, w_cat_ref, w_out_ref,
):
    group, cin, frames = x_ref.shape
    width = w_in_ref.shape[0]

    @pl.when(pl.program_id(0) == 0)
    def _():
        high, low = split(0.5 * w_in_ref[...].T)
        w_cat_ref[0:cin] = high
        w_cat_ref[cin : 2 * cin] = high
        w_cat_ref[2 * cin : 3 * cin] = low
        row = lax.broadcasted_iota(jnp.int32, (LANE, width), 0)
        bias = jnp.broadcast_to(0.5 * bias_ref[...], (LANE, width))
        near = bias.astype(BF16).astype(F32)
        w_cat_ref[3 * cin :] = jnp.where(row == 0, near, jnp.where(row == 1, bias - near, 0.0)).astype(BF16)
        for number, ref in enumerate((w_res_ref, w_skip_ref)):
            high, low = split(ref[...] * gain_ref[...])
            start = number * cin
            w_out_ref[start : start + cin] = high
            w_out_ref[2 * cin + start : 3 * cin + start] = high
            w_out_ref[4 * cin + start : 5 * cin + start] = low

    step = min(PIECE, frames)
    for number in range(group):
        item = pl.program_id(0) * group + number
        end = lengths_ref[item] - origin_ref[0]
        first = second = jnp.zeros((8, LANE), F32)
        for start in range(0, frames, step):
            xt = x_ref[number, :, start : start + step].astype(BF16).T
            ones = jnp.ones((step, LANE), BF16)
            weights = jnp.concatenate([w_cat_ref[0:cin], w_cat_ref[3 * cin :]], axis=0)
            half = product(jnp.concatenate([xt, ones], axis=1), weights)
            valid = frame_of(start, step) < end
            for lanes in lane_tiles(width):
                c0, c1 = half_slopes(slope_ref[0:1, lanes])
                value = act_half(half[:, lanes].reshape(step // 8, 8, LANE), c0, c1)
                value = jnp.where(valid, value, 0.0)
                first = first + jnp.sum(value, axis=0)
                second = second + jnp.sum(value * value, axis=0)
        row = place((total(first), total(second)))
        for block in range(sums_ref.shape[0]):
            sums_ref[block, pl.ds(item, 1), :] = row
        left_ref[number, :, 0:cin] = x_ref[number, :, 0:LANE].T[0:HALO]
        right_ref[number, :, 0:cin] = x_ref[number, :, frames - LANE : frames].T[LANE - HALO : LANE]
        left_ref[number, 0:STEP, cin : 2 * cin] = res_l_ref[number].T[0:STEP]
        left_ref[number, STEP:HALO, cin : 2 * cin] = skip_l_ref[number].T[0:STEP]
        right_ref[number, 0:STEP, cin : 2 * cin] = res_r_ref[number].T[LANE - STEP : LANE]
        right_ref[number, STEP:HALO, cin : 2 * cin] = skip_r_ref[number].T[LANE - STEP : LANE]


def at(base):
    return base if isinstance(base, int) else pl.multiple_of(base, 8)


def sweep(frames, rows, end, body, init, rest=None):
    if end is None:
        carry = init
        for base in range(0, frames, rows):
            carry = body(base, False, carry)
        return carry
    live = jnp.clip(end, 0, frames)
    full, some = lax.div(live, rows), lax.div(live + (rows - 1), rows)
    carry = lax.fori_loop(0, full, lambda n, c: body(pl.multiple_of(n * rows, rows), False, c), init)
    carry = lax.fori_loop(full, some, lambda n, c: body(pl.multiple_of(n * rows, rows), True, c), carry)
    if rest is not None:

        def clear(n, c):
            rest(pl.multiple_of(n * rows, rows))
            return c

        lax.fori_loop(some, frames // rows, clear, 0)
    return carry


def both_ways(full, run):
    pl.when(full)(lambda: run(True))
    pl.when(jnp.logical_not(full))(lambda: run(False))


def where_valid(valid, value):
    return value if valid is None else jnp.where(valid, value, 0.0)


def counts(lengths_ref, items, width):
    row = lax.broadcasted_iota(jnp.int32, (items, 1), 0)
    lengths = jnp.zeros((items, 1), jnp.int32)
    for item in range(items):
        lengths = jnp.where(row == item, lengths_ref[item], lengths)
    return lengths.astype(F32) * float(width)


def first_norm(sums_ref, count):
    sums = jnp.sum(sums_ref[...], axis=0)
    mean = 2.0 * sums[:, 0:1] / count
    var = 4.0 * sums[:, 1:2] / count - mean * mean
    return mean, lax.rsqrt(var + EPS)


def second_kernel(
    lengths_ref, origin_ref, sums_ref, from_left_ref, from_right_ref, x_all, res_all, skip_all,
    w_cat_ref, w_out_ref, slope_ref, gain_ref, shift_ref, taps_ref, tap_bias_ref, slope_mid_ref,
    half_all, mid_all, back_all, edge_ref, out_ref, d_high_ref, d_low_ref, x_high_ref, x_low_ref, cot_ref,
    halo_ref, normal_ref, coef_ref,
):
    items = out_ref.shape[1]
    group, frames, width = half_all.shape
    cin = x_all.shape[1]
    origin = origin_ref[0]

    @pl.when(pl.program_id(0) == 0)
    def _():
        mean, scale = first_norm(sums_ref, counts(lengths_ref, items, width))
        coef_ref[0] = jnp.broadcast_to(scale, (items, LANE))
        coef_ref[1] = jnp.broadcast_to(scale * mean, (items, LANE))
        for side, ref in enumerate((from_left_ref, from_right_ref)):
            high, low = split(ref[:, :, 0:cin].reshape(items * HALO, cin))
            ones = jnp.ones((items * HALO, LANE), BF16)
            value = product(jnp.concatenate([high, low, high, ones], axis=1), w_cat_ref[...])
            halo_ref[side] = value.reshape(items, HALO, width)
            cots = jnp.concatenate([ref[:, 0:STEP, cin : 2 * cin], ref[:, STEP:HALO, cin : 2 * cin]], axis=2)
            high, low = split(cots.reshape(items * STEP, 2 * cin))
            value = product(jnp.concatenate([high, low, high], axis=1), w_out_ref[...])
            edge_ref[:, side * STEP : (side + 1) * STEP, :] = value.reshape(items, STEP, width)

    def run(number, item, end, full):
        half_ref, res_ref, skip_ref, mid_ref, back_ref = (
            ref.at[number : number + 1] for ref in (half_all, res_all, skip_all, mid_all, back_all)
        )
        x_high, x_low = split(x_all[number])
        x_high_ref[number] = x_high
        x_low_ref[number] = x_low
        high, low = x_high.T, x_low.T
        ones = jnp.ones((frames, LANE), BF16)
        half_ref[0] = product(jnp.concatenate([high, low, high, ones], axis=1), w_cat_ref[...])
        rows = SECOND_ROWS if full and frames % SECOND_ROWS == 0 else ROWS
        both = jnp.concatenate([res_ref[0], skip_ref[0]], axis=0)
        lane = lax.broadcasted_iota(jnp.int32, (1, LANE), 1)
        cots = jnp.zeros((2 * cin, LANE), F32)
        for lanes in lane_tiles(frames):
            piece = both[:, lanes]
            cots = cots + (piece if full else jnp.where(lane + lanes.start < end, piece, 0.0))
        cot_ref[number] = cots
        d_high, d_low = split(both)
        d_high_ref[number] = d_high
        d_low_ref[number] = d_low
        high, low = d_high.T, d_low.T
        back_ref[0] = product(jnp.concatenate([high, low, high], axis=1), w_out_ref[...])

        scale, scale_mean = coef_ref[0, pl.ds(item, 1), :], coef_ref[1, pl.ds(item, 1), :]
        window = jnp.clip(end - STEP, 0, frames - HALO)
        window = pl.multiple_of(lax.div(window, 8) * 8, 8)
        tots = [jnp.zeros((8, LANE), F32)] * 10
        for lanes in lane_tiles(width):
            c0, c1 = half_slopes(slope_ref[0:1, lanes])
            gain, shift = gain_ref[0:1, lanes], shift_ref[0:1, lanes]
            factor, offset = 2.0 * gain * scale, shift - gain * scale_mean
            hole = tile(-offset / factor)

            def normed(half, valid):
                value = act_half(half, c0, c1)
                return value if valid is None else jnp.where(valid, value, hole)

            def store(base, count, value):
                normal_ref[pl.ds(base, count), lanes] = value.reshape(count, LANE)

            frame = frame_of(-HALO, HALO)
            store(0, HALO, normed(halo_ref[0, item, :, lanes].reshape(2, 8, LANE), (frame < end) & (frame >= -origin)))
            frame = frame_of(frames, HALO)
            store(HALO + frames, HALO, normed(halo_ref[1, item, :, lanes].reshape(2, 8, LANE), frame < end))

            def fill(base, masked, carry):
                valid = frame_of(base, rows) < end if masked else None
                store(at(base + HALO), rows, normed(load(half_ref.at[0], base, rows, lanes), valid))
                return carry

            def clear(base):
                normal_ref[pl.ds(at(base + HALO), rows), lanes] = jnp.broadcast_to(-offset / factor, (rows, LANE))

            sweep(frames, rows, None if full else end, fill, 0, clear)

            rows_of = [0.5 * taps_ref[tap : tap + 1, lanes] for tap in range(3)]
            taps = [tile(factor * row) for row in rows_of]
            tap_bias = tile(0.5 * tap_bias_ref[0:1, lanes] + offset * (rows_of[0] + rows_of[1] + rows_of[2]))
            m0, m1 = half_slopes(slope_mid_ref[0:1, lanes])

            def conv(base, count):
                value = taps[0] * load(normal_ref, base, count, lanes)
                value = value + taps[1] * load(normal_ref, at(base + STEP), count, lanes)
                value = value + taps[2] * load(normal_ref, at(base + HALO), count, lanes) + tap_bias
                mid_ref[0, pl.ds(base, count), lanes] = value.reshape(count, LANE)
                return value

            conv(0, STEP)
            conv(frames + STEP, STEP)

            def gather(base, masked, carry):
                valid = frame_of(base, rows) < end if masked else None
                mid = conv(at(base + STEP), rows)
                act, grad, _ = act_parts(mid, m0, m1)
                back = load(back_ref.at[0], base, rows, lanes)
                act, grad, back = where_valid(valid, act), where_valid(valid, grad), where_valid(valid, back)
                ex, ez = grad * back, grad * act
                terms = (act, act * act, back, back * act, ex, grad, ez, ex * mid, grad * mid, ez * mid)
                return tuple(old + jnp.sum(new, axis=0) for old, new in zip(carry, terms))

            sums = sweep(frames, rows, None if full else end, gather, (jnp.zeros((8, LANE), F32),) * 10)

            def edge_sums(base, mask):
                mid = load(mid_ref.at[0], at(base + STEP), HALO, lanes)
                act, grad, _ = act_parts(mid, m0, m1)
                back = load(back_ref.at[0], base, HALO, lanes)
                return [jnp.sum(jnp.where(mask, term, 0.0), axis=0) for term in (grad * back, grad, grad * act)]

            frame = frame_of(0, HALO)
            low_sums = edge_sums(0, (frame < end) & (frame + origin < STEP))
            frame = frame_of(window, HALO)
            high_sums = edge_sums(window, (frame < end) & (frame >= end - STEP))
            w0, w1, w2 = (tile(taps_ref[tap : tap + 1, lanes]) for tap in range(3))
            for term in range(4):
                tots[term] = tots[term] + sums[term]
            for term in range(3):
                plain = sums[4 + term]
                edged = (w0 + w1 + w2) * plain - w0 * low_sums[term] - w2 * high_sums[term]
                tots[4 + term] = tots[4 + term] + gain * edged
                tots[7 + term] = (
                    tots[7 + term] + 2.0 * sums[7 + term] - tap_bias_ref[0:1, lanes] * plain - shift * edged
                )

        row = place([total(value) for value in tots])
        for block in range(out_ref.shape[0]):
            out_ref[block, pl.ds(item, 1), :] = row

    for number in range(group):
        item = pl.program_id(0) * group + number
        end = lengths_ref[item] - origin_ref[0]
        both_ways(end >= frames, functools.partial(run, number, item, end))


GRAD_ROWS = 16


def second_norm(mids_ref, count):
    mids = jnp.sum(mids_ref[...], axis=0)
    m = [mids[:, term : term + 1] for term in range(10)]
    mean = 2.0 * m[0] / count
    return m, mean, lax.rsqrt(4.0 * m[1] / count - mean * mean + EPS)


def flatten(flat_ref, grads_ref, half):
    height, width = grads_ref.shape
    tiles = lane_tiles(width)
    count = len(tiles) // 2
    for number, lanes in enumerate(tiles[half * count : (half + 1) * count]):
        flat_ref[number * height : (number + 1) * height] = grads_ref[:, lanes]
    used = height * count
    if used < flat_ref.shape[0]:
        flat_ref[used:] = jnp.zeros((flat_ref.shape[0] - used, LANE), F32)


def third_kernel(
    lengths_ref, origin_ref, core_ref, sums_ref, mids_ref, x_high_all, x_low_all, d_high_all, d_low_all, cots_all,
    half_all, mid_all, back_all, edge_all,
    slope_ref, gain_ref, shift_ref, taps_ref, slope_mid_ref,
    r_high_all, r_low_all, u_high_all, u_low_all, keep_ref, send_ref,
    grad_ref, coef_ref, vector_ref, grads_ref, cot_ref,
):
    items = coef_ref.shape[1]
    group, cin, frames = x_high_all.shape
    width = half_all.shape[2]
    origin = origin_ref[0]

    @pl.when(pl.program_id(0) == 0)
    def _():
        count = counts(lengths_ref, items, width)
        mean1, scale1 = first_norm(sums_ref, count)
        m, mean2, scale2 = second_norm(mids_ref, count)
        beta = scale2 * scale2 * (2.0 * m[3] - mean2 * m[2]) / count
        alpha = m[2] / count - mean2 * beta
        mean_a = scale2 * (m[4] - alpha * m[5] - 2.0 * beta * m[6]) / count
        mean_b = scale2 * (m[7] - alpha * m[8] - 2.0 * beta * m[9]) / count
        values = (
            scale1, scale1 * mean1, scale1 * (mean_a - mean1 * scale1 * mean_b), 2.0 * scale1 * scale1 * mean_b,
            scale2, alpha, 2.0 * beta, scale2 * mean2,
        )
        for number, value in enumerate(values):
            coef_ref[number] = jnp.broadcast_to(value, (items, LANE))
        vector_ref[...] = jnp.zeros(vector_ref.shape, F32)
        grads_ref[...] = jnp.zeros(grads_ref.shape, F32)
        cot_ref[...] = jnp.zeros(cot_ref.shape, F32)

    def run(number, item, end, full):
        half_ref, mid_ref, back_ref, edge_ref = (
            ref.at[number : number + 1] for ref in (half_all, mid_all, back_all, edge_all)
        )
        r_high_ref, r_low_ref, u_high_ref, u_low_ref = (
            ref.at[number : number + 1] for ref in (r_high_all, r_low_all, u_high_all, u_low_all)
        )
        rows = THIRD_ROWS if full else ROWS
        coefs = [tile(coef_ref[number, pl.ds(item, 1), :]) for number in range(8)]
        scale1, scale_mean1, dp_a, dp_b, scale2, dr_a, dr_b, z_a = coefs
        d_high, d_low = d_high_all[number], d_low_all[number]
        cots = cots_all[number]
        cot_ref[0] += cots
        cot_ref[1] += z_a[0:1] * cots

        for lanes in lane_tiles(width):
            m0, m1 = half_slopes(slope_mid_ref[0:1, lanes])

            def middle(base, count, valid, back):
                act, slope, cut = act_parts(load(mid_ref.at[0], base, count, lanes), m0, m1)
                grad = (back - dr_a) - dr_b * act
                grad = where_valid(valid, grad)
                grad_ref[pl.ds(base, count), lanes] = (grad * slope).reshape(count, LANE)
                return act, grad * cut

            frame = frame_of(-STEP, STEP)
            middle(0, STEP, (frame < end) & (frame >= -origin), edge_ref[0:1, 0:STEP, lanes])
            middle(frames + STEP, STEP, frame_of(frames, STEP) < end, edge_ref[0:1, STEP:HALO, lanes])

            def inner(base, masked, carry):
                valid = frame_of(base, rows) < end if masked else None
                act, term = middle(at(base + STEP), rows, valid, load(back_ref.at[0], base, rows, lanes))
                high, low = split(where_valid(valid, act).reshape(rows, LANE))
                r_high_ref[0, pl.ds(base, rows), lanes] = high
                r_low_ref[0, pl.ds(base, rows), lanes] = low
                return carry + jnp.sum(term, axis=0)

            def inner_clear(base):
                grad_ref[pl.ds(at(base + STEP), rows), lanes] = jnp.zeros((rows, LANE), F32)
                r_high_ref[0, pl.ds(base, rows), lanes] = jnp.zeros((rows, LANE), BF16)
                r_low_ref[0, pl.ds(base, rows), lanes] = jnp.zeros((rows, LANE), BF16)

            vector_ref[8, :, lanes] += scale2 / m0 * sweep(
                frames, rows, None if full else end, inner, jnp.zeros((8, LANE), F32), inner_clear
            )

            c0, c1 = half_slopes(slope_ref[0:1, lanes])
            gain, shift = gain_ref[0:1, lanes], shift_ref[0:1, lanes]
            taps = [tile(taps_ref[tap : tap + 1, lanes]) for tap in range(3)]
            outer = gain * scale1
            scaled = [tap * (outer * scale2) for tap in taps]

            def body(base, masked, carry):
                valid = frame_of(base, rows) < end if masked else None
                ahead = load(grad_ref, at(base + HALO), rows, lanes)
                here = load(grad_ref, at(base + STEP), rows, lanes)
                behind = where_valid(valid, load(grad_ref, base, rows, lanes))
                act, slope, cut = act_parts(load(half_ref.at[0], base, rows, lanes), c0, c1)
                dp = scaled[0] * ahead + scaled[1] * here + scaled[2] * behind
                dp = where_valid(valid, (dp - dp_a) - dp_b * act)
                du = dp * slope
                high, low = split(du.reshape(rows, LANE))
                u_high_ref[0, pl.ds(base, rows), lanes] = high
                u_low_ref[0, pl.ds(base, rows), lanes] = low
                terms = (dp * cut, here, ahead * act, here * act, behind * act)
                return tuple(old + jnp.sum(new, axis=0) for old, new in zip(carry, terms))

            def clear(base):
                u_high_ref[0, pl.ds(base, rows), lanes] = jnp.zeros((rows, LANE), BF16)
                u_low_ref[0, pl.ds(base, rows), lanes] = jnp.zeros((rows, LANE), BF16)

            sums = sweep(frames, rows, None if full else end, body, (jnp.zeros((8, LANE), F32),) * 5, clear)
            window = pl.multiple_of(lax.div(jnp.clip(end, 0, frames - HALO), 8) * 8, 8)
            row = frame_of(window, HALO)
            inside = jnp.where((row >= end) & (row < end + STEP), load(grad_ref, window, HALO, lanes), 0.0)
            plains = (
                sums[1] - grad_ref[STEP:HALO, lanes] + grad_ref[frames + STEP : frames + HALO, lanes],
                sums[1],
                sums[1] - grad_ref[frames : frames + STEP, lanes] + grad_ref[0:STEP, lanes] - jnp.sum(inside, axis=0),
            )
            factor, offset = 2.0 * outer, shift - gain * scale_mean1
            vector_ref[1, :, lanes] += sums[0] / c0
            gain_sum = shift_sum = jnp.zeros((8, LANE), F32)
            for tap in range(3):
                plain, times = scale2 * plains[tap], scale2 * sums[2 + tap]
                vector_ref[4 + tap, :, lanes] += factor * times + offset * plain
                gain_sum = gain_sum + taps[tap] * (2.0 * scale1 * times - scale_mean1 * plain)
                shift_sum = shift_sum + taps[tap] * plain
            vector_ref[2, :, lanes] += gain_sum
            vector_ref[3, :, lanes] += shift_sum
            vector_ref[7, :, lanes] += scale2 * sums[1]

        r_high, r_low = r_high_ref[0], r_low_ref[0]
        mixed = product(
            jnp.concatenate([d_high, d_low, d_high], axis=1), jnp.concatenate([r_high, r_high, r_low], axis=0)
        )
        z_0 = 2.0 * scale2[0:1]
        for lanes in lane_tiles(width):
            grads_ref[0 : 2 * cin, lanes] += z_0 * mixed[:, lanes]
        u_high, u_low = u_high_ref[0], u_low_ref[0]
        x_high, x_low = x_high_all[number], x_low_all[number]
        rows_of = jnp.concatenate([x_high, x_low, x_high], axis=1)
        ones = jnp.ones((GRAD_ROWS, frames), BF16)
        ones = jnp.concatenate([ones, jnp.zeros((GRAD_ROWS, frames), BF16), ones], axis=1)
        grads_ref[2 * cin : 3 * cin + GRAD_ROWS] += product(
            jnp.concatenate([rows_of, ones], axis=0), jnp.concatenate([u_high, u_high, u_low], axis=0)
        )

    for number in range(group):
        item = pl.program_id(0) * group + number
        end = lengths_ref[item] - origin_ref[0]
        both_ways(end >= frames, functools.partial(run, number, item, end))

    @pl.when(pl.program_id(0) == items // group - 1)
    def _():
        base = 3 * cin
        grads_ref[0 : 2 * cin] = grads_ref[0 : 2 * cin] - jnp.sum(cot_ref[1], axis=1, keepdims=True)
        for row in range(1, 9):
            grads_ref[base + row : base + row + 1] = jnp.sum(vector_ref[row], axis=0, keepdims=True)
        column = jnp.broadcast_to(jnp.sum(cot_ref[0], axis=1, keepdims=True), (2 * cin, LANE)).T[0:1]
        grads_ref[base + 9 : base + 10] = jnp.zeros((1, width), F32)
        for number in range(2 * cin // LANE):
            grads_ref[base + 9 + number : base + 10 + number, 0:LANE] = column[:, number * LANE : (number + 1) * LANE]
            grads_ref[base + 9 + number : base + 10 + number, width // 2 : width // 2 + LANE] = column[
                :, number * LANE : (number + 1) * LANE
            ]
        for core in range(2):

            @pl.when(core_ref[0] == core)
            def _():
                flatten(keep_ref, grads_ref, core)
                flatten(send_ref, grads_ref, 1 - core)


def outer_kernel(
    lengths_ref, origin_ref, mids_ref, x_ref, res_ref, r_high_ref, r_low_ref, u_high_ref, u_low_ref,
    w_cat_ref, w_out_ref, w_res_ref, w_skip_ref, gain_ref, shift_ref, bias_res_ref, bias_skip_ref, *rest_refs, offset,
):
    res_out_ref, skip_out_ref, x_grad_ref, coef_ref, column_ref, out_turned_ref, in_turned_ref = rest_refs[-7:]
    items = coef_ref.shape[1]
    group, cin, frames = x_ref.shape
    width = w_cat_ref.shape[1]

    @pl.when(pl.program_id(0) == 0)
    def _():
        _, mean, scale = second_norm(mids_ref, counts(lengths_ref, items, width))
        coef_ref[0] = jnp.broadcast_to(2.0 * scale, (items, LANE))
        coef_ref[1] = jnp.broadcast_to(scale * mean, (items, LANE))
        high, low = w_out_ref[0 : 2 * cin].T, w_out_ref[4 * cin : 6 * cin].T
        out_turned_ref[0:width] = high
        out_turned_ref[width : 2 * width] = high
        out_turned_ref[2 * width : 3 * width] = low
        in_turned_ref[:, 0:cin] = w_cat_ref[0:cin].T
        in_turned_ref[:, cin : 2 * cin] = w_cat_ref[2 * cin : 3 * cin].T
        for number, (w_ref, b_ref) in enumerate(((w_res_ref, bias_res_ref), (w_skip_ref, bias_skip_ref))):
            rows = slice(number * cin, (number + 1) * cin)
            column_ref[0, rows] = jnp.broadcast_to(b_ref[...], (LANE, cin)).T
            for spot, vector_of in ((1, shift_ref), (2, gain_ref)):
                value = jnp.sum(w_ref[...] * vector_of[...], axis=1, keepdims=True)
                column_ref[spot, rows] = jnp.broadcast_to(value, (cin, LANE))

    lane = lax.broadcasted_iota(jnp.int32, (1, LANE), 1)
    for number in range(group):
        item = offset + pl.program_id(0) * group + number
        end = lengths_ref[item] - origin_ref[0]
        z_0, z_a = coef_ref[0, pl.ds(item, 1), :], coef_ref[1, pl.ds(item, 1), :]
        r_high, r_low = r_high_ref[number], r_low_ref[number]
        out = product(jnp.concatenate([r_high, r_low, r_high], axis=1), out_turned_ref[...]).T
        pair = product(u_high_ref[number], in_turned_ref[...])
        x_grad = (pair[:, 0:cin] + pair[:, cin : 2 * cin] + product(u_low_ref[number], in_turned_ref[:, 0:cin])).T
        inside = column_ref[1] - z_a * column_ref[2]
        for lanes in lane_tiles(frames):
            valid = lane + lanes.start < end
            wide = column_ref[0] + jnp.where(valid, inside, 0.0) + z_0 * out[:, lanes]
            res_out_ref[number, :, lanes] = wide[0:cin] + x_ref[number, :, lanes]
            skip_out_ref[number, :, lanes] = wide[cin : 2 * cin]
            x_grad_ref[number, :, lanes] = jnp.where(valid, res_ref[number, :, lanes], 0.0) + 2.0 * x_grad[:, lanes]


def last_kernel(
    core_ref, mine_ref, theirs_ref, w_res_ref, w_skip_ref, gain_ref, shift_ref,
    w_in_out, bias_in_out, slope_in_out, gain_in_out, shift_in_out, taps_out, tap_bias_out, slope_mid_out,
    gain_mid_out, shift_mid_out, w_res_out, bias_res_out, w_skip_out, bias_skip_out,
):
    cin, width = w_res_ref.shape
    height = 3 * cin + GRAD_ROWS
    base = 3 * cin
    vectors = ((0, bias_in_out), (1, slope_in_out), (2, gain_in_out), (3, shift_in_out), (7, tap_bias_out), (8, slope_mid_out))
    groups = ((w_res_ref, w_res_out), (w_skip_ref, w_skip_out))
    columns = []
    for number, bias_out in enumerate((bias_res_out, bias_skip_out)):
        row = mine_ref[base + 9 + number : base + 10 + number]
        bias_out[...] = row
        columns.append(jnp.broadcast_to(row, (cin, cin)).T[:, 0:1])
    tiles = lane_tiles(width)
    count = len(tiles) // 2

    def place_half(ref, half):
        for number, lanes in enumerate(tiles[half * count : (half + 1) * count]):
            grads = ref.at[number * height : (number + 1) * height]
            w_in_out[lanes] = grads[2 * cin : 3 * cin].T
            for row, out in vectors:
                out[:, lanes] = grads[base + row : base + row + 1]
            taps_out[:, lanes] = grads[base + 4 : base + 7]
            gain_sum = shift_sum = jnp.zeros((1, LANE), F32)
            for group, (w_ref, w_out) in enumerate(groups):
                products = grads[group * cin : (group + 1) * cin]
                column = columns[group]
                w_out[:, lanes] = gain_ref[:, lanes] * products + shift_ref[:, lanes] * column
                gain_sum = gain_sum + jnp.sum(w_ref[:, lanes] * products, axis=0, keepdims=True)
                shift_sum = shift_sum + jnp.sum(w_ref[:, lanes] * column, axis=0, keepdims=True)
            gain_mid_out[:, lanes] = gain_sum
            shift_mid_out[:, lanes] = shift_sum

    for core in range(2):

        @pl.when(core_ref[0] == core)
        def _():
            place_half(mine_ref, core)
            place_half(theirs_ref, 1 - core)


def whole(array):
    return pl.BlockSpec(array.shape, lambda item: (0,) * len(array.shape))


def per_item(array, group=1, offset=0):
    return pl.BlockSpec((group,) + array.shape[1:], lambda item: (item + offset, 0, 0))


def edge_block(array, group, position):
    return pl.BlockSpec((group, array.shape[1], LANE), lambda item: (item, 0, position))


def sds(*shape, dtype=F32):
    return jax.ShapeDtypeStruct(shape, dtype)


def cost(flops, size):
    return pl.CostEstimate(flops=flops, bytes_accessed=size, transcendentals=0)


def params():
    return pltpu.CompilerParams(dimension_semantics=("arbitrary",), vmem_limit_bytes=VMEM_LIMIT)


def exchange(pieces, axes):
    return lax.all_to_all(pieces, axes, 0, 0)


def local(
    inputs, weight_in, bias_in, slope_in, gain_in, shift_in, depthwise_weight, depthwise_bias, slope_mid, gain_mid,
    shift_mid, weight_res, bias_res, weight_skip, bias_skip, lengths, cot_res, cot_skip,
):
    items, cin, frames = inputs.shape
    width = weight_in.shape[0]
    blocks = lax.axis_size("blk")
    origin = (lax.axis_index("blk") * frames).astype(jnp.int32).reshape(1)
    core = lax.axis_index("core").astype(jnp.int32).reshape(1)
    bias_in, slope_in, gain_in, shift_in, tap_bias, slope_mid, gain_mid, shift_mid, bias_res, bias_skip = (
        vector.reshape(1, -1)
        for vector in (
            bias_in, slope_in, gain_in, shift_in, depthwise_bias, slope_mid, gain_mid, shift_mid, bias_res, bias_skip
        )
    )
    taps = depthwise_weight.T
    ends_spec = pl.BlockSpec(memory_space=pltpu.SMEM)

    half = sds(items, frames, width)
    halo = sds(items, HALO, 2 * cin)
    last = frames // LANE - 1
    sums = sds(blocks, items, LANE)
    w_cat, w_out = sds(3 * cin + LANE, width, dtype=BF16), sds(6 * cin, width, dtype=BF16)
    weights = (weight_in, bias_in, slope_in, weight_res, weight_skip, gain_mid)
    pair = 2 if items % 2 == 0 else 1
    quad = 4 if items % 4 == 0 else 1
    first_sums, to_left, to_right, w_cat, w_out = pl.pallas_call(
        first_kernel,
        grid=(items // quad,),
        in_specs=[ends_spec, ends_spec, per_item(inputs, quad)]
        + [edge_block(array, quad, spot) for array in (cot_res, cot_skip) for spot in (0, last)]
        + [whole(array) for array in weights],
        out_specs=[whole(sums), per_item(halo, quad), per_item(halo, quad), whole(w_cat), whole(w_out)],
        out_shape=[sums, halo, halo, w_cat, w_out],
        compiler_params=params(),
    )(lengths, origin, inputs, cot_res, cot_res, cot_skip, cot_skip, *weights)

    forward = [(block, block + 1) for block in range(blocks - 1)]
    backward = [(target, source) for source, target in forward]
    first_sums = exchange(first_sums, "blk")
    from_left = lax.ppermute(to_right, "blk", forward)
    from_right = lax.ppermute(to_left, "blk", backward)

    mid, edge = sds(items, frames + HALO, width), sds(items, HALO, width)
    small = (first_sums, from_left, from_right)
    weights = (w_cat, w_out, slope_in, gain_in, shift_in, taps, tap_bias, slope_mid)
    rounded = sds(items, frames, width, dtype=BF16)
    kept = (
        sds(items, 2 * cin, frames, dtype=BF16), sds(items, 2 * cin, frames, dtype=BF16),
        sds(items, cin, frames, dtype=BF16), sds(items, cin, frames, dtype=BF16), sds(items, 2 * cin, LANE),
    )
    half, mid, back, edge, mid_sums, d_high, d_low, x_high, x_low, cots = pl.pallas_call(
        second_kernel,
        grid=(items // pair,),
        in_specs=[ends_spec, ends_spec]
        + [whole(array) for array in small]
        + [per_item(array, pair) for array in (inputs, cot_res, cot_skip)]
        + [whole(array) for array in weights],
        out_specs=[per_item(half, pair), per_item(mid, pair), per_item(half, pair), whole(edge), whole(sums)]
        + [per_item(array, pair) for array in kept],
        out_shape=[half, mid, half, edge, sums, *kept],
        scratch_shapes=[
            pltpu.VMEM((2, items, HALO, width), F32),
            pltpu.VMEM((frames + 2 * HALO, width), F32),
            pltpu.VMEM((2, items, LANE), F32),
        ],
        compiler_params=params(),
        cost_estimate=cost(20 * items * frames * cin * width, items * frames * width * 14),
    )(lengths, origin, *small, inputs, cot_res, cot_skip, *weights)
    mid_sums = exchange(mid_sums, "blk")

    small = (first_sums, mid_sums)
    large = (x_high, x_low, d_high, d_low, cots, half, mid, back, edge)
    weights = (slope_in, gain_in, shift_in, taps, slope_mid)
    wide = sds(*inputs.shape)
    height = 3 * cin + GRAD_ROWS
    chips = blocks * lax.axis_size("side")
    piece = -(-height * (width // LANE) // (2 * chips * 8)) * 8
    flat = sds(chips * piece, LANE)
    r_high, r_low, u_high, u_low, keep, send = pl.pallas_call(
        third_kernel,
        grid=(items // pair,),
        in_specs=[ends_spec] * 3
        + [whole(array) for array in small]
        + [per_item(array, pair) for array in large]
        + [whole(array) for array in weights],
        out_specs=[per_item(rounded, pair)] * 4 + [whole(flat)] * 2,
        out_shape=[rounded] * 4 + [flat] * 2,
        scratch_shapes=[
            pltpu.VMEM((frames + HALO, width), F32),
            pltpu.VMEM((8, items, LANE), F32),
            pltpu.VMEM((9, 8, width), F32),
            pltpu.VMEM((height, width), F32),
            pltpu.VMEM((2, 2 * cin, LANE), F32),
        ],
        compiler_params=params(),
        cost_estimate=cost(18 * items * frames * cin * width, items * frames * width * 20),
    )(lengths, origin, core, *small, *large, *weights)

    swap = [(0, 1), (1, 0)]
    keep = keep + lax.ppermute(send, "core", swap)
    keep, r_high = lax.optimization_barrier((keep, r_high))
    pieces = exchange(keep.reshape(chips, piece, LANE), ("blk", "side"))

    weights = (w_cat, w_out, weight_res, weight_skip, gain_mid, shift_mid, bias_res, bias_skip)
    count = items // 2

    def outer(offset, size, earlier):
        pair = 2 if size % 2 == 0 and offset % 2 == 0 else 1
        large = (inputs, cot_res, r_high, r_low, u_high, u_low)
        return pl.pallas_call(
            functools.partial(outer_kernel, offset=offset),
            grid=(size // pair,),
            in_specs=[ends_spec, ends_spec, whole(mid_sums)]
            + [per_item(array, pair, offset // pair) for array in large]
            + [whole(array) for array in weights]
            + [pl.BlockSpec(memory_space=pl.ANY)] * len(earlier),
            out_specs=[per_item(wide, pair, offset // pair)] * 3,
            out_shape=[wide] * 3,
            scratch_shapes=[
                pltpu.VMEM((2, items, LANE), F32),
                pltpu.VMEM((3, 2 * cin, LANE), F32),
                pltpu.VMEM((3 * width, 2 * cin), BF16),
                pltpu.VMEM((width, 2 * cin), BF16),
            ],
            input_output_aliases={17: 0, 18: 1, 19: 2} if earlier else {},
            compiler_params=params(),
            cost_estimate=cost(12 * size * frames * cin * width, size * frames * width * 8),
        )(lengths, origin, mid_sums, *large, *weights, *earlier)

    residual_out, skip_out, grad_inputs = outer(0, count, ())
    pieces, residual_out = lax.optimization_barrier((pieces, residual_out))
    mine = exchange(jnp.broadcast_to(jnp.sum(pieces, axis=0), pieces.shape), ("blk", "side")).reshape(-1, LANE)
    residual_out, skip_out, grad_inputs = outer(count, items - count, (residual_out, skip_out, grad_inputs))
    mine, residual_out = lax.optimization_barrier((mine, residual_out))
    theirs = lax.ppermute(mine, "core", swap)
    vector, short = sds(1, width), sds(1, cin)
    ends_of = (
        sds(width, cin), vector, vector, vector, vector, sds(3, width), vector, vector, vector, vector,
        sds(cin, width), short, sds(cin, width), short,
    )
    tail = pl.pallas_call(
        last_kernel,
        in_specs=[pl.BlockSpec(memory_space=pltpu.SMEM)] + [pl.BlockSpec(memory_space=pltpu.VMEM)] * 6,
        out_shape=ends_of,
    )(core, mine, theirs, weight_res, weight_skip, gain_mid, shift_mid)
    tail = [
        value if number in (0, 10, 12) else value.T if number == 5 else value.reshape(-1)
        for number, value in enumerate(tail)
    ]
    return (residual_out, skip_out, grad_inputs) + tuple(tail)


def solution(mesh):
    devices = mesh.devices
    split_mesh = jax.sharding.Mesh(devices.reshape(devices.shape[0], -1, 2), ("blk", "side", "core"))
    batch = ("side", "core")
    items = P(batch, None, "blk")
    return jax.shard_map(
        local,
        mesh=split_mesh,
        in_specs=(items,) + (P(),) * 14 + (P(batch), items, items),
        out_specs=(items,) * 3 + (P(),) * 14,
        check_vma=False,
    )
```

```python
import functools

import jax
import jax.numpy as jnp
from jax import lax
from jax.experimental import pallas as pl
from jax.experimental.pallas import tpu as pltpu
from jax.sharding import PartitionSpec as P

STEP = 8
HALO = 2 * STEP
EPS = 1e-05
LANE = 128
ROWS = 64
SECOND_ROWS = 128
PIECE = 256
THIRD_ROWS = 32
F32 = jnp.float32
BF16 = jnp.bfloat16
VMEM_LIMIT = 60 * 1024 * 1024


def split(value):
    high = value.astype(BF16)
    low = (value - high.astype(F32)).astype(BF16)
    return high, low


def product(left, right):
    return jnp.dot(left, right, preferred_element_type=F32)


def product_nt(left, right):
    return lax.dot_general(left, right, (((1,), (1,)), ((), ())), preferred_element_type=F32)


def tile(row):
    return jnp.broadcast_to(row, (8, LANE))


def load(ref, base, rows, lanes):
    return ref[pl.ds(base, rows), lanes].reshape(rows // 8, 8, LANE)


def frame_of(base, rows):
    shape = (rows // 8, 8, LANE)
    return lax.broadcasted_iota(jnp.int32, shape, 0) * 8 + lax.broadcasted_iota(jnp.int32, shape, 1) + base


def half_slopes(row):
    return tile(0.5 - 0.5 * row), tile(0.5 + 0.5 * row)


def act_half(half, c0, c1):
    return half * (c1 + c0 * jnp.tanh(half))


def act_parts(half, c0, c1):
    th = jnp.tanh(half)
    ratio = c1 + c0 * th
    act = half * ratio
    cut = half - act
    return act, ratio + cut * (1.0 + th), cut


def total(value):
    return jnp.sum(jnp.sum(value, axis=0, keepdims=True), axis=1, keepdims=True)


def place(values):
    lane = lax.broadcasted_iota(jnp.int32, (1, LANE), 1)
    row = jnp.zeros((1, LANE), F32)
    for position, value in enumerate(values):
        row = jnp.where(lane == position, value, row)
    return row


def lane_tiles(width):
    return [slice(start, start + LANE) for start in range(0, width, LANE)]


def first_kernel(
    lengths_ref, origin_ref, x_ref, res_l_ref, res_r_ref, skip_l_ref, skip_r_ref, w_in_ref, bias_ref, slope_ref,
    w_res_ref, w_skip_ref, gain_ref,
    sums_ref, left_ref, right_ref, w_cat_ref, w_out_ref,
):
    group, cin, frames = x_ref.shape
    width = w_in_ref.shape[0]

    @pl.when(pl.program_id(0) == 0)
    def _():
        high, low = split(0.5 * w_in_ref[...].T)
        w_cat_ref[0:cin] = high
        w_cat_ref[cin : 2 * cin] = high
        w_cat_ref[2 * cin : 3 * cin] = low
        row = lax.broadcasted_iota(jnp.int32, (LANE, width), 0)
        bias = jnp.broadcast_to(0.5 * bias_ref[...], (LANE, width))
        near = bias.astype(BF16).astype(F32)
        w_cat_ref[3 * cin :] = jnp.where(row == 0, near, jnp.where(row == 1, bias - near, 0.0)).astype(BF16)
        for number, ref in enumerate((w_res_ref, w_skip_ref)):
            high, low = split(ref[...] * gain_ref[...])
            start = number * cin
            w_out_ref[start : start + cin] = high
            w_out_ref[2 * cin + start : 3 * cin + start] = high
            w_out_ref[4 * cin + start : 5 * cin + start] = low

    step = min(PIECE, frames)
    for number in range(group):
        item = pl.program_id(0) * group + number
        end = lengths_ref[item] - origin_ref[0]
        first = second = jnp.zeros((8, LANE), F32)
        for start in range(0, frames, step):
            xt = x_ref[number, :, start : start + step].astype(BF16).T
            ones = jnp.ones((step, LANE), BF16)
            weights = jnp.concatenate([w_cat_ref[0:cin], w_cat_ref[3 * cin :]], axis=0)
            half = product(jnp.concatenate([xt, ones], axis=1), weights)
            valid = frame_of(start, step) < end
            for lanes in lane_tiles(width):
                c0, c1 = half_slopes(slope_ref[0:1, lanes])
                value = act_half(half[:, lanes].reshape(step // 8, 8, LANE), c0, c1)
                value = jnp.where(valid, value, 0.0)
                first = first + jnp.sum(value, axis=0)
                second = second + jnp.sum(value * value, axis=0)
        row = place((total(first), total(second)))
        for block in range(sums_ref.shape[0]):
            sums_ref[block, pl.ds(item, 1), :] = row
        left_ref[number, :, 0:cin] = x_ref[number, :, 0:LANE].T[0:HALO]
        right_ref[number, :, 0:cin] = x_ref[number, :, frames - LANE : frames].T[LANE - HALO : LANE]
        left_ref[number, 0:STEP, cin : 2 * cin] = res_l_ref[number].T[0:STEP]
        left_ref[number, STEP:HALO, cin : 2 * cin] = skip_l_ref[number].T[0:STEP]
        right_ref[number, 0:STEP, cin : 2 * cin] = res_r_ref[number].T[LANE - STEP : LANE]
        right_ref[number, STEP:HALO, cin : 2 * cin] = skip_r_ref[number].T[LANE - STEP : LANE]


def at(base):
    return base if isinstance(base, int) else pl.multiple_of(base, 8)


def sweep(frames, rows, end, body, init, rest=None):
    if end is None:
        carry = init
        for base in range(0, frames, rows):
            carry = body(base, False, carry)
        return carry
    live = jnp.clip(end, 0, frames)
    full, some = lax.div(live, rows), lax.div(live + (rows - 1), rows)
    carry = lax.fori_loop(0, full, lambda n, c: body(pl.multiple_of(n * rows, rows), False, c), init)
    carry = lax.fori_loop(full, some, lambda n, c: body(pl.multiple_of(n * rows, rows), True, c), carry)
    if rest is not None:

        def clear(n, c):
            rest(pl.multiple_of(n * rows, rows))
            return c

        lax.fori_loop(some, frames // rows, clear, 0)
    return carry


def both_ways(full, run):
    pl.when(full)(lambda: run(True))
    pl.when(jnp.logical_not(full))(lambda: run(False))


def where_valid(valid, value):
    return value if valid is None else jnp.where(valid, value, 0.0)


def counts(lengths_ref, items, width):
    row = lax.broadcasted_iota(jnp.int32, (items, 1), 0)
    lengths = jnp.zeros((items, 1), jnp.int32)
    for item in range(items):
        lengths = jnp.where(row == item, lengths_ref[item], lengths)
    return lengths.astype(F32) * float(width)


def first_norm(sums_ref, count):
    sums = jnp.sum(sums_ref[...], axis=0)
    mean = 2.0 * sums[:, 0:1] / count
    var = 4.0 * sums[:, 1:2] / count - mean * mean
    return mean, lax.rsqrt(var + EPS)


def second_kernel(
    lengths_ref, origin_ref, sums_ref, from_left_ref, from_right_ref, x_all, res_all, skip_all,
    w_cat_ref, w_out_ref, slope_ref, gain_ref, shift_ref, taps_ref, tap_bias_ref, slope_mid_ref,
    half_all, mid_all, back_all, edge_ref, out_ref,
    halo_ref, normal_ref, coef_ref,
):
    items = out_ref.shape[1]
    group, frames, width = half_all.shape
    cin = x_all.shape[1]
    origin = origin_ref[0]

    @pl.when(pl.program_id(0) == 0)
    def _():
        mean, scale = first_norm(sums_ref, counts(lengths_ref, items, width))
        coef_ref[0] = jnp.broadcast_to(scale, (items, LANE))
        coef_ref[1] = jnp.broadcast_to(scale * mean, (items, LANE))
        for side, ref in enumerate((from_left_ref, from_right_ref)):
            high, low = split(ref[:, :, 0:cin].reshape(items * HALO, cin))
            ones = jnp.ones((items * HALO, LANE), BF16)
            value = product(jnp.concatenate([high, low, high, ones], axis=1), w_cat_ref[...])
            halo_ref[side] = value.reshape(items, HALO, width)
            cots = jnp.concatenate([ref[:, 0:STEP, cin : 2 * cin], ref[:, STEP:HALO, cin : 2 * cin]], axis=2)
            high, low = split(cots.reshape(items * STEP, 2 * cin))
            value = product(jnp.concatenate([high, low, high], axis=1), w_out_ref[...])
            edge_ref[:, side * STEP : (side + 1) * STEP, :] = value.reshape(items, STEP, width)

    def run(number, item, end, full):
        half_ref, res_ref, skip_ref, mid_ref, back_ref = (
            ref.at[number : number + 1] for ref in (half_all, res_all, skip_all, mid_all, back_all)
        )
        high, low = split(x_all[number].T)
        ones = jnp.ones((frames, LANE), BF16)
        half_ref[0] = product(jnp.concatenate([high, low, high, ones], axis=1), w_cat_ref[...])
        rows = SECOND_ROWS if full and frames % SECOND_ROWS == 0 else ROWS
        d_high, d_low = split(jnp.concatenate([res_ref[0], skip_ref[0]], axis=0))
        high, low = d_high.T, d_low.T
        back_ref[0] = product(jnp.concatenate([high, low, high], axis=1), w_out_ref[...])

        scale, scale_mean = coef_ref[0, pl.ds(item, 1), :], coef_ref[1, pl.ds(item, 1), :]
        window = jnp.clip(end - STEP, 0, frames - HALO)
        window = pl.multiple_of(lax.div(window, 8) * 8, 8)
        tots = [jnp.zeros((8, LANE), F32)] * 10
        for lanes in lane_tiles(width):
            c0, c1 = half_slopes(slope_ref[0:1, lanes])
            gain, shift = gain_ref[0:1, lanes], shift_ref[0:1, lanes]
            factor, offset = 2.0 * gain * scale, shift - gain * scale_mean
            hole = tile(-offset / factor)

            def normed(half, valid):
                value = act_half(half, c0, c1)
                return value if valid is None else jnp.where(valid, value, hole)

            def store(base, count, value):
                normal_ref[pl.ds(base, count), lanes] = value.reshape(count, LANE)

            frame = frame_of(-HALO, HALO)
            store(0, HALO, normed(halo_ref[0, item, :, lanes].reshape(2, 8, LANE), (frame < end) & (frame >= -origin)))
            frame = frame_of(frames, HALO)
            store(HALO + frames, HALO, normed(halo_ref[1, item, :, lanes].reshape(2, 8, LANE), frame < end))

            def fill(base, masked, carry):
                valid = frame_of(base, rows) < end if masked else None
                store(at(base + HALO), rows, normed(load(half_ref.at[0], base, rows, lanes), valid))
                return carry

            def clear(base):
                normal_ref[pl.ds(at(base + HALO), rows), lanes] = jnp.broadcast_to(-offset / factor, (rows, LANE))

            sweep(frames, rows, None if full else end, fill, 0, clear)

            rows_of = [0.5 * taps_ref[tap : tap + 1, lanes] for tap in range(3)]
            taps = [tile(factor * row) for row in rows_of]
            tap_bias = tile(0.5 * tap_bias_ref[0:1, lanes] + offset * (rows_of[0] + rows_of[1] + rows_of[2]))
            m0, m1 = half_slopes(slope_mid_ref[0:1, lanes])

            def conv(base, count):
                value = taps[0] * load(normal_ref, base, count, lanes)
                value = value + taps[1] * load(normal_ref, at(base + STEP), count, lanes)
                value = value + taps[2] * load(normal_ref, at(base + HALO), count, lanes) + tap_bias
                mid_ref[0, pl.ds(base, count), lanes] = value.reshape(count, LANE)
                return value

            conv(0, STEP)
            conv(frames + STEP, STEP)

            def gather(base, masked, carry):
                valid = frame_of(base, rows) < end if masked else None
                mid = conv(at(base + STEP), rows)
                act, grad, _ = act_parts(mid, m0, m1)
                back = load(back_ref.at[0], base, rows, lanes)
                act, grad, back = where_valid(valid, act), where_valid(valid, grad), where_valid(valid, back)
                ex, ez = grad * back, grad * act
                terms = (act, act * act, back, back * act, ex, grad, ez, ex * mid, grad * mid, ez * mid)
                return tuple(old + jnp.sum(new, axis=0) for old, new in zip(carry, terms))

            sums = sweep(frames, rows, None if full else end, gather, (jnp.zeros((8, LANE), F32),) * 10)

            def edge_sums(base, mask):
                mid = load(mid_ref.at[0], at(base + STEP), HALO, lanes)
                act, grad, _ = act_parts(mid, m0, m1)
                back = load(back_ref.at[0], base, HALO, lanes)
                return [jnp.sum(jnp.where(mask, term, 0.0), axis=0) for term in (grad * back, grad, grad * act)]

            frame = frame_of(0, HALO)
            low_sums = edge_sums(0, (frame < end) & (frame + origin < STEP))
            frame = frame_of(window, HALO)
            high_sums = edge_sums(window, (frame < end) & (frame >= end - STEP))
            w0, w1, w2 = (tile(taps_ref[tap : tap + 1, lanes]) for tap in range(3))
            for term in range(4):
                tots[term] = tots[term] + sums[term]
            for term in range(3):
                plain = sums[4 + term]
                edged = (w0 + w1 + w2) * plain - w0 * low_sums[term] - w2 * high_sums[term]
                tots[4 + term] = tots[4 + term] + gain * edged
                tots[7 + term] = (
                    tots[7 + term] + 2.0 * sums[7 + term] - tap_bias_ref[0:1, lanes] * plain - shift * edged
                )

        row = place([total(value) for value in tots])
        for block in range(out_ref.shape[0]):
            out_ref[block, pl.ds(item, 1), :] = row

    for number in range(group):
        item = pl.program_id(0) * group + number
        end = lengths_ref[item] - origin_ref[0]
        both_ways(end >= frames, functools.partial(run, number, item, end))


GRAD_ROWS = 16


def second_norm(mids_ref, count):
    mids = jnp.sum(mids_ref[...], axis=0)
    m = [mids[:, term : term + 1] for term in range(10)]
    mean = 2.0 * m[0] / count
    return m, mean, lax.rsqrt(4.0 * m[1] / count - mean * mean + EPS)


def flatten(flat_ref, grads_ref, half):
    height, width = grads_ref.shape
    tiles = lane_tiles(width)
    count = len(tiles) // 2
    for number, lanes in enumerate(tiles[half * count : (half + 1) * count]):
        flat_ref[number * height : (number + 1) * height] = grads_ref[:, lanes]
    used = height * count
    if used < flat_ref.shape[0]:
        flat_ref[used:] = jnp.zeros((flat_ref.shape[0] - used, LANE), F32)


def third_kernel(
    lengths_ref, origin_ref, core_ref, sums_ref, mids_ref, x_all, res_all, skip_all, half_all, mid_all, back_all, edge_all,
    slope_ref, gain_ref, shift_ref, taps_ref, slope_mid_ref,
    r_high_all, r_low_all, u_high_all, u_low_all, keep_ref, send_ref,
    grad_ref, coef_ref, vector_ref, grads_ref, cot_ref,
):
    items = coef_ref.shape[1]
    group, cin, frames = x_all.shape
    width = half_all.shape[2]
    origin = origin_ref[0]

    @pl.when(pl.program_id(0) == 0)
    def _():
        count = counts(lengths_ref, items, width)
        mean1, scale1 = first_norm(sums_ref, count)
        m, mean2, scale2 = second_norm(mids_ref, count)
        beta = scale2 * scale2 * (2.0 * m[3] - mean2 * m[2]) / count
        alpha = m[2] / count - mean2 * beta
        mean_a = scale2 * (m[4] - alpha * m[5] - 2.0 * beta * m[6]) / count
        mean_b = scale2 * (m[7] - alpha * m[8] - 2.0 * beta * m[9]) / count
        values = (
            scale1, scale1 * mean1, scale1 * (mean_a - mean1 * scale1 * mean_b), 2.0 * scale1 * scale1 * mean_b,
            scale2, alpha, 2.0 * beta, scale2 * mean2,
        )
        for number, value in enumerate(values):
            coef_ref[number] = jnp.broadcast_to(value, (items, LANE))
        vector_ref[...] = jnp.zeros(vector_ref.shape, F32)
        grads_ref[...] = jnp.zeros(grads_ref.shape, F32)
        cot_ref[...] = jnp.zeros(cot_ref.shape, F32)

    def run(number, item, end, full):
        x_ref, res_ref, skip_ref, half_ref, mid_ref, back_ref, edge_ref = (
            ref.at[number : number + 1] for ref in (x_all, res_all, skip_all, half_all, mid_all, back_all, edge_all)
        )
        r_high_ref, r_low_ref, u_high_ref, u_low_ref = (
            ref.at[number : number + 1] for ref in (r_high_all, r_low_all, u_high_all, u_low_all)
        )
        rows = THIRD_ROWS if full else ROWS
        coefs = [tile(coef_ref[number, pl.ds(item, 1), :]) for number in range(8)]
        scale1, scale_mean1, dp_a, dp_b, scale2, dr_a, dr_b, z_a = coefs
        both = jnp.concatenate([res_ref[0], skip_ref[0]], axis=0)
        d_high, d_low = split(both)
        lane = lax.broadcasted_iota(jnp.int32, (1, LANE), 1)
        cots = jnp.zeros((2 * cin, LANE), F32)
        for lanes in lane_tiles(frames):
            piece = both[:, lanes]
            cots = cots + (piece if full else jnp.where(lane + lanes.start < end, piece, 0.0))
        cot_ref[0] += cots
        cot_ref[1] += z_a[0:1] * cots

        for lanes in lane_tiles(width):
            m0, m1 = half_slopes(slope_mid_ref[0:1, lanes])

            def middle(base, count, valid, back):
                act, slope, cut = act_parts(load(mid_ref.at[0], base, count, lanes), m0, m1)
                grad = (back - dr_a) - dr_b * act
                grad = where_valid(valid, grad)
                grad_ref[pl.ds(base, count), lanes] = (grad * slope).reshape(count, LANE)
                return act, grad * cut

            frame = frame_of(-STEP, STEP)
            middle(0, STEP, (frame < end) & (frame >= -origin), edge_ref[0:1, 0:STEP, lanes])
            middle(frames + STEP, STEP, frame_of(frames, STEP) < end, edge_ref[0:1, STEP:HALO, lanes])

            def inner(base, masked, carry):
                valid = frame_of(base, rows) < end if masked else None
                act, term = middle(at(base + STEP), rows, valid, load(back_ref.at[0], base, rows, lanes))
                high, low = split(where_valid(valid, act).reshape(rows, LANE))
                r_high_ref[0, pl.ds(base, rows), lanes] = high
                r_low_ref[0, pl.ds(base, rows), lanes] = low
                return carry + jnp.sum(term, axis=0)

            def inner_clear(base):
                grad_ref[pl.ds(at(base + STEP), rows), lanes] = jnp.zeros((rows, LANE), F32)
                r_high_ref[0, pl.ds(base, rows), lanes] = jnp.zeros((rows, LANE), BF16)
                r_low_ref[0, pl.ds(base, rows), lanes] = jnp.zeros((rows, LANE), BF16)

            vector_ref[8, :, lanes] += scale2 / m0 * sweep(
                frames, rows, None if full else end, inner, jnp.zeros((8, LANE), F32), inner_clear
            )

            c0, c1 = half_slopes(slope_ref[0:1, lanes])
            gain, shift = gain_ref[0:1, lanes], shift_ref[0:1, lanes]
            taps = [tile(taps_ref[tap : tap + 1, lanes]) for tap in range(3)]
            outer = gain * scale1
            scaled = [tap * (outer * scale2) for tap in taps]

            def body(base, masked, carry):
                valid = frame_of(base, rows) < end if masked else None
                ahead = load(grad_ref, at(base + HALO), rows, lanes)
                here = load(grad_ref, at(base + STEP), rows, lanes)
                behind = where_valid(valid, load(grad_ref, base, rows, lanes))
                act, slope, cut = act_parts(load(half_ref.at[0], base, rows, lanes), c0, c1)
                dp = scaled[0] * ahead + scaled[1] * here + scaled[2] * behind
                dp = where_valid(valid, (dp - dp_a) - dp_b * act)
                du = dp * slope
                high, low = split(du.reshape(rows, LANE))
                u_high_ref[0, pl.ds(base, rows), lanes] = high
                u_low_ref[0, pl.ds(base, rows), lanes] = low
                terms = (dp * cut, here, ahead * act, here * act, behind * act)
                return tuple(old + jnp.sum(new, axis=0) for old, new in zip(carry, terms))

            def clear(base):
                u_high_ref[0, pl.ds(base, rows), lanes] = jnp.zeros((rows, LANE), BF16)
                u_low_ref[0, pl.ds(base, rows), lanes] = jnp.zeros((rows, LANE), BF16)

            sums = sweep(frames, rows, None if full else end, body, (jnp.zeros((8, LANE), F32),) * 5, clear)
            window = pl.multiple_of(lax.div(jnp.clip(end, 0, frames - HALO), 8) * 8, 8)
            row = frame_of(window, HALO)
            inside = jnp.where((row >= end) & (row < end + STEP), load(grad_ref, window, HALO, lanes), 0.0)
            plains = (
                sums[1] - grad_ref[STEP:HALO, lanes] + grad_ref[frames + STEP : frames + HALO, lanes],
                sums[1],
                sums[1] - grad_ref[frames : frames + STEP, lanes] + grad_ref[0:STEP, lanes] - jnp.sum(inside, axis=0),
            )
            factor, offset = 2.0 * outer, shift - gain * scale_mean1
            vector_ref[1, :, lanes] += sums[0] / c0
            gain_sum = shift_sum = jnp.zeros((8, LANE), F32)
            for tap in range(3):
                plain, times = scale2 * plains[tap], scale2 * sums[2 + tap]
                vector_ref[4 + tap, :, lanes] += factor * times + offset * plain
                gain_sum = gain_sum + taps[tap] * (2.0 * scale1 * times - scale_mean1 * plain)
                shift_sum = shift_sum + taps[tap] * plain
            vector_ref[2, :, lanes] += gain_sum
            vector_ref[3, :, lanes] += shift_sum
            vector_ref[7, :, lanes] += scale2 * sums[1]

        mixed = product(jnp.concatenate([d_high, d_low], axis=0), r_high_ref[0])
        mixed = mixed[0 : 2 * cin] + mixed[2 * cin : 4 * cin] + product(d_high, r_low_ref[0])
        z_0 = 2.0 * scale2[0:1]
        for lanes in lane_tiles(width):
            grads_ref[0 : 2 * cin, lanes] += z_0 * mixed[:, lanes]
        x_high, x_low = split(x_ref[0])
        x_high = jnp.concatenate([x_high, jnp.ones((GRAD_ROWS, frames), BF16)], axis=0)
        mixed = product(jnp.concatenate([x_high, x_low], axis=0), u_high_ref[0])
        high_rows = cin + GRAD_ROWS
        outer_sums = mixed[0:high_rows] + product(x_high, u_low_ref[0])
        grads_ref[2 * cin : 3 * cin] += outer_sums[0:cin] + mixed[high_rows : high_rows + cin]
        grads_ref[3 * cin : 3 * cin + GRAD_ROWS] += outer_sums[cin:high_rows]

    for number in range(group):
        item = pl.program_id(0) * group + number
        end = lengths_ref[item] - origin_ref[0]
        both_ways(end >= frames, functools.partial(run, number, item, end))

    @pl.when(pl.program_id(0) == items // group - 1)
    def _():
        base = 3 * cin
        grads_ref[0 : 2 * cin] = grads_ref[0 : 2 * cin] - jnp.sum(cot_ref[1], axis=1, keepdims=True)
        for row in range(1, 9):
            grads_ref[base + row : base + row + 1] = jnp.sum(vector_ref[row], axis=0, keepdims=True)
        column = jnp.broadcast_to(jnp.sum(cot_ref[0], axis=1, keepdims=True), (2 * cin, LANE)).T[0:1]
        grads_ref[base + 9 : base + 10] = jnp.zeros((1, width), F32)
        for number in range(2 * cin // LANE):
            grads_ref[base + 9 + number : base + 10 + number, 0:LANE] = column[:, number * LANE : (number + 1) * LANE]
            grads_ref[base + 9 + number : base + 10 + number, width // 2 : width // 2 + LANE] = column[
                :, number * LANE : (number + 1) * LANE
            ]
        for core in range(2):

            @pl.when(core_ref[0] == core)
            def _():
                flatten(keep_ref, grads_ref, core)
                flatten(send_ref, grads_ref, 1 - core)


def outer_kernel(
    lengths_ref, origin_ref, mids_ref, x_ref, res_ref, r_high_ref, r_low_ref, u_high_ref, u_low_ref,
    w_cat_ref, w_out_ref, w_res_ref, w_skip_ref, gain_ref, shift_ref, bias_res_ref, bias_skip_ref, *rest_refs, offset,
):
    res_out_ref, skip_out_ref, x_grad_ref, coef_ref, column_ref, out_turned_ref, in_turned_ref = rest_refs[-7:]
    items = coef_ref.shape[1]
    group, cin, frames = x_ref.shape
    width = w_cat_ref.shape[1]

    @pl.when(pl.program_id(0) == 0)
    def _():
        _, mean, scale = second_norm(mids_ref, counts(lengths_ref, items, width))
        coef_ref[0] = jnp.broadcast_to(2.0 * scale, (items, LANE))
        coef_ref[1] = jnp.broadcast_to(scale * mean, (items, LANE))
        high, low = w_out_ref[0 : 2 * cin].T, w_out_ref[4 * cin : 6 * cin].T
        out_turned_ref[0:width] = high
        out_turned_ref[width : 2 * width] = high
        out_turned_ref[2 * width : 3 * width] = low
        in_turned_ref[:, 0:cin] = w_cat_ref[0:cin].T
        in_turned_ref[:, cin : 2 * cin] = w_cat_ref[2 * cin : 3 * cin].T
        for number, (w_ref, b_ref) in enumerate(((w_res_ref, bias_res_ref), (w_skip_ref, bias_skip_ref))):
            rows = slice(number * cin, (number + 1) * cin)
            column_ref[0, rows] = jnp.broadcast_to(b_ref[...], (LANE, cin)).T
            for spot, vector_of in ((1, shift_ref), (2, gain_ref)):
                value = jnp.sum(w_ref[...] * vector_of[...], axis=1, keepdims=True)
                column_ref[spot, rows] = jnp.broadcast_to(value, (cin, LANE))

    lane = lax.broadcasted_iota(jnp.int32, (1, LANE), 1)
    for number in range(group):
        item = offset + pl.program_id(0) * group + number
        end = lengths_ref[item] - origin_ref[0]
        z_0, z_a = coef_ref[0, pl.ds(item, 1), :], coef_ref[1, pl.ds(item, 1), :]
        r_high, r_low = r_high_ref[number], r_low_ref[number]
        out = product(jnp.concatenate([r_high, r_low, r_high], axis=1), out_turned_ref[...]).T
        pair = product(u_high_ref[number], in_turned_ref[...])
        x_grad = (pair[:, 0:cin] + pair[:, cin : 2 * cin] + product(u_low_ref[number], in_turned_ref[:, 0:cin])).T
        inside = column_ref[1] - z_a * column_ref[2]
        for lanes in lane_tiles(frames):
            valid = lane + lanes.start < end
            wide = column_ref[0] + jnp.where(valid, inside, 0.0) + z_0 * out[:, lanes]
            res_out_ref[number, :, lanes] = wide[0:cin] + x_ref[number, :, lanes]
            skip_out_ref[number, :, lanes] = wide[cin : 2 * cin]
            x_grad_ref[number, :, lanes] = jnp.where(valid, res_ref[number, :, lanes], 0.0) + 2.0 * x_grad[:, lanes]


def last_kernel(
    core_ref, mine_ref, theirs_ref, w_res_ref, w_skip_ref, gain_ref, shift_ref,
    w_in_out, bias_in_out, slope_in_out, gain_in_out, shift_in_out, taps_out, tap_bias_out, slope_mid_out,
    gain_mid_out, shift_mid_out, w_res_out, bias_res_out, w_skip_out, bias_skip_out,
):
    cin, width = w_res_ref.shape
    height = 3 * cin + GRAD_ROWS
    base = 3 * cin
    vectors = ((0, bias_in_out), (1, slope_in_out), (2, gain_in_out), (3, shift_in_out), (7, tap_bias_out), (8, slope_mid_out))
    groups = ((w_res_ref, w_res_out), (w_skip_ref, w_skip_out))
    columns = []
    for number, bias_out in enumerate((bias_res_out, bias_skip_out)):
        row = mine_ref[base + 9 + number : base + 10 + number]
        bias_out[...] = row
        columns.append(jnp.broadcast_to(row, (cin, cin)).T[:, 0:1])
    tiles = lane_tiles(width)
    count = len(tiles) // 2

    def place_half(ref, half):
        for number, lanes in enumerate(tiles[half * count : (half + 1) * count]):
            grads = ref.at[number * height : (number + 1) * height]
            w_in_out[lanes] = grads[2 * cin : 3 * cin].T
            for row, out in vectors:
                out[:, lanes] = grads[base + row : base + row + 1]
            taps_out[:, lanes] = grads[base + 4 : base + 7]
            gain_sum = shift_sum = jnp.zeros((1, LANE), F32)
            for group, (w_ref, w_out) in enumerate(groups):
                products = grads[group * cin : (group + 1) * cin]
                column = columns[group]
                w_out[:, lanes] = gain_ref[:, lanes] * products + shift_ref[:, lanes] * column
                gain_sum = gain_sum + jnp.sum(w_ref[:, lanes] * products, axis=0, keepdims=True)
                shift_sum = shift_sum + jnp.sum(w_ref[:, lanes] * column, axis=0, keepdims=True)
            gain_mid_out[:, lanes] = gain_sum
            shift_mid_out[:, lanes] = shift_sum

    for core in range(2):

        @pl.when(core_ref[0] == core)
        def _():
            place_half(mine_ref, core)
            place_half(theirs_ref, 1 - core)


def whole(array):
    return pl.BlockSpec(array.shape, lambda item: (0,) * len(array.shape))


def per_item(array, group=1, offset=0):
    return pl.BlockSpec((group,) + array.shape[1:], lambda item: (item + offset, 0, 0))


def edge_block(array, group, position):
    return pl.BlockSpec((group, array.shape[1], LANE), lambda item: (item, 0, position))


def sds(*shape, dtype=F32):
    return jax.ShapeDtypeStruct(shape, dtype)


def cost(flops, size):
    return pl.CostEstimate(flops=flops, bytes_accessed=size, transcendentals=0)


def params():
    return pltpu.CompilerParams(dimension_semantics=("arbitrary",), vmem_limit_bytes=VMEM_LIMIT)


def exchange(pieces, axes):
    return lax.all_to_all(pieces, axes, 0, 0)


def local(
    inputs, weight_in, bias_in, slope_in, gain_in, shift_in, depthwise_weight, depthwise_bias, slope_mid, gain_mid,
    shift_mid, weight_res, bias_res, weight_skip, bias_skip, lengths, cot_res, cot_skip,
):
    items, cin, frames = inputs.shape
    width = weight_in.shape[0]
    blocks = lax.axis_size("blk")
    origin = (lax.axis_index("blk") * frames).astype(jnp.int32).reshape(1)
    core = lax.axis_index("core").astype(jnp.int32).reshape(1)
    bias_in, slope_in, gain_in, shift_in, tap_bias, slope_mid, gain_mid, shift_mid, bias_res, bias_skip = (
        vector.reshape(1, -1)
        for vector in (
            bias_in, slope_in, gain_in, shift_in, depthwise_bias, slope_mid, gain_mid, shift_mid, bias_res, bias_skip
        )
    )
    taps = depthwise_weight.T
    ends_spec = pl.BlockSpec(memory_space=pltpu.SMEM)

    half = sds(items, frames, width)
    halo = sds(items, HALO, 2 * cin)
    last = frames // LANE - 1
    sums = sds(blocks, items, LANE)
    w_cat, w_out = sds(3 * cin + LANE, width, dtype=BF16), sds(6 * cin, width, dtype=BF16)
    weights = (weight_in, bias_in, slope_in, weight_res, weight_skip, gain_mid)
    pair = 2 if items % 2 == 0 else 1
    quad = 4 if items % 4 == 0 else 1
    first_sums, to_left, to_right, w_cat, w_out = pl.pallas_call(
        first_kernel,
        grid=(items // quad,),
        in_specs=[ends_spec, ends_spec, per_item(inputs, quad)]
        + [edge_block(array, quad, spot) for array in (cot_res, cot_skip) for spot in (0, last)]
        + [whole(array) for array in weights],
        out_specs=[whole(sums), per_item(halo, quad), per_item(halo, quad), whole(w_cat), whole(w_out)],
        out_shape=[sums, halo, halo, w_cat, w_out],
        compiler_params=params(),
    )(lengths, origin, inputs, cot_res, cot_res, cot_skip, cot_skip, *weights)

    forward = [(block, block + 1) for block in range(blocks - 1)]
    backward = [(target, source) for source, target in forward]
    first_sums = exchange(first_sums, "blk")
    from_left = lax.ppermute(to_right, "blk", forward)
    from_right = lax.ppermute(to_left, "blk", backward)

    mid, edge = sds(items, frames + HALO, width), sds(items, HALO, width)
    small = (first_sums, from_left, from_right)
    weights = (w_cat, w_out, slope_in, gain_in, shift_in, taps, tap_bias, slope_mid)
    rounded = sds(items, frames, width, dtype=BF16)
    half, mid, back, edge, mid_sums = pl.pallas_call(
        second_kernel,
        grid=(items // pair,),
        in_specs=[ends_spec, ends_spec]
        + [whole(array) for array in small]
        + [per_item(array, pair) for array in (inputs, cot_res, cot_skip)]
        + [whole(array) for array in weights],
        out_specs=[per_item(half, pair), per_item(mid, pair), per_item(half, pair), whole(edge), whole(sums)],
        out_shape=[half, mid, half, edge, sums],
        scratch_shapes=[
            pltpu.VMEM((2, items, HALO, width), F32),
            pltpu.VMEM((frames + 2 * HALO, width), F32),
            pltpu.VMEM((2, items, LANE), F32),
        ],
        compiler_params=params(),
        cost_estimate=cost(20 * items * frames * cin * width, items * frames * width * 14),
    )(lengths, origin, *small, inputs, cot_res, cot_skip, *weights)
    mid_sums = exchange(mid_sums, "blk")

    small = (first_sums, mid_sums)
    large = (inputs, cot_res, cot_skip, half, mid, back, edge)
    weights = (slope_in, gain_in, shift_in, taps, slope_mid)
    wide = sds(*inputs.shape)
    height = 3 * cin + GRAD_ROWS
    chips = blocks * lax.axis_size("side")
    piece = -(-height * (width // LANE) // (2 * chips * 8)) * 8
    flat = sds(chips * piece, LANE)
    r_high, r_low, u_high, u_low, keep, send = pl.pallas_call(
        third_kernel,
        grid=(items // pair,),
        in_specs=[ends_spec] * 3
        + [whole(array) for array in small]
        + [per_item(array, pair) for array in large]
        + [whole(array) for array in weights],
        out_specs=[per_item(rounded, pair)] * 4 + [whole(flat)] * 2,
        out_shape=[rounded] * 4 + [flat] * 2,
        scratch_shapes=[
            pltpu.VMEM((frames + HALO, width), F32),
            pltpu.VMEM((8, items, LANE), F32),
            pltpu.VMEM((9, 8, width), F32),
            pltpu.VMEM((height, width), F32),
            pltpu.VMEM((2, 2 * cin, LANE), F32),
        ],
        compiler_params=params(),
        cost_estimate=cost(18 * items * frames * cin * width, items * frames * width * 20),
    )(lengths, origin, core, *small, *large, *weights)

    swap = [(0, 1), (1, 0)]
    keep = keep + lax.ppermute(send, "core", swap)
    keep, r_high = lax.optimization_barrier((keep, r_high))
    pieces = exchange(keep.reshape(chips, piece, LANE), ("blk", "side"))

    weights = (w_cat, w_out, weight_res, weight_skip, gain_mid, shift_mid, bias_res, bias_skip)
    count = items // 2

    def outer(offset, size, earlier):
        pair = 2 if size % 2 == 0 and offset % 2 == 0 else 1
        large = (inputs, cot_res, r_high, r_low, u_high, u_low)
        return pl.pallas_call(
            functools.partial(outer_kernel, offset=offset),
            grid=(size // pair,),
            in_specs=[ends_spec, ends_spec, whole(mid_sums)]
            + [per_item(array, pair, offset // pair) for array in large]
            + [whole(array) for array in weights]
            + [pl.BlockSpec(memory_space=pl.ANY)] * len(earlier),
            out_specs=[per_item(wide, pair, offset // pair)] * 3,
            out_shape=[wide] * 3,
            scratch_shapes=[
                pltpu.VMEM((2, items, LANE), F32),
                pltpu.VMEM((3, 2 * cin, LANE), F32),
                pltpu.VMEM((3 * width, 2 * cin), BF16),
                pltpu.VMEM((width, 2 * cin), BF16),
            ],
            input_output_aliases={17: 0, 18: 1, 19: 2} if earlier else {},
            compiler_params=params(),
            cost_estimate=cost(12 * size * frames * cin * width, size * frames * width * 8),
        )(lengths, origin, mid_sums, *large, *weights, *earlier)

    residual_out, skip_out, grad_inputs = outer(0, count, ())
    pieces, residual_out = lax.optimization_barrier((pieces, residual_out))
    mine = exchange(jnp.broadcast_to(jnp.sum(pieces, axis=0), pieces.shape), ("blk", "side")).reshape(-1, LANE)
    residual_out, skip_out, grad_inputs = outer(count, items - count, (residual_out, skip_out, grad_inputs))
    mine, residual_out = lax.optimization_barrier((mine, residual_out))
    theirs = lax.ppermute(mine, "core", swap)
    vector, short = sds(1, width), sds(1, cin)
    ends_of = (
        sds(width, cin), vector, vector, vector, vector, sds(3, width), vector, vector, vector, vector,
        sds(cin, width), short, sds(cin, width), short,
    )
    tail = pl.pallas_call(
        last_kernel,
        in_specs=[pl.BlockSpec(memory_space=pltpu.SMEM)] + [pl.BlockSpec(memory_space=pltpu.VMEM)] * 6,
        out_shape=ends_of,
    )(core, mine, theirs, weight_res, weight_skip, gain_mid, shift_mid)
    tail = [
        value if number in (0, 10, 12) else value.T if number == 5 else value.reshape(-1)
        for number, value in enumerate(tail)
    ]
    return (residual_out, skip_out, grad_inputs) + tuple(tail)


def solution(mesh):
    devices = mesh.devices
    split_mesh = jax.sharding.Mesh(devices.reshape(devices.shape[0], -1, 2), ("blk", "side", "core"))
    batch = ("side", "core")
    items = P(batch, None, "blk")
    return jax.shard_map(
        local,
        mesh=split_mesh,
        in_specs=(items,) + (P(),) * 14 + (P(batch), items, items),
        out_specs=(items,) * 3 + (P(),) * 14,
        check_vma=False,
    )
```

```python
import functools

import jax
import jax.numpy as jnp
from jax import lax
from jax.experimental import pallas as pl
from jax.experimental.pallas import tpu as pltpu
from jax.sharding import PartitionSpec as P

STEP = 8
HALO = 2 * STEP
EPS = 1e-05
LANE = 128
ROWS = 64
SECOND_ROWS = 128
PIECE = 256
THIRD_ROWS = 32
F32 = jnp.float32
BF16 = jnp.bfloat16
VMEM_LIMIT = 60 * 1024 * 1024


def split(value):
    high = value.astype(BF16)
    low = (value - high.astype(F32)).astype(BF16)
    return high, low


def product(left, right):
    return jnp.dot(left, right, preferred_element_type=F32)


def product_nt(left, right):
    return lax.dot_general(left, right, (((1,), (1,)), ((), ())), preferred_element_type=F32)


def tile(row):
    return jnp.broadcast_to(row, (8, LANE))


def load(ref, base, rows, lanes):
    return ref[pl.ds(base, rows), lanes].reshape(rows // 8, 8, LANE)


def frame_of(base, rows):
    shape = (rows // 8, 8, LANE)
    return lax.broadcasted_iota(jnp.int32, shape, 0) * 8 + lax.broadcasted_iota(jnp.int32, shape, 1) + base


def half_slopes(row):
    return tile(0.5 - 0.5 * row), tile(0.5 + 0.5 * row)


def act_half(half, c0, c1):
    return half * (c1 + c0 * jnp.tanh(half))


def act_parts(half, c0, c1):
    th = jnp.tanh(half)
    ratio = c1 + c0 * th
    act = half * ratio
    cut = half - act
    return act, ratio + cut * (1.0 + th), cut


def total(value):
    return jnp.sum(jnp.sum(value, axis=0, keepdims=True), axis=1, keepdims=True)


def place(values):
    lane = lax.broadcasted_iota(jnp.int32, (1, LANE), 1)
    row = jnp.zeros((1, LANE), F32)
    for position, value in enumerate(values):
        row = jnp.where(lane == position, value, row)
    return row


def lane_tiles(width):
    return [slice(start, start + LANE) for start in range(0, width, LANE)]


def first_kernel(
    lengths_ref, origin_ref, x_ref, res_l_ref, res_r_ref, skip_l_ref, skip_r_ref, w_in_ref, bias_ref, slope_ref,
    w_res_ref, w_skip_ref, gain_ref,
    sums_ref, left_ref, right_ref, w_cat_ref, w_out_ref,
):
    group, cin, frames = x_ref.shape
    width = w_in_ref.shape[0]

    @pl.when(pl.program_id(0) == 0)
    def _():
        high, low = split(0.5 * w_in_ref[...].T)
        w_cat_ref[0:cin] = high
        w_cat_ref[cin : 2 * cin] = high
        w_cat_ref[2 * cin : 3 * cin] = low
        row = lax.broadcasted_iota(jnp.int32, (LANE, width), 0)
        bias = jnp.broadcast_to(0.5 * bias_ref[...], (LANE, width))
        near = bias.astype(BF16).astype(F32)
        w_cat_ref[3 * cin :] = jnp.where(row == 0, near, jnp.where(row == 1, bias - near, 0.0)).astype(BF16)
        for number, ref in enumerate((w_res_ref, w_skip_ref)):
            high, low = split(ref[...] * gain_ref[...])
            start = number * cin
            w_out_ref[start : start + cin] = high
            w_out_ref[2 * cin + start : 3 * cin + start] = high
            w_out_ref[4 * cin + start : 5 * cin + start] = low

    step = min(PIECE, frames)
    for number in range(group):
        item = pl.program_id(0) * group + number
        end = lengths_ref[item] - origin_ref[0]
        first = second = jnp.zeros((8, LANE), F32)
        for start in range(0, frames, step):
            xt = x_ref[number, :, start : start + step].astype(BF16).T
            ones = jnp.ones((step, LANE), BF16)
            weights = jnp.concatenate([w_cat_ref[0:cin], w_cat_ref[3 * cin :]], axis=0)
            half = product(jnp.concatenate([xt, ones], axis=1), weights)
            valid = frame_of(start, step) < end
            for lanes in lane_tiles(width):
                c0, c1 = half_slopes(slope_ref[0:1, lanes])
                value = act_half(half[:, lanes].reshape(step // 8, 8, LANE), c0, c1)
                value = jnp.where(valid, value, 0.0)
                first = first + jnp.sum(value, axis=0)
                second = second + jnp.sum(value * value, axis=0)
        row = place((total(first), total(second)))
        for block in range(sums_ref.shape[0]):
            sums_ref[block, pl.ds(item, 1), :] = row
        left_ref[number, :, 0:cin] = x_ref[number, :, 0:LANE].T[0:HALO]
        right_ref[number, :, 0:cin] = x_ref[number, :, frames - LANE : frames].T[LANE - HALO : LANE]
        left_ref[number, 0:STEP, cin : 2 * cin] = res_l_ref[number].T[0:STEP]
        left_ref[number, STEP:HALO, cin : 2 * cin] = skip_l_ref[number].T[0:STEP]
        right_ref[number, 0:STEP, cin : 2 * cin] = res_r_ref[number].T[LANE - STEP : LANE]
        right_ref[number, STEP:HALO, cin : 2 * cin] = skip_r_ref[number].T[LANE - STEP : LANE]


def at(base):
    return base if isinstance(base, int) else pl.multiple_of(base, 8)


def sweep(frames, rows, end, body, init, rest=None):
    if end is None:
        carry = init
        for base in range(0, frames, rows):
            carry = body(base, False, carry)
        return carry
    live = jnp.clip(end, 0, frames)
    full, some = lax.div(live, rows), lax.div(live + (rows - 1), rows)
    carry = lax.fori_loop(0, full, lambda n, c: body(pl.multiple_of(n * rows, rows), False, c), init)
    carry = lax.fori_loop(full, some, lambda n, c: body(pl.multiple_of(n * rows, rows), True, c), carry)
    if rest is not None:

        def clear(n, c):
            rest(pl.multiple_of(n * rows, rows))
            return c

        lax.fori_loop(some, frames // rows, clear, 0)
    return carry


def both_ways(full, run):
    pl.when(full)(lambda: run(True))
    pl.when(jnp.logical_not(full))(lambda: run(False))


def where_valid(valid, value):
    return value if valid is None else jnp.where(valid, value, 0.0)


def counts(lengths_ref, items, width):
    row = lax.broadcasted_iota(jnp.int32, (items, 1), 0)
    lengths = jnp.zeros((items, 1), jnp.int32)
    for item in range(items):
        lengths = jnp.where(row == item, lengths_ref[item], lengths)
    return lengths.astype(F32) * float(width)


def first_norm(sums_ref, count):
    sums = jnp.sum(sums_ref[...], axis=0)
    mean = 2.0 * sums[:, 0:1] / count
    var = 4.0 * sums[:, 1:2] / count - mean * mean
    return mean, lax.rsqrt(var + EPS)


def second_kernel(
    lengths_ref, origin_ref, sums_ref, from_left_ref, from_right_ref, x_all, res_all, skip_all,
    w_cat_ref, w_out_ref, slope_ref, gain_ref, shift_ref, taps_ref, tap_bias_ref, slope_mid_ref,
    half_all, mid_all, back_all, edge_ref, out_ref,
    halo_ref, normal_ref, coef_ref,
):
    items = out_ref.shape[1]
    group, frames, width = half_all.shape
    cin = x_all.shape[1]
    origin = origin_ref[0]

    @pl.when(pl.program_id(0) == 0)
    def _():
        mean, scale = first_norm(sums_ref, counts(lengths_ref, items, width))
        coef_ref[0] = jnp.broadcast_to(scale, (items, LANE))
        coef_ref[1] = jnp.broadcast_to(scale * mean, (items, LANE))
        for side, ref in enumerate((from_left_ref, from_right_ref)):
            high, low = split(ref[:, :, 0:cin].reshape(items * HALO, cin))
            ones = jnp.ones((items * HALO, LANE), BF16)
            value = product(jnp.concatenate([high, low, high, ones], axis=1), w_cat_ref[...])
            halo_ref[side] = value.reshape(items, HALO, width)
            cots = jnp.concatenate([ref[:, 0:STEP, cin : 2 * cin], ref[:, STEP:HALO, cin : 2 * cin]], axis=2)
            high, low = split(cots.reshape(items * STEP, 2 * cin))
            value = product(jnp.concatenate([high, low, high], axis=1), w_out_ref[...])
            edge_ref[:, side * STEP : (side + 1) * STEP, :] = value.reshape(items, STEP, width)

    def run(number, item, end, full):
        half_ref, res_ref, skip_ref, mid_ref, back_ref = (
            ref.at[number : number + 1] for ref in (half_all, res_all, skip_all, mid_all, back_all)
        )
        high, low = split(x_all[number].T)
        ones = jnp.ones((frames, LANE), BF16)
        half_ref[0] = product(jnp.concatenate([high, low, high, ones], axis=1), w_cat_ref[...])
        rows = SECOND_ROWS if full and frames % SECOND_ROWS == 0 else ROWS
        d_high, d_low = split(jnp.concatenate([res_ref[0], skip_ref[0]], axis=0))
        high, low = d_high.T, d_low.T
        back_ref[0] = product(jnp.concatenate([high, low, high], axis=1), w_out_ref[...])

        scale, scale_mean = coef_ref[0, pl.ds(item, 1), :], coef_ref[1, pl.ds(item, 1), :]
        window = jnp.clip(end - STEP, 0, frames - HALO)
        window = pl.multiple_of(lax.div(window, 8) * 8, 8)
        tots = [jnp.zeros((8, LANE), F32)] * 10
        for lanes in lane_tiles(width):
            c0, c1 = half_slopes(slope_ref[0:1, lanes])
            gain, shift = gain_ref[0:1, lanes], shift_ref[0:1, lanes]
            factor, offset = 2.0 * gain * scale, shift - gain * scale_mean
            hole = tile(-offset / factor)

            def normed(half, valid):
                value = act_half(half, c0, c1)
                return value if valid is None else jnp.where(valid, value, hole)

            def store(base, count, value):
                normal_ref[pl.ds(base, count), lanes] = value.reshape(count, LANE)

            frame = frame_of(-HALO, HALO)
            store(0, HALO, normed(halo_ref[0, item, :, lanes].reshape(2, 8, LANE), (frame < end) & (frame >= -origin)))
            frame = frame_of(frames, HALO)
            store(HALO + frames, HALO, normed(halo_ref[1, item, :, lanes].reshape(2, 8, LANE), frame < end))

            def fill(base, masked, carry):
                valid = frame_of(base, rows) < end if masked else None
                store(at(base + HALO), rows, normed(load(half_ref.at[0], base, rows, lanes), valid))
                return carry

            def clear(base):
                normal_ref[pl.ds(at(base + HALO), rows), lanes] = jnp.broadcast_to(-offset / factor, (rows, LANE))

            sweep(frames, rows, None if full else end, fill, 0, clear)

            rows_of = [0.5 * taps_ref[tap : tap + 1, lanes] for tap in range(3)]
            taps = [tile(factor * row) for row in rows_of]
            tap_bias = tile(0.5 * tap_bias_ref[0:1, lanes] + offset * (rows_of[0] + rows_of[1] + rows_of[2]))
            m0, m1 = half_slopes(slope_mid_ref[0:1, lanes])

            def conv(base, count):
                value = taps[0] * load(normal_ref, base, count, lanes)
                value = value + taps[1] * load(normal_ref, at(base + STEP), count, lanes)
                value = value + taps[2] * load(normal_ref, at(base + HALO), count, lanes) + tap_bias
                mid_ref[0, pl.ds(base, count), lanes] = value.reshape(count, LANE)
                return value

            conv(0, STEP)
            conv(frames + STEP, STEP)

            def gather(base, masked, carry):
                valid = frame_of(base, rows) < end if masked else None
                mid = conv(at(base + STEP), rows)
                act, grad, _ = act_parts(mid, m0, m1)
                back = load(back_ref.at[0], base, rows, lanes)
                act, grad, back = where_valid(valid, act), where_valid(valid, grad), where_valid(valid, back)
                ex, ez = grad * back, grad * act
                terms = (act, act * act, back, back * act, ex, grad, ez, ex * mid, grad * mid, ez * mid)
                return tuple(old + jnp.sum(new, axis=0) for old, new in zip(carry, terms))

            sums = sweep(frames, rows, None if full else end, gather, (jnp.zeros((8, LANE), F32),) * 10)

            def edge_sums(base, mask):
                mid = load(mid_ref.at[0], at(base + STEP), HALO, lanes)
                act, grad, _ = act_parts(mid, m0, m1)
                back = load(back_ref.at[0], base, HALO, lanes)
                return [jnp.sum(jnp.where(mask, term, 0.0), axis=0) for term in (grad * back, grad, grad * act)]

            frame = frame_of(0, HALO)
            low_sums = edge_sums(0, (frame < end) & (frame + origin < STEP))
            frame = frame_of(window, HALO)
            high_sums = edge_sums(window, (frame < end) & (frame >= end - STEP))
            w0, w1, w2 = (tile(taps_ref[tap : tap + 1, lanes]) for tap in range(3))
            for term in range(4):
                tots[term] = tots[term] + sums[term]
            for term in range(3):
                plain = sums[4 + term]
                edged = (w0 + w1 + w2) * plain - w0 * low_sums[term] - w2 * high_sums[term]
                tots[4 + term] = tots[4 + term] + gain * edged
                tots[7 + term] = (
                    tots[7 + term] + 2.0 * sums[7 + term] - tap_bias_ref[0:1, lanes] * plain - shift * edged
                )

        row = place([total(value) for value in tots])
        for block in range(out_ref.shape[0]):
            out_ref[block, pl.ds(item, 1), :] = row

    for number in range(group):
        item = pl.program_id(0) * group + number
        end = lengths_ref[item] - origin_ref[0]
        both_ways(end >= frames, functools.partial(run, number, item, end))


GRAD_ROWS = 16


def second_norm(mids_ref, count):
    mids = jnp.sum(mids_ref[...], axis=0)
    m = [mids[:, term : term + 1] for term in range(10)]
    mean = 2.0 * m[0] / count
    return m, mean, lax.rsqrt(4.0 * m[1] / count - mean * mean + EPS)


def flatten(flat_ref, grads_ref, half):
    height, width = grads_ref.shape
    tiles = lane_tiles(width)
    count = len(tiles) // 2
    for number, lanes in enumerate(tiles[half * count : (half + 1) * count]):
        flat_ref[number * height : (number + 1) * height] = grads_ref[:, lanes]
    used = height * count
    if used < flat_ref.shape[0]:
        flat_ref[used:] = jnp.zeros((flat_ref.shape[0] - used, LANE), F32)


def third_kernel(
    lengths_ref, origin_ref, core_ref, sums_ref, mids_ref, x_all, res_all, skip_all, half_all, mid_all, back_all, edge_all,
    slope_ref, gain_ref, shift_ref, taps_ref, slope_mid_ref,
    r_high_all, r_low_all, u_high_all, u_low_all, keep_ref, send_ref,
    grad_ref, coef_ref, vector_ref, grads_ref, cot_ref,
):
    items = coef_ref.shape[1]
    group, cin, frames = x_all.shape
    width = half_all.shape[2]
    origin = origin_ref[0]

    @pl.when(pl.program_id(0) == 0)
    def _():
        count = counts(lengths_ref, items, width)
        mean1, scale1 = first_norm(sums_ref, count)
        m, mean2, scale2 = second_norm(mids_ref, count)
        beta = scale2 * scale2 * (2.0 * m[3] - mean2 * m[2]) / count
        alpha = m[2] / count - mean2 * beta
        mean_a = scale2 * (m[4] - alpha * m[5] - 2.0 * beta * m[6]) / count
        mean_b = scale2 * (m[7] - alpha * m[8] - 2.0 * beta * m[9]) / count
        values = (
            scale1, scale1 * mean1, scale1 * (mean_a - mean1 * scale1 * mean_b), 2.0 * scale1 * scale1 * mean_b,
            scale2, alpha, 2.0 * beta, scale2 * mean2,
        )
        for number, value in enumerate(values):
            coef_ref[number] = jnp.broadcast_to(value, (items, LANE))
        vector_ref[...] = jnp.zeros(vector_ref.shape, F32)
        grads_ref[...] = jnp.zeros(grads_ref.shape, F32)
        cot_ref[...] = jnp.zeros(cot_ref.shape, F32)

    def run(number, item, end, full):
        x_ref, res_ref, skip_ref, half_ref, mid_ref, back_ref, edge_ref = (
            ref.at[number : number + 1] for ref in (x_all, res_all, skip_all, half_all, mid_all, back_all, edge_all)
        )
        r_high_ref, r_low_ref, u_high_ref, u_low_ref = (
            ref.at[number : number + 1] for ref in (r_high_all, r_low_all, u_high_all, u_low_all)
        )
        rows = THIRD_ROWS if full else ROWS
        coefs = [tile(coef_ref[number, pl.ds(item, 1), :]) for number in range(8)]
        scale1, scale_mean1, dp_a, dp_b, scale2, dr_a, dr_b, z_a = coefs
        both = jnp.concatenate([res_ref[0], skip_ref[0]], axis=0)
        d_high, d_low = split(both)
        lane = lax.broadcasted_iota(jnp.int32, (1, LANE), 1)
        cots = jnp.zeros((2 * cin, LANE), F32)
        for lanes in lane_tiles(frames):
            piece = both[:, lanes]
            cots = cots + (piece if full else jnp.where(lane + lanes.start < end, piece, 0.0))
        cot_ref[0] += cots
        cot_ref[1] += z_a[0:1] * cots

        for lanes in lane_tiles(width):
            m0, m1 = half_slopes(slope_mid_ref[0:1, lanes])

            def middle(base, count, valid, back):
                act, slope, cut = act_parts(load(mid_ref.at[0], base, count, lanes), m0, m1)
                grad = (back - dr_a) - dr_b * act
                grad = where_valid(valid, grad)
                grad_ref[pl.ds(base, count), lanes] = (grad * slope).reshape(count, LANE)
                return act, grad * cut

            frame = frame_of(-STEP, STEP)
            middle(0, STEP, (frame < end) & (frame >= -origin), edge_ref[0:1, 0:STEP, lanes])
            middle(frames + STEP, STEP, frame_of(frames, STEP) < end, edge_ref[0:1, STEP:HALO, lanes])

            def inner(base, masked, carry):
                valid = frame_of(base, rows) < end if masked else None
                act, term = middle(at(base + STEP), rows, valid, load(back_ref.at[0], base, rows, lanes))
                high, low = split(where_valid(valid, act).reshape(rows, LANE))
                r_high_ref[0, pl.ds(base, rows), lanes] = high
                r_low_ref[0, pl.ds(base, rows), lanes] = low
                return carry + jnp.sum(term, axis=0)

            def inner_clear(base):
                grad_ref[pl.ds(at(base + STEP), rows), lanes] = jnp.zeros((rows, LANE), F32)
                r_high_ref[0, pl.ds(base, rows), lanes] = jnp.zeros((rows, LANE), BF16)
                r_low_ref[0, pl.ds(base, rows), lanes] = jnp.zeros((rows, LANE), BF16)

            vector_ref[8, :, lanes] += scale2 / m0 * sweep(
                frames, rows, None if full else end, inner, jnp.zeros((8, LANE), F32), inner_clear
            )

            c0, c1 = half_slopes(slope_ref[0:1, lanes])
            gain, shift = gain_ref[0:1, lanes], shift_ref[0:1, lanes]
            taps = [tile(taps_ref[tap : tap + 1, lanes]) for tap in range(3)]
            outer = gain * scale1
            scaled = [tap * (outer * scale2) for tap in taps]

            def body(base, masked, carry):
                valid = frame_of(base, rows) < end if masked else None
                ahead = load(grad_ref, at(base + HALO), rows, lanes)
                here = load(grad_ref, at(base + STEP), rows, lanes)
                behind = where_valid(valid, load(grad_ref, base, rows, lanes))
                act, slope, cut = act_parts(load(half_ref.at[0], base, rows, lanes), c0, c1)
                dp = scaled[0] * ahead + scaled[1] * here + scaled[2] * behind
                dp = where_valid(valid, (dp - dp_a) - dp_b * act)
                du = dp * slope
                high, low = split(du.reshape(rows, LANE))
                u_high_ref[0, pl.ds(base, rows), lanes] = high
                u_low_ref[0, pl.ds(base, rows), lanes] = low
                terms = (dp * cut, here, ahead * act, here * act, behind * act)
                return tuple(old + jnp.sum(new, axis=0) for old, new in zip(carry, terms))

            def clear(base):
                u_high_ref[0, pl.ds(base, rows), lanes] = jnp.zeros((rows, LANE), BF16)
                u_low_ref[0, pl.ds(base, rows), lanes] = jnp.zeros((rows, LANE), BF16)

            sums = sweep(frames, rows, None if full else end, body, (jnp.zeros((8, LANE), F32),) * 5, clear)
            window = pl.multiple_of(lax.div(jnp.clip(end, 0, frames - HALO), 8) * 8, 8)
            row = frame_of(window, HALO)
            inside = jnp.where((row >= end) & (row < end + STEP), load(grad_ref, window, HALO, lanes), 0.0)
            plains = (
                sums[1] - grad_ref[STEP:HALO, lanes] + grad_ref[frames + STEP : frames + HALO, lanes],
                sums[1],
                sums[1] - grad_ref[frames : frames + STEP, lanes] + grad_ref[0:STEP, lanes] - jnp.sum(inside, axis=0),
            )
            factor, offset = 2.0 * outer, shift - gain * scale_mean1
            vector_ref[1, :, lanes] += sums[0] / c0
            gain_sum = shift_sum = jnp.zeros((8, LANE), F32)
            for tap in range(3):
                plain, times = scale2 * plains[tap], scale2 * sums[2 + tap]
                vector_ref[4 + tap, :, lanes] += factor * times + offset * plain
                gain_sum = gain_sum + taps[tap] * (2.0 * scale1 * times - scale_mean1 * plain)
                shift_sum = shift_sum + taps[tap] * plain
            vector_ref[2, :, lanes] += gain_sum
            vector_ref[3, :, lanes] += shift_sum
            vector_ref[7, :, lanes] += scale2 * sums[1]

        r_high, r_low = r_high_ref[0], r_low_ref[0]
        mixed = product(
            jnp.concatenate([d_high, d_low, d_high], axis=1), jnp.concatenate([r_high, r_high, r_low], axis=0)
        )
        z_0 = 2.0 * scale2[0:1]
        for lanes in lane_tiles(width):
            grads_ref[0 : 2 * cin, lanes] += z_0 * mixed[:, lanes]
        u_high, u_low = u_high_ref[0], u_low_ref[0]
        x_high, x_low = split(x_ref[0])
        rows_of = jnp.concatenate([x_high, x_low, x_high], axis=1)
        ones = jnp.ones((GRAD_ROWS, frames), BF16)
        ones = jnp.concatenate([ones, jnp.zeros((GRAD_ROWS, frames), BF16), ones], axis=1)
        grads_ref[2 * cin : 3 * cin + GRAD_ROWS] += product(
            jnp.concatenate([rows_of, ones], axis=0), jnp.concatenate([u_high, u_high, u_low], axis=0)
        )

    for number in range(group):
        item = pl.program_id(0) * group + number
        end = lengths_ref[item] - origin_ref[0]
        both_ways(end >= frames, functools.partial(run, number, item, end))

    @pl.when(pl.program_id(0) == items // group - 1)
    def _():
        base = 3 * cin
        grads_ref[0 : 2 * cin] = grads_ref[0 : 2 * cin] - jnp.sum(cot_ref[1], axis=1, keepdims=True)
        for row in range(1, 9):
            grads_ref[base + row : base + row + 1] = jnp.sum(vector_ref[row], axis=0, keepdims=True)
        column = jnp.broadcast_to(jnp.sum(cot_ref[0], axis=1, keepdims=True), (2 * cin, LANE)).T[0:1]
        grads_ref[base + 9 : base + 10] = jnp.zeros((1, width), F32)
        for number in range(2 * cin // LANE):
            grads_ref[base + 9 + number : base + 10 + number, 0:LANE] = column[:, number * LANE : (number + 1) * LANE]
            grads_ref[base + 9 + number : base + 10 + number, width // 2 : width // 2 + LANE] = column[
                :, number * LANE : (number + 1) * LANE
            ]
        for core in range(2):

            @pl.when(core_ref[0] == core)
            def _():
                flatten(keep_ref, grads_ref, core)
                flatten(send_ref, grads_ref, 1 - core)


def outer_kernel(
    lengths_ref, origin_ref, mids_ref, x_ref, res_ref, r_high_ref, r_low_ref, u_high_ref, u_low_ref,
    w_cat_ref, w_out_ref, w_res_ref, w_skip_ref, gain_ref, shift_ref, bias_res_ref, bias_skip_ref, *rest_refs, offset,
):
    res_out_ref, skip_out_ref, x_grad_ref, coef_ref, column_ref, out_turned_ref, in_turned_ref = rest_refs[-7:]
    items = coef_ref.shape[1]
    group, cin, frames = x_ref.shape
    width = w_cat_ref.shape[1]

    @pl.when(pl.program_id(0) == 0)
    def _():
        _, mean, scale = second_norm(mids_ref, counts(lengths_ref, items, width))
        coef_ref[0] = jnp.broadcast_to(2.0 * scale, (items, LANE))
        coef_ref[1] = jnp.broadcast_to(scale * mean, (items, LANE))
        high, low = w_out_ref[0 : 2 * cin].T, w_out_ref[4 * cin : 6 * cin].T
        out_turned_ref[0:width] = high
        out_turned_ref[width : 2 * width] = high
        out_turned_ref[2 * width : 3 * width] = low
        in_turned_ref[:, 0:cin] = w_cat_ref[0:cin].T
        in_turned_ref[:, cin : 2 * cin] = w_cat_ref[2 * cin : 3 * cin].T
        for number, (w_ref, b_ref) in enumerate(((w_res_ref, bias_res_ref), (w_skip_ref, bias_skip_ref))):
            rows = slice(number * cin, (number + 1) * cin)
            column_ref[0, rows] = jnp.broadcast_to(b_ref[...], (LANE, cin)).T
            for spot, vector_of in ((1, shift_ref), (2, gain_ref)):
                value = jnp.sum(w_ref[...] * vector_of[...], axis=1, keepdims=True)
                column_ref[spot, rows] = jnp.broadcast_to(value, (cin, LANE))

    lane = lax.broadcasted_iota(jnp.int32, (1, LANE), 1)
    for number in range(group):
        item = offset + pl.program_id(0) * group + number
        end = lengths_ref[item] - origin_ref[0]
        z_0, z_a = coef_ref[0, pl.ds(item, 1), :], coef_ref[1, pl.ds(item, 1), :]
        r_high, r_low = r_high_ref[number], r_low_ref[number]
        out = product(jnp.concatenate([r_high, r_low, r_high], axis=1), out_turned_ref[...]).T
        pair = product(u_high_ref[number], in_turned_ref[...])
        x_grad = (pair[:, 0:cin] + pair[:, cin : 2 * cin] + product(u_low_ref[number], in_turned_ref[:, 0:cin])).T
        inside = column_ref[1] - z_a * column_ref[2]
        for lanes in lane_tiles(frames):
            valid = lane + lanes.start < end
            wide = column_ref[0] + jnp.where(valid, inside, 0.0) + z_0 * out[:, lanes]
            res_out_ref[number, :, lanes] = wide[0:cin] + x_ref[number, :, lanes]
            skip_out_ref[number, :, lanes] = wide[cin : 2 * cin]
            x_grad_ref[number, :, lanes] = jnp.where(valid, res_ref[number, :, lanes], 0.0) + 2.0 * x_grad[:, lanes]


def last_kernel(
    core_ref, mine_ref, theirs_ref, w_res_ref, w_skip_ref, gain_ref, shift_ref,
    w_in_out, bias_in_out, slope_in_out, gain_in_out, shift_in_out, taps_out, tap_bias_out, slope_mid_out,
    gain_mid_out, shift_mid_out, w_res_out, bias_res_out, w_skip_out, bias_skip_out,
):
    cin, width = w_res_ref.shape
    height = 3 * cin + GRAD_ROWS
    base = 3 * cin
    vectors = ((0, bias_in_out), (1, slope_in_out), (2, gain_in_out), (3, shift_in_out), (7, tap_bias_out), (8, slope_mid_out))
    groups = ((w_res_ref, w_res_out), (w_skip_ref, w_skip_out))
    columns = []
    for number, bias_out in enumerate((bias_res_out, bias_skip_out)):
        row = mine_ref[base + 9 + number : base + 10 + number]
        bias_out[...] = row
        columns.append(jnp.broadcast_to(row, (cin, cin)).T[:, 0:1])
    tiles = lane_tiles(width)
    count = len(tiles) // 2

    def place_half(ref, half):
        for number, lanes in enumerate(tiles[half * count : (half + 1) * count]):
            grads = ref.at[number * height : (number + 1) * height]
            w_in_out[lanes] = grads[2 * cin : 3 * cin].T
            for row, out in vectors:
                out[:, lanes] = grads[base + row : base + row + 1]
            taps_out[:, lanes] = grads[base + 4 : base + 7]
            gain_sum = shift_sum = jnp.zeros((1, LANE), F32)
            for group, (w_ref, w_out) in enumerate(groups):
                products = grads[group * cin : (group + 1) * cin]
                column = columns[group]
                w_out[:, lanes] = gain_ref[:, lanes] * products + shift_ref[:, lanes] * column
                gain_sum = gain_sum + jnp.sum(w_ref[:, lanes] * products, axis=0, keepdims=True)
                shift_sum = shift_sum + jnp.sum(w_ref[:, lanes] * column, axis=0, keepdims=True)
            gain_mid_out[:, lanes] = gain_sum
            shift_mid_out[:, lanes] = shift_sum

    for core in range(2):

        @pl.when(core_ref[0] == core)
        def _():
            place_half(mine_ref, core)
            place_half(theirs_ref, 1 - core)


def whole(array):
    return pl.BlockSpec(array.shape, lambda item: (0,) * len(array.shape))


def per_item(array, group=1, offset=0):
    return pl.BlockSpec((group,) + array.shape[1:], lambda item: (item + offset, 0, 0))


def edge_block(array, group, position):
    return pl.BlockSpec((group, array.shape[1], LANE), lambda item: (item, 0, position))


def sds(*shape, dtype=F32):
    return jax.ShapeDtypeStruct(shape, dtype)


def cost(flops, size):
    return pl.CostEstimate(flops=flops, bytes_accessed=size, transcendentals=0)


def params():
    return pltpu.CompilerParams(dimension_semantics=("arbitrary",), vmem_limit_bytes=VMEM_LIMIT)


def exchange(pieces, axes):
    return lax.all_to_all(pieces, axes, 0, 0)


def local(
    inputs, weight_in, bias_in, slope_in, gain_in, shift_in, depthwise_weight, depthwise_bias, slope_mid, gain_mid,
    shift_mid, weight_res, bias_res, weight_skip, bias_skip, lengths, cot_res, cot_skip,
):
    items, cin, frames = inputs.shape
    width = weight_in.shape[0]
    blocks = lax.axis_size("blk")
    origin = (lax.axis_index("blk") * frames).astype(jnp.int32).reshape(1)
    core = lax.axis_index("core").astype(jnp.int32).reshape(1)
    bias_in, slope_in, gain_in, shift_in, tap_bias, slope_mid, gain_mid, shift_mid, bias_res, bias_skip = (
        vector.reshape(1, -1)
        for vector in (
            bias_in, slope_in, gain_in, shift_in, depthwise_bias, slope_mid, gain_mid, shift_mid, bias_res, bias_skip
        )
    )
    taps = depthwise_weight.T
    ends_spec = pl.BlockSpec(memory_space=pltpu.SMEM)

    half = sds(items, frames, width)
    halo = sds(items, HALO, 2 * cin)
    last = frames // LANE - 1
    sums = sds(blocks, items, LANE)
    w_cat, w_out = sds(3 * cin + LANE, width, dtype=BF16), sds(6 * cin, width, dtype=BF16)
    weights = (weight_in, bias_in, slope_in, weight_res, weight_skip, gain_mid)
    pair = 2 if items % 2 == 0 else 1
    first_sums, to_left, to_right, w_cat, w_out = pl.pallas_call(
        first_kernel,
        grid=(items // pair,),
        in_specs=[ends_spec, ends_spec, per_item(inputs, pair)]
        + [edge_block(array, pair, spot) for array in (cot_res, cot_skip) for spot in (0, last)]
        + [whole(array) for array in weights],
        out_specs=[whole(sums), per_item(halo, pair), per_item(halo, pair), whole(w_cat), whole(w_out)],
        out_shape=[sums, halo, halo, w_cat, w_out],
        compiler_params=params(),
    )(lengths, origin, inputs, cot_res, cot_res, cot_skip, cot_skip, *weights)

    forward = [(block, block + 1) for block in range(blocks - 1)]
    backward = [(target, source) for source, target in forward]
    first_sums = exchange(first_sums, "blk")
    from_left = lax.ppermute(to_right, "blk", forward)
    from_right = lax.ppermute(to_left, "blk", backward)

    mid, edge = sds(items, frames + HALO, width), sds(items, HALO, width)
    small = (first_sums, from_left, from_right)
    weights = (w_cat, w_out, slope_in, gain_in, shift_in, taps, tap_bias, slope_mid)
    rounded = sds(items, frames, width, dtype=BF16)
    half, mid, back, edge, mid_sums = pl.pallas_call(
        second_kernel,
        grid=(items // pair,),
        in_specs=[ends_spec, ends_spec]
        + [whole(array) for array in small]
        + [per_item(array, pair) for array in (inputs, cot_res, cot_skip)]
        + [whole(array) for array in weights],
        out_specs=[per_item(half, pair), per_item(mid, pair), per_item(half, pair), whole(edge), whole(sums)],
        out_shape=[half, mid, half, edge, sums],
        scratch_shapes=[
            pltpu.VMEM((2, items, HALO, width), F32),
            pltpu.VMEM((frames + 2 * HALO, width), F32),
            pltpu.VMEM((2, items, LANE), F32),
        ],
        compiler_params=params(),
        cost_estimate=cost(20 * items * frames * cin * width, items * frames * width * 14),
    )(lengths, origin, *small, inputs, cot_res, cot_skip, *weights)
    mid_sums = exchange(mid_sums, "blk")

    small = (first_sums, mid_sums)
    large = (inputs, cot_res, cot_skip, half, mid, back, edge)
    weights = (slope_in, gain_in, shift_in, taps, slope_mid)
    wide = sds(*inputs.shape)
    height = 3 * cin + GRAD_ROWS
    chips = blocks * lax.axis_size("side")
    piece = -(-height * (width // LANE) // (2 * chips * 8)) * 8
    flat = sds(chips * piece, LANE)
    r_high, r_low, u_high, u_low, keep, send = pl.pallas_call(
        third_kernel,
        grid=(items // pair,),
        in_specs=[ends_spec] * 3
        + [whole(array) for array in small]
        + [per_item(array, pair) for array in large]
        + [whole(array) for array in weights],
        out_specs=[per_item(rounded, pair)] * 4 + [whole(flat)] * 2,
        out_shape=[rounded] * 4 + [flat] * 2,
        scratch_shapes=[
            pltpu.VMEM((frames + HALO, width), F32),
            pltpu.VMEM((8, items, LANE), F32),
            pltpu.VMEM((9, 8, width), F32),
            pltpu.VMEM((height, width), F32),
            pltpu.VMEM((2, 2 * cin, LANE), F32),
        ],
        compiler_params=params(),
        cost_estimate=cost(18 * items * frames * cin * width, items * frames * width * 20),
    )(lengths, origin, core, *small, *large, *weights)

    swap = [(0, 1), (1, 0)]
    keep = keep + lax.ppermute(send, "core", swap)
    keep, r_high = lax.optimization_barrier((keep, r_high))
    pieces = exchange(keep.reshape(chips, piece, LANE), ("blk", "side"))

    weights = (w_cat, w_out, weight_res, weight_skip, gain_mid, shift_mid, bias_res, bias_skip)
    count = items // 2

    def outer(offset, size, earlier):
        pair = 2 if size % 2 == 0 and offset % 2 == 0 else 1
        large = (inputs, cot_res, r_high, r_low, u_high, u_low)
        return pl.pallas_call(
            functools.partial(outer_kernel, offset=offset),
            grid=(size // pair,),
            in_specs=[ends_spec, ends_spec, whole(mid_sums)]
            + [per_item(array, pair, offset // pair) for array in large]
            + [whole(array) for array in weights]
            + [pl.BlockSpec(memory_space=pl.ANY)] * len(earlier),
            out_specs=[per_item(wide, pair, offset // pair)] * 3,
            out_shape=[wide] * 3,
            scratch_shapes=[
                pltpu.VMEM((2, items, LANE), F32),
                pltpu.VMEM((3, 2 * cin, LANE), F32),
                pltpu.VMEM((3 * width, 2 * cin), BF16),
                pltpu.VMEM((width, 2 * cin), BF16),
            ],
            input_output_aliases={17: 0, 18: 1, 19: 2} if earlier else {},
            compiler_params=params(),
            cost_estimate=cost(12 * size * frames * cin * width, size * frames * width * 8),
        )(lengths, origin, mid_sums, *large, *weights, *earlier)

    residual_out, skip_out, grad_inputs = outer(0, count, ())
    pieces, residual_out = lax.optimization_barrier((pieces, residual_out))
    mine = exchange(jnp.broadcast_to(jnp.sum(pieces, axis=0), pieces.shape), ("blk", "side")).reshape(-1, LANE)
    residual_out, skip_out, grad_inputs = outer(count, items - count, (residual_out, skip_out, grad_inputs))
    mine, residual_out = lax.optimization_barrier((mine, residual_out))
    theirs = lax.ppermute(mine, "core", swap)
    vector, short = sds(1, width), sds(1, cin)
    ends_of = (
        sds(width, cin), vector, vector, vector, vector, sds(3, width), vector, vector, vector, vector,
        sds(cin, width), short, sds(cin, width), short,
    )
    tail = pl.pallas_call(
        last_kernel,
        in_specs=[pl.BlockSpec(memory_space=pltpu.SMEM)] + [pl.BlockSpec(memory_space=pltpu.VMEM)] * 6,
        out_shape=ends_of,
    )(core, mine, theirs, weight_res, weight_skip, gain_mid, shift_mid)
    tail = [
        value if number in (0, 10, 12) else value.T if number == 5 else value.reshape(-1)
        for number, value in enumerate(tail)
    ]
    return (residual_out, skip_out, grad_inputs) + tuple(tail)


def solution(mesh):
    devices = mesh.devices
    split_mesh = jax.sharding.Mesh(devices.reshape(devices.shape[0], -1, 2), ("blk", "side", "core"))
    batch = ("side", "core")
    items = P(batch, None, "blk")
    return jax.shard_map(
        local,
        mesh=split_mesh,
        in_specs=(items,) + (P(),) * 14 + (P(batch), items, items),
        out_specs=(items,) * 3 + (P(),) * 14,
        check_vma=False,
    )
```
